32 devices in a mesh: tile: 16 (over z, y, core), scan: 2 (over x).
Axes of the slice: x: 2, y: 2, z: 4, core: 2. Of those that a mesh axis runs over, the one named last changes fastest.
Arguments:
- object_slab: float32 [2, 2, 1024, 512], P(None, None, 'tile', 'scan'), may hold values from -6 to 6
- probe_wave: bfloat16 [2, 512, 512], P(None, None, 'scan'), may hold values from -6 to 6
- amplitudes: float32 [32, 512, 512], P('tile', 'scan'), may hold values from 0.2 to 2
- row_offsets: int32 [32], P('tile'), may hold values from 0 to 63
- position_counts: int32 [16], P('tile'), may hold values from 0 to 2, as said below
Outputs:
- object_grad: float32 [2, 2, 1024, 512], P(None, None, 'tile', 'scan')
The draws below stay inside these ranges and needn't reach their ends.
Inputs may be any that keep to these rules, and one draw needn't show every extreme that they name: position_counts is 1 to 2 on the first 8 tiles, equal to 2 on at least one of them, and 0 on the last 8 tiles.
All inputs are finite; a program needn't handle non-finite values.
Results may differ from the reference program's by a relative error of at most 0.0065.
Values may be sent and summed in bfloat16 or wider, within the bound.
No kernel may reach another device: no remote copies, remote signals or barrier semaphores. Data moves between devices by JAX's collectives and lax.ppermute only.
A program may use at most 64 MiB of HBM per device.

```python
import math
import jax
import jax.numpy as jnp
from jax import lax

P_SIZE = 512
S = 2
TH = 64
POS_DEV = 2
TILES = 16
ROWS = 1024
NPOS = 32


def draw_position_counts(key, part):
    first_key, second_key = jax.random.split(jax.random.fold_in(key, 17))
    usable = TILES - P_SIZE // TH
    places = jnp.arange(TILES)
    counted = jax.random.randint(first_key, (TILES,), 1, POS_DEV + 1)
    busiest = jax.random.randint(second_key, (), 0, usable)
    counted = jnp.where(places == busiest, POS_DEV, counted)
    return jnp.where(places < usable, counted, 0).astype(jnp.int32)


def with_ends(values, own_key, low, top_value):
    index_at = [jax.random.randint(jax.random.fold_in(own_key, axis), (), 0, length) for axis, length in enumerate(values.shape)]
    widest = values.shape.index(max(values.shape))
    beside = index_at[:widest] + [(index_at[widest] + 1) % values.shape[widest]] + index_at[widest + 1:]
    return values.at[tuple(index_at)].set(low).at[tuple(beside)].set(top_value)


def block_scale(key, dims, shards, least, top_value):
    def one(axis_at, blocks):
        heights = jax.random.uniform(jax.random.fold_in(jax.random.fold_in(key, 6), axis_at), (blocks,), jnp.float32, least / len(shards), top_value / len(shards))
        return jnp.repeat(jnp.exp(heights), dims[axis_at] // blocks).reshape((-1,) + (1,) * (len(dims) - axis_at - 1))

    factor_of = one(*shards[0])
    for cut in shards[1:]:
        factor_of = factor_of * one(*cut)
    return factor_of


def bell_draw(key, shape, scale, limit, shards=(), kind=jnp.bfloat16):
    loudness = block_scale(key, shape, shards, -0.22, 0.18) if shards else 1.0
    entries = jax.random.normal(key, shape, jnp.float32) * scale * loudness
    return jnp.minimum(jnp.maximum(entries, -limit), limit).astype(kind)


def setup_inputs(seed: int = 0) -> dict:
    streams_of = jax.random.split(jax.random.key(seed), 6)
    object_slab = bell_draw(streams_of[0], (S, 2, ROWS, P_SIZE), 1.0, 6.0, ((2, 16), (3, 2)), jnp.float32)
    probe_wave = bell_draw(streams_of[1], (2, P_SIZE, P_SIZE), 1.0, 6.0, ((2, 2),))
    amplitudes = jnp.clip(0.2 + 1.8 * jax.random.uniform(streams_of[2], (NPOS, P_SIZE, P_SIZE), jnp.float32) ** block_scale(streams_of[2], (NPOS, P_SIZE, P_SIZE), ((0, 16), (1, 2)), -0.2, 0.2), 0.2, 2.0)
    row_offsets = with_ends(jax.random.randint(streams_of[3], (NPOS,), 0, TH), jax.random.fold_in(streams_of[3], 1), 0, TH - 1).astype(jnp.int32)
    position_counts = draw_position_counts(jax.random.fold_in(streams_of[5], 71), 0)
    return dict(object_slab=object_slab, probe_wave=probe_wave, amplitudes=amplitudes, row_offsets=row_offsets, position_counts=position_counts)


fresnel = 0.5
smooth = 1.0

def tables():
    index = jnp.arange(P_SIZE, dtype=jnp.int32)
    modded = index[:, None] * index[None, :] % P_SIZE
    angles = 2.0 * jnp.pi / P_SIZE * modded.astype(jnp.float32)
    cosine = jnp.cos(angles)
    sine_table = jnp.sin(angles)
    scaling = 1.0 / math.sqrt(P_SIZE)
    far_table = jnp.stack([cosine * scaling, -sine_table * scaling]).astype(jnp.bfloat16)
    centred = jnp.where(index < P_SIZE // 2, index, index - P_SIZE).astype(jnp.float32)
    phases = -jnp.pi * fresnel / P_SIZE * centred * centred
    kernel_real = jnp.cos(phases)
    kernel_imag = jnp.sin(phases)
    scaled_real = cosine * kernel_real[None, :] - sine_table * kernel_imag[None, :]
    scaled_imag = cosine * kernel_imag[None, :] + sine_table * kernel_real[None, :]
    highest = lax.Precision.HIGHEST
    fresnel_real = (jnp.dot(scaled_real, cosine, precision=highest) + jnp.dot(scaled_imag, sine_table, precision=highest)) / P_SIZE
    fresnel_imag = (jnp.dot(scaled_imag, cosine, precision=highest) - jnp.dot(scaled_real, sine_table, precision=highest)) / P_SIZE
    return (far_table, jnp.stack([fresnel_real, fresnel_imag]).astype(jnp.bfloat16))

def product(left, right):
    return jnp.dot(left.astype(jnp.float32), right.astype(jnp.float32), preferred_element_type=jnp.float32)

def left_apply(table, conjugate, real_part, imaginary):
    table_real = table[0]
    table_imag = -table[1] if conjugate else table[1]
    return (product(table_real, real_part) - product(table_imag, imaginary), product(table_real, imaginary) + product(table_imag, real_part))

def right_apply(table, conjugate, real_part, imaginary):
    table_real = table[0]
    table_imag = -table[1] if conjugate else table[1]
    return (product(real_part, table_real) - product(imaginary, table_imag), product(real_part, table_imag) + product(imaginary, table_real))

def halves(pair):
    return (pair[0].astype(jnp.bfloat16), pair[1].astype(jnp.bfloat16))

def position_terms(patch, probe_wave, measured, far_table, fresnel_table):
    single = jnp.float32
    first_real = patch[0, 0].astype(single)
    first_imag = patch[0, 1].astype(single)
    second_real = patch[1, 0].astype(single)
    second_imag = patch[1, 1].astype(single)
    probe_real = probe_wave[0].astype(single)
    probe_imag = probe_wave[1].astype(single)
    psi_one = halves((probe_real * first_real - probe_imag * first_imag, probe_real * first_imag + probe_imag * first_real))
    half_one = halves(left_apply(fresnel_table, False, psi_one[0], psi_one[1]))
    psi_two = halves(right_apply(fresnel_table, False, half_one[0], half_one[1]))
    wave_real = psi_two[0].astype(single)
    wave_imag = psi_two[1].astype(single)
    exit_wave = halves((wave_real * second_real - wave_imag * second_imag, wave_real * second_imag + wave_imag * second_real))
    half_two = halves(left_apply(far_table, False, exit_wave[0], exit_wave[1]))
    field_real, field_imag = right_apply(far_table, False, half_two[0], half_two[1])
    modulus = jnp.sqrt(field_real * field_real + field_imag * field_imag + smooth)
    keeping = 1.0 - measured / modulus
    chi_wave = halves((field_real * keeping, field_imag * keeping))
    back_one = halves(right_apply(far_table, True, chi_wave[0], chi_wave[1]))
    exit_real, exit_imag = left_apply(far_table, True, back_one[0], back_one[1])
    term_two = jnp.stack([wave_real * exit_real + wave_imag * exit_imag, wave_real * exit_imag - wave_imag * exit_real])
    grad_wave = halves((second_real * exit_real + second_imag * exit_imag, second_real * exit_imag - second_imag * exit_real))
    back_two = halves(right_apply(fresnel_table, True, grad_wave[0], grad_wave[1]))
    enter_real, enter_imag = left_apply(fresnel_table, True, back_two[0], back_two[1])
    term_one = jnp.stack([probe_real * enter_real + probe_imag * enter_imag, probe_real * enter_imag - probe_imag * enter_real])
    return jnp.stack([term_one, term_two])

def reference(object_slab, probe_wave, amplitudes, row_offsets, position_counts):
    far_table, fresnel_table = tables()
    slab_half = object_slab.astype(jnp.bfloat16)
    total = jnp.zeros(object_slab.shape, jnp.float32)

    def visit(position, total):
        position = jnp.asarray(position).astype(jnp.int32)
        home_tile = position // POS_DEV
        slot_index = position % POS_DEV
        start = (home_tile * TH + row_offsets[position]).astype(jnp.int32)

        def update(total):
            patch = lax.dynamic_slice_in_dim(slab_half, start, P_SIZE, 2)
            terms = position_terms(patch, probe_wave, amplitudes[position], far_table, fresnel_table)
            current = lax.dynamic_slice_in_dim(total, start, P_SIZE, 2)
            return lax.dynamic_update_slice_in_dim(total, current + terms, start, 2)

        def unchanged(total):
            return total
        return lax.cond(slot_index < position_counts[home_tile], update, unchanged, total)
    return lax.fori_loop(0, NPOS, visit, total)
```

```python
import functools
import math

import jax
import jax.numpy as jnp
import ml_dtypes
import numpy as np
from jax import lax
from jax.experimental import pallas as pl
from jax.experimental.pallas import tpu as pltpu
from jax.sharding import PartitionSpec as P

fresnel = 0.5
smooth = 1.0
bf16 = jnp.bfloat16
f32 = jnp.float32


def tables(size):
    index = np.arange(size)
    angles = 2.0 * np.pi / size * (index[:, None] * index[None, :] % size)
    base = np.exp(1j * angles)
    far = np.conj(base) / math.sqrt(size)
    centred = np.where(index < size // 2, index, index - size).astype(np.float64)
    kernel = np.exp(-1j * np.pi * fresnel / size * centred * centred)
    near = (base * kernel[None, :]) @ np.conj(base).T / size

    def parts(table):
        stacked = np.stack([table.real, table.imag, -table.imag])
        return jnp.asarray(stacked.astype(ml_dtypes.bfloat16))

    return parts(far), parts(near)


def left(table, conjugate, wave, size):
    plus, minus = (1, 2) if not conjugate else (2, 1)
    top = jnp.concatenate([table[0], table[minus]], axis=1)
    bottom = jnp.concatenate([table[plus], table[0]], axis=1)
    real = jnp.dot(top, wave, preferred_element_type=f32)
    imag = jnp.dot(bottom, wave, preferred_element_type=f32)
    return real, imag


def right(table, conjugate, wave, size):
    plus, minus = (1, 2) if not conjugate else (2, 1)
    real_side = jnp.concatenate([table[0], table[minus]], axis=0)
    imag_side = jnp.concatenate([table[plus], table[0]], axis=0)
    real = jnp.dot(wave, real_side, preferred_element_type=f32)
    imag = jnp.dot(wave, imag_side, preferred_element_type=f32)
    return real, imag


def roll_kernel(size, meta, probe, far, probe_out, near_side, far_side):
    offset = meta[0]
    row = lax.broadcasted_iota(jnp.int32, (size, size), 0)
    col = lax.broadcasted_iota(jnp.int32, (size, size), 1)
    gap = row - col - offset
    down = jnp.where((gap == 0) | (gap == -size), 1.0, 0.0).astype(bf16)
    gap = col - row - offset
    across = jnp.where((gap == 0) | (gap == -size), 1.0, 0.0).astype(bf16)
    for c in range(2):
        whole = jnp.concatenate([probe[h, c] for h in range(probe.shape[0])], axis=1)
        probe_out[c] = jnp.dot(down, whole, preferred_element_type=f32).astype(bf16)
    for c in range(3):
        near_side[c] = jnp.dot(far[c], across, preferred_element_type=f32).astype(bf16)
        far_side[c] = jnp.dot(down, far[c], preferred_element_type=f32).astype(bf16)


def rolled(probe, far, meta, size):
    whole = pl.BlockSpec(memory_space=pltpu.VMEM)
    return pl.pallas_call(
        functools.partial(roll_kernel, size),
        out_shape=[
            jax.ShapeDtypeStruct((2, size, size), bf16),
            jax.ShapeDtypeStruct(far.shape, bf16),
            jax.ShapeDtypeStruct(far.shape, bf16),
        ],
        in_specs=[pl.BlockSpec(memory_space=pltpu.SMEM), whole, whole],
        out_specs=[whole] * 3,
        compiler_params=pltpu.CompilerParams(vmem_limit_bytes=32 * 1024 * 1024),
        cost_estimate=pl.CostEstimate(
            flops=16 * size**3, bytes_accessed=24 * size * size, transcendentals=0
        ),
        name="rolled",
    )(meta, probe, far)


def wave_kernel(
    size, span, tiles, tile_rows,
    meta, windows, probe_hbm, amp_hbm, far_hbm, far_near_hbm, far_far_hbm, near_hbm, out_hbm,
    wave, last, probe, amps, far, far_near, far_far, near, rows_buf, cols_buf, psi2, zero, sems,
):
    offset, live, base = meta[0], meta[1], meta[2]
    parts = windows.shape[1]
    half = size // parts

    @pl.when(live == 1)
    def _():
        loads = [
            pltpu.make_async_copy(probe_hbm, probe, sems.at[0]),
            pltpu.make_async_copy(near_hbm, near, sems.at[1]),
            pltpu.make_async_copy(far_near_hbm, far_near, sems.at[2]),
            pltpu.make_async_copy(far_hbm, far, sems.at[3]),
            pltpu.make_async_copy(amp_hbm, amps, sems.at[4]),
            pltpu.make_async_copy(far_far_hbm, far_far, sems.at[5]),
            pltpu.make_async_copy(windows.at[base + span], last, sems.at[6]),
        ]
        chunks = []
        for k in range(span):
            for h in range(parts):
                chunks.append(
                    pltpu.make_async_copy(
                        windows.at[base + k, h],
                        wave.at[:, :, pl.ds(k * tile_rows, tile_rows), pl.ds(h * half, half)],
                        sems.at[7 + parts * k + h],
                    )
                )
        for one in loads[6:] + chunks + loads[:6]:
            one.start()
        for one in loads[6:] + chunks:
            one.wait()
        early = lax.broadcasted_iota(jnp.int32, (tile_rows, half), 0) < offset
        for s in range(2):
            for c in range(2):
                for h in range(parts):
                    cols = pl.ds(h * half, half)
                    wave[s, c, 0:tile_rows, cols] = jnp.where(
                        early, last[h, s, c].astype(f32), wave[s, c, 0:tile_rows, cols].astype(f32)
                    ).astype(bf16)

        def put_rows(pair):
            rows_buf[0:size, :] = pair[0].astype(bf16)
            rows_buf[size : 2 * size, :] = pair[1].astype(bf16)

        def put_cols(pair):
            cols_buf[:, 0:size] = pair[0].astype(bf16)
            cols_buf[:, size : 2 * size] = pair[1].astype(bf16)

        def pair_of(ref):
            return ref[0].astype(f32), ref[1].astype(f32)

        loads[0].wait()
        loads[1].wait()
        pr, pi = pair_of(probe)
        ar, ai = pair_of(wave.at[0])
        put_rows((pr * ar - pi * ai, pr * ai + pi * ar))
        put_cols(left(near, False, rows_buf[...], size))
        two = right(near, False, cols_buf[...], size)
        psi2[0] = two[0].astype(bf16)
        psi2[1] = two[1].astype(bf16)
        wr, wi = pair_of(psi2)
        br, bi = pair_of(wave.at[1])
        put_rows((wr * br - wi * bi, wr * bi + wi * br))
        loads[2].wait()
        put_cols(left(far_near, False, rows_buf[...], size))
        loads[3].wait()
        fr, fi = right(far, False, cols_buf[...], size)
        loads[4].wait()
        keeping = 1.0 - amps[...].astype(f32) * lax.rsqrt(fr * fr + fi * fi + smooth)
        put_cols((fr * keeping, fi * keeping))
        put_rows(right(far, True, cols_buf[...], size))
        loads[5].wait()
        er, ei = left(far_far, True, rows_buf[...], size)
        br, bi = pair_of(wave.at[1])
        put_cols((br * er + bi * ei, br * ei - bi * er))
        wr, wi = pair_of(psi2)
        wave[1, 0] = (wr * er + wi * ei).astype(bf16)
        wave[1, 1] = (wr * ei - wi * er).astype(bf16)
        put_rows(right(near, True, cols_buf[...], size))
        gr, gi = left(near, True, rows_buf[...], size)
        pr, pi = pair_of(probe)
        wave[0, 0] = (pr * gr + pi * gi).astype(bf16)
        wave[0, 1] = (pr * gi - pi * gr).astype(bf16)
        zero[...] = jnp.zeros(zero.shape, bf16)
        for s in range(2):
            for c in range(2):
                for h in range(parts):
                    cols = pl.ds(h * half, half)
                    both = wave[s, c, 0:tile_rows, cols].astype(f32)
                    last[h, s, c] = jnp.where(early, both, 0.0).astype(bf16)
                    wave[s, c, 0:tile_rows, cols] = jnp.where(early, 0.0, both).astype(bf16)
        stores = [pltpu.make_async_copy(last, out_hbm.at[base + span], sems.at[6])]
        for k in range(span):
            for h in range(parts):
                stores.append(
                    pltpu.make_async_copy(
                        wave.at[:, :, pl.ds(k * tile_rows, tile_rows), pl.ds(h * half, half)],
                        out_hbm.at[base + k, h],
                        sems.at[7 + parts * k + h],
                    )
                )
        for k in range(tiles - span - 1):
            place = lax.rem(base + span + 1 + k, tiles)
            stores.append(
                pltpu.make_async_copy(zero, out_hbm.at[place], sems.at[7 + parts * span + k])
            )
        for one in stores:
            one.start()
        for one in stores:
            one.wait()

    @pl.when(live == 0)
    def _():
        zero[...] = jnp.zeros(zero.shape, bf16)
        stores = [
            pltpu.make_async_copy(zero, out_hbm.at[k], sems.at[7 + k]) for k in range(tiles)
        ]
        for one in stores:
            one.start()
        for one in stores:
            one.wait()


def waves(windows, probe, amps, meta, size):
    tiles, parts, _, _, tile_rows, _ = windows.shape
    span = size // tile_rows
    far, near = tables(size)
    turned, far_near, far_far = rolled(probe, far, meta, size)
    anywhere = pl.BlockSpec(memory_space=pl.ANY)
    return pl.pallas_call(
        functools.partial(wave_kernel, size, span, tiles, tile_rows),
        out_shape=jax.ShapeDtypeStruct(windows.shape, bf16),
        in_specs=[pl.BlockSpec(memory_space=pltpu.SMEM)] + [anywhere] * 7,
        out_specs=anywhere,
        scratch_shapes=[
            pltpu.VMEM((2, 2, size, size), bf16),
            pltpu.VMEM(windows.shape[1:], bf16),
            pltpu.VMEM((2, size, size), bf16),
            pltpu.VMEM((size, size), amps.dtype),
            pltpu.VMEM(far.shape, bf16),
            pltpu.VMEM(far.shape, bf16),
            pltpu.VMEM(far.shape, bf16),
            pltpu.VMEM(near.shape, bf16),
            pltpu.VMEM((2 * size, size), bf16),
            pltpu.VMEM((size, 2 * size), bf16),
            pltpu.VMEM((2, size, size), bf16),
            pltpu.VMEM(windows.shape[1:], bf16),
            pltpu.SemaphoreType.DMA((7 + parts * span + tiles,)),
        ],
        compiler_params=pltpu.CompilerParams(vmem_limit_bytes=56 * 1024 * 1024),
        cost_estimate=pl.CostEstimate(
            flops=64 * size**3, bytes_accessed=24 * size * size, transcendentals=size * size
        ),
        name="waves",
    )(meta, windows, turned, amps, far, far_near, far_far, near)


def passed_along(value, axis, steps):
    count = lax.axis_size(axis)
    first, last = (max(0, -steps), min(count, count - steps))
    return lax.ppermute(value, axis, [(source, source + steps) for source in range(first, last)])


def shards(size, object_slab, probe_wave, amplitudes, row_offsets, position_counts):
    tile_rows = object_slab.shape[2]
    span = size // tile_rows
    tile_count = lax.axis_size("tile")
    small = tile_count <= 2 * span
    tile = lax.axis_index("tile")
    slot = lax.axis_index("scan")
    own = object_slab.astype(bf16)
    parts = lax.axis_size("scan")
    slots = amplitudes.shape[0]
    if parts == slots == 2:
        other = amplitudes[1 - slot].astype(bf16)
        mine = amplitudes[slot].astype(bf16)
        theirs = lax.ppermute(other, "scan", [(0, 1), (1, 0)])
        amps = jnp.concatenate(
            [jnp.where(slot == 0, mine, theirs), jnp.where(slot == 0, theirs, mine)]
        )
    else:
        every = lax.all_gather(amplitudes.astype(bf16), "scan")
        amps = every[:, jnp.minimum(slot, slots - 1)].reshape((size, size))
    probe = lax.all_gather(probe_wave, "scan")
    if small:
        windows = lax.all_gather(own, ("tile", "scan")).reshape((tile_count, parts) + own.shape)
        base = jnp.minimum(tile, tile_count - span - 1)
    else:
        pieces = [own] + [passed_along(own, "tile", -d) for d in range(1, span + 1)]
        windows = jnp.swapaxes(lax.all_gather(jnp.stack(pieces), "scan"), 0, 1)
        base = jnp.int32(0)
    live = (slot < position_counts[0]).astype(jnp.int32)
    if small:
        live = jnp.where(tile + span < tile_count, live, 0)
    meta = jnp.stack([row_offsets[jnp.minimum(slot, slots - 1)], live, base.astype(jnp.int32)])
    terms = waves(windows, probe, amps, meta, size)
    if small:
        chunks = terms.reshape((parts * tile_count,) + own.shape)
        result = lax.psum_scatter(chunks, ("tile", "scan"), scatter_dimension=0, tiled=False)
        return result.astype(f32)
    summed = lax.psum_scatter(jnp.swapaxes(terms, 0, 1), "scan", scatter_dimension=0, tiled=False)
    parts = [summed[k].astype(f32) for k in range(span + 1)]
    parts[0] = parts[0] + passed_along(summed[span], "tile", span).astype(f32)
    for level in reversed(range(span.bit_length() - 1)):
        stride = 1 << level
        block = jnp.stack(parts[stride : 2 * stride]).astype(bf16)
        moved = passed_along(block, "tile", stride)
        for number in range(stride):
            parts[number] = parts[number] + moved[number].astype(f32)
    return parts[0]


def solution(mesh):
    in_specs = (
        P(None, None, "tile", "scan"),
        P(None, None, "scan"),
        P("tile", "scan", None),
        P("tile"),
        P("tile"),
    )
    out_specs = P(None, None, "tile", "scan")

    def run(object_slab, *rest):
        return jax.shard_map(
            functools.partial(shards, object_slab.shape[3]),
            mesh=mesh, in_specs=in_specs, out_specs=out_specs, check_vma=False,
        )(object_slab, *rest)

    return run
```

```python
import functools
import math

import jax
import jax.numpy as jnp
import ml_dtypes
import numpy as np
from jax import lax
from jax.experimental import pallas as pl
from jax.experimental.pallas import tpu as pltpu
from jax.sharding import PartitionSpec as P

fresnel = 0.5
smooth = 1.0
bf16 = jnp.bfloat16
f32 = jnp.float32


def tables(size):
    index = np.arange(size)
    angles = 2.0 * np.pi / size * (index[:, None] * index[None, :] % size)
    base = np.exp(1j * angles)
    far = np.conj(base) / math.sqrt(size)
    centred = np.where(index < size // 2, index, index - size).astype(np.float64)
    kernel = np.exp(-1j * np.pi * fresnel / size * centred * centred)
    near = (base * kernel[None, :]) @ np.conj(base).T / size

    def parts(table):
        stacked = np.stack([table.real, table.imag, -table.imag])
        return jnp.asarray(stacked.astype(ml_dtypes.bfloat16))

    return parts(far), parts(near)


def left(table, conjugate, wave, size):
    plus, minus = (1, 2) if not conjugate else (2, 1)
    top = jnp.concatenate([table[0], table[minus]], axis=1)
    bottom = jnp.concatenate([table[plus], table[0]], axis=1)
    real = jnp.dot(top, wave, preferred_element_type=f32)
    imag = jnp.dot(bottom, wave, preferred_element_type=f32)
    return real, imag


def right(table, conjugate, wave, size):
    plus, minus = (1, 2) if not conjugate else (2, 1)
    real_side = jnp.concatenate([table[0], table[minus]], axis=0)
    imag_side = jnp.concatenate([table[plus], table[0]], axis=0)
    real = jnp.dot(wave, real_side, preferred_element_type=f32)
    imag = jnp.dot(wave, imag_side, preferred_element_type=f32)
    return real, imag


def roll_kernel(size, meta, far, *refs):
    pieces, (probe_out, near_side, far_side) = refs[:-3], refs[-3:]
    offset, slot = meta[0], meta[2]
    row = lax.broadcasted_iota(jnp.int32, (size, size), 0)
    col = lax.broadcasted_iota(jnp.int32, (size, size), 1)
    gap = row - col - offset
    down = jnp.where((gap == 0) | (gap == -size), 1.0, 0.0).astype(bf16)
    gap = col - row - offset
    across = jnp.where((gap == 0) | (gap == -size), 1.0, 0.0).astype(bf16)
    for c in range(3):
        near_side[c] = jnp.dot(far[c], across, preferred_element_type=f32).astype(bf16)
        far_side[c] = jnp.dot(down, far[c], preferred_element_type=f32).astype(bf16)
    for c in range(2):
        done = 0
        for piece in pieces:
            turned = jnp.dot(down, piece[c], preferred_element_type=f32).astype(bf16)
            width = turned.shape[1]
            if len(pieces) == 2:
                at = pl.multiple_of(jnp.where(slot == done, 0, width), width)
                probe_out[c, :, pl.ds(at, width)] = turned
                done += 1
            else:
                probe_out[c, :, done : done + width] = turned
                done += width


def rolled(pieces, far, meta, size):
    whole = pl.BlockSpec(memory_space=pltpu.VMEM)
    return pl.pallas_call(
        functools.partial(roll_kernel, size),
        out_shape=[
            jax.ShapeDtypeStruct((2, size, size), bf16),
            jax.ShapeDtypeStruct(far.shape, bf16),
            jax.ShapeDtypeStruct(far.shape, bf16),
        ],
        in_specs=[pl.BlockSpec(memory_space=pltpu.SMEM)] + [whole] * (1 + len(pieces)),
        out_specs=[whole] * 3,
        compiler_params=pltpu.CompilerParams(vmem_limit_bytes=32 * 1024 * 1024),
        cost_estimate=pl.CostEstimate(
            flops=16 * size**3, bytes_accessed=24 * size * size, transcendentals=0
        ),
        name="rolled",
    )(meta, far, *pieces)


def wave_kernel(
    size, span, tile_rows,
    meta, mine, theirs, probe_hbm, far_hbm, far_near_hbm, far_far_hbm, near_hbm, *refs,
):
    measured = refs[:-16]
    keep, send = refs[-16:-14]
    wave, last, probe, amps, far, far_near, far_far, near = refs[-14:-6]
    rows_buf, cols_buf, psi2, zero, sems, amp_sems = refs[-6:]
    offset, live, slot, core = meta[0], meta[1], meta[2], meta[3]
    parts = mine.shape[1]
    half = size // parts

    def chunk(same, other, k):
        return same.at[k // 2] if k % 2 == 0 else other.at[k // 2 + core]

    @pl.when(live == 1)
    def _():
        loads = [
            pltpu.make_async_copy(probe_hbm, probe, sems.at[0]),
            pltpu.make_async_copy(near_hbm, near, sems.at[1]),
            pltpu.make_async_copy(far_near_hbm, far_near, sems.at[2]),
            pltpu.make_async_copy(far_hbm, far, sems.at[3]),
            pltpu.make_async_copy(far_far_hbm, far_far, sems.at[4]),
            pltpu.make_async_copy(chunk(mine, theirs, span), last, sems.at[5]),
        ]
        amp_loads = []
        for number, piece in enumerate(measured):
            rows = piece.shape[0]
            at = pl.multiple_of(jnp.where(slot == number, 0, size - rows), rows)
            amp_loads.append(
                pltpu.make_async_copy(piece, amps.at[pl.ds(at, rows)], amp_sems.at[number])
            )
        chunks = []
        for k in range(span):
            for h in range(parts):
                chunks.append(
                    pltpu.make_async_copy(
                        chunk(mine, theirs, k).at[h],
                        wave.at[:, :, pl.ds(k * tile_rows, tile_rows), pl.ds(h * half, half)],
                        sems.at[6 + parts * k + h],
                    )
                )
        for one in loads[5:] + chunks + loads[:4] + amp_loads + loads[4:5]:
            one.start()
        for one in loads[5:] + chunks:
            one.wait()
        early = lax.broadcasted_iota(jnp.int32, (tile_rows, half), 0) < offset
        for s in range(2):
            for c in range(2):
                for h in range(parts):
                    cols = pl.ds(h * half, half)
                    wave[s, c, 0:tile_rows, cols] = jnp.where(
                        early, last[h, s, c].astype(f32), wave[s, c, 0:tile_rows, cols].astype(f32)
                    ).astype(bf16)

        def put_rows(pair):
            rows_buf[0:size, :] = pair[0].astype(bf16)
            rows_buf[size : 2 * size, :] = pair[1].astype(bf16)

        def put_cols(pair):
            cols_buf[:, 0:size] = pair[0].astype(bf16)
            cols_buf[:, size : 2 * size] = pair[1].astype(bf16)

        def pair_of(ref):
            return ref[0].astype(f32), ref[1].astype(f32)

        loads[0].wait()
        loads[1].wait()
        pr, pi = pair_of(probe)
        ar, ai = pair_of(wave.at[0])
        put_rows((pr * ar - pi * ai, pr * ai + pi * ar))
        put_cols(left(near, False, rows_buf[...], size))
        two = right(near, False, cols_buf[...], size)
        psi2[0] = two[0].astype(bf16)
        psi2[1] = two[1].astype(bf16)
        wr, wi = pair_of(psi2)
        br, bi = pair_of(wave.at[1])
        put_rows((wr * br - wi * bi, wr * bi + wi * br))
        loads[2].wait()
        put_cols(left(far_near, False, rows_buf[...], size))
        loads[3].wait()
        fr, fi = right(far, False, cols_buf[...], size)
        for one in amp_loads:
            one.wait()
        keeping = 1.0 - amps[...].astype(f32) * lax.rsqrt(fr * fr + fi * fi + smooth)
        put_cols((fr * keeping, fi * keeping))
        put_rows(right(far, True, cols_buf[...], size))
        loads[4].wait()
        er, ei = left(far_far, True, rows_buf[...], size)
        br, bi = pair_of(wave.at[1])
        put_cols((br * er + bi * ei, br * ei - bi * er))
        wr, wi = pair_of(psi2)
        wave[1, 0] = (wr * er + wi * ei).astype(bf16)
        wave[1, 1] = (wr * ei - wi * er).astype(bf16)
        put_rows(right(near, True, cols_buf[...], size))
        gr, gi = left(near, True, rows_buf[...], size)
        pr, pi = pair_of(probe)
        wave[0, 0] = (pr * gr + pi * gi).astype(bf16)
        wave[0, 1] = (pr * gi - pi * gr).astype(bf16)
        zero[...] = jnp.zeros(zero.shape, bf16)
        for s in range(2):
            for c in range(2):
                for h in range(parts):
                    cols = pl.ds(h * half, half)
                    both = wave[s, c, 0:tile_rows, cols].astype(f32)
                    last[h, s, c] = jnp.where(early, both, 0.0).astype(bf16)
                    wave[s, c, 0:tile_rows, cols] = jnp.where(early, 0.0, both).astype(bf16)
        stores = [
            pltpu.make_async_copy(last, chunk(keep, send, span), sems.at[5]),
            pltpu.make_async_copy(zero, send.at[(1 - core) * (span // 2)], sems.at[0]),
        ]
        for k in range(span):
            for h in range(parts):
                stores.append(
                    pltpu.make_async_copy(
                        wave.at[:, :, pl.ds(k * tile_rows, tile_rows), pl.ds(h * half, half)],
                        chunk(keep, send, k).at[h],
                        sems.at[6 + parts * k + h],
                    )
                )
        for one in stores:
            one.start()
        for one in stores:
            one.wait()

    @pl.when(live == 0)
    def _():
        zero[...] = jnp.zeros(zero.shape, bf16)
        stores = []
        for k in range(span // 2 + 1):
            stores.append(pltpu.make_async_copy(zero, keep.at[k], sems.at[2 * k]))
            stores.append(pltpu.make_async_copy(zero, send.at[k], sems.at[2 * k + 1]))
        for one in stores:
            one.start()
        for one in stores:
            one.wait()


def waves(mine, theirs, probe_pieces, amp_pieces, meta, size):
    parts, _, _, tile_rows, _ = mine.shape[1:]
    span = size // tile_rows
    far, near = tables(size)
    turned, far_near, far_far = rolled(probe_pieces, far, meta, size)
    anywhere = pl.BlockSpec(memory_space=pl.ANY)
    return pl.pallas_call(
        functools.partial(wave_kernel, size, span, tile_rows),
        out_shape=[jax.ShapeDtypeStruct(mine.shape, bf16)] * 2,
        in_specs=[pl.BlockSpec(memory_space=pltpu.SMEM)] + [anywhere] * (7 + len(amp_pieces)),
        out_specs=[anywhere] * 2,
        scratch_shapes=[
            pltpu.VMEM((2, 2, size, size), bf16),
            pltpu.VMEM(mine.shape[1:], bf16),
            pltpu.VMEM((2, size, size), bf16),
            pltpu.VMEM((size, size), bf16),
            pltpu.VMEM(far.shape, bf16),
            pltpu.VMEM(far.shape, bf16),
            pltpu.VMEM(far.shape, bf16),
            pltpu.VMEM(near.shape, bf16),
            pltpu.VMEM((2 * size, size), bf16),
            pltpu.VMEM((size, 2 * size), bf16),
            pltpu.VMEM((2, size, size), bf16),
            pltpu.VMEM(mine.shape[1:], bf16),
            pltpu.SemaphoreType.DMA((6 + parts * span,)),
            pltpu.SemaphoreType.DMA((len(amp_pieces),)),
        ],
        compiler_params=pltpu.CompilerParams(vmem_limit_bytes=56 * 1024 * 1024),
        cost_estimate=pl.CostEstimate(
            flops=64 * size**3, bytes_accessed=24 * size * size, transcendentals=size * size
        ),
        name="waves",
    )(meta, mine, theirs, turned, far, far_near, far_far, near, *amp_pieces)


def shards(size, object_slab, probe_wave, amplitudes, row_offsets, position_counts):
    tile_rows = object_slab.shape[2]
    span = size // tile_rows
    count = lax.axis_size("tile")
    parts = lax.axis_size("scan")
    slots = amplitudes.shape[0]
    paired = parts == slots == 2
    slot = lax.axis_index("scan")
    ahead = span // 2
    homes = range(ahead, count - ahead)
    swap = [(0, 1), (1, 0)]

    def brought(value, steps):
        return lax.ppermute(value, "tile", [(home + steps, home) for home in homes])

    def returned(value, steps):
        return lax.ppermute(value, "tile", [(home, home + steps) for home in homes])

    def to_partner(value):
        return lax.ppermute(value, "tile", [(home, home ^ 1) for home in homes])

    def by_slot(first, second):
        return jnp.where(slot == 0, first, second)

    own = object_slab.astype(bf16)
    if paired:
        beside = lax.ppermute(own, "scan", swap)
        whole = jnp.stack([by_slot(own, beside), by_slot(beside, own)])
        probe_pieces = [probe_wave, lax.ppermute(probe_wave, "scan", swap)]
    else:
        whole = lax.all_gather(own, "scan")
        every = lax.all_gather(probe_wave, "scan")
        probe_pieces = [every[number] for number in range(parts)]
    notes = brought(jnp.concatenate([row_offsets, position_counts]), -ahead)
    live = (slot < notes[slots]).astype(jnp.int32)
    core = lax.rem(lax.axis_index("tile"), 2)
    meta = jnp.stack(
        [notes[jnp.minimum(slot, slots - 1)], live, slot.astype(jnp.int32), core.astype(jnp.int32)]
    )
    steps = range(-ahead, ahead + 1, 2)
    mine = jnp.stack([brought(whole, step) if step else whole for step in steps])
    theirs = to_partner(mine)
    if paired:
        amp_pieces = [
            lax.ppermute(
                by_slot(amplitudes[which], amplitudes[1 - which]).astype(bf16),
                ("tile", "scan"),
                [
                    ((home - ahead) * 2 + x, home * 2 + (x + which) % 2)
                    for home in homes
                    for x in range(2)
                ],
            )
            for which in range(2)
        ]
    else:
        every = lax.all_gather(brought(amplitudes.astype(bf16), -ahead), "scan")
        amp_pieces = [every[:, jnp.minimum(slot, slots - 1)].reshape((size, size))]
    keep, send = waves(mine, theirs, probe_pieces, amp_pieces, meta, size)
    merged = (keep.astype(f32) + to_partner(send).astype(f32)).astype(bf16)
    total = sum(
        (returned(merged[i], step) if step else merged[i]).astype(f32)
        for i, step in enumerate(steps)
    )
    if paired:
        away = lax.ppermute(by_slot(total[1], total[0]).astype(bf16), "scan", swap)
        return by_slot(total[0], total[1]) + away.astype(f32)
    return lax.psum_scatter(total, "scan", scatter_dimension=0, tiled=False)


def solution(mesh):
    in_specs = (
        P(None, None, "tile", "scan"),
        P(None, None, "scan"),
        P("tile", "scan", None),
        P("tile"),
        P("tile"),
    )
    out_specs = P(None, None, "tile", "scan")

    def run(object_slab, *rest):
        return jax.shard_map(
            functools.partial(shards, object_slab.shape[3]),
            mesh=mesh, in_specs=in_specs, out_specs=out_specs, check_vma=False,
        )(object_slab, *rest)

    return run
```

```python
import functools
import math

import jax
import jax.numpy as jnp
import ml_dtypes
import numpy as np
from jax import lax
from jax.experimental import pallas as pl
from jax.experimental.pallas import tpu as pltpu
from jax.sharding import PartitionSpec as P

fresnel = 0.5
smooth = 1.0
bf16 = jnp.bfloat16
f32 = jnp.float32


def tables(size):
    index = np.arange(size)
    angles = 2.0 * np.pi / size * (index[:, None] * index[None, :] % size)
    base = np.exp(1j * angles)
    far = np.conj(base) / math.sqrt(size)
    centred = np.where(index < size // 2, index, index - size).astype(np.float64)
    kernel = np.exp(-1j * np.pi * fresnel / size * centred * centred)
    near = (base * kernel[None, :]) @ np.conj(base).T / size

    def parts(table):
        stacked = np.stack([table.real, table.imag, -table.imag])
        return jnp.asarray(stacked.astype(ml_dtypes.bfloat16))

    order = np.concatenate([index[0::2], index[1::2]])
    return parts(far[order]), parts(far[:, order]), parts(near)


def left(table, conjugate, wave):
    real, plus, minus = table if not conjugate else (table[0], table[2], table[1])
    top = jnp.concatenate([real, minus], axis=1)
    bottom = jnp.concatenate([plus, real], axis=1)
    return (
        jnp.dot(top, wave, preferred_element_type=f32),
        jnp.dot(bottom, wave, preferred_element_type=f32),
    )


def right(table, conjugate, wave):
    real, plus, minus = table if not conjugate else (table[0], table[2], table[1])
    real_side = jnp.concatenate([real, minus], axis=0)
    imag_side = jnp.concatenate([plus, real], axis=0)
    return (
        jnp.dot(wave, real_side, preferred_element_type=f32),
        jnp.dot(wave, imag_side, preferred_element_type=f32),
    )


def one_hot(size, hit):
    row = lax.broadcasted_iota(jnp.int32, (size, size), 0)
    col = lax.broadcasted_iota(jnp.int32, (size, size), 1)
    return jnp.where(hit(row, col), 1.0, 0.0).astype(bf16)


def roll_kernel(size, count, meta, far_rows, far_cols, *refs):
    pieces, measured = refs[:count], refs[count:-5]
    probe_out, near_side, far_side, ordered, amps = refs[-5:]
    offset, slot = meta[0], meta[2]
    half = size // 2

    def moved(to, source):
        gap = to - source - offset
        return (gap == 0) | (gap == -size)

    down = one_hot(size, moved)
    across = one_hot(size, lambda row, col: moved(col, row))
    for c in range(3):
        near_side[c] = jnp.dot(
            far_rows[c], across[:, :half], preferred_element_type=f32
        ).astype(bf16)
        far_side[c] = jnp.dot(down[:half], far_cols[c], preferred_element_type=f32).astype(bf16)
    for c in range(2):
        done = 0
        for piece in pieces:
            turned = jnp.dot(down, piece[c], preferred_element_type=f32).astype(bf16)
            width = turned.shape[1]
            if len(pieces) == 2:
                at = pl.multiple_of(jnp.where(slot == done, 0, width), width)
                probe_out[c, :, pl.ds(at, width)] = turned
                done += 1
            else:
                probe_out[c, :, done : done + width] = turned
                done += width
    for number, piece in enumerate(measured):
        rows = piece.shape[0]
        at = pl.multiple_of(jnp.where(slot == number, 0, size - rows), rows)
        amps[pl.ds(at, rows), :] = piece[...]

    def frequency(place, natural):
        return natural == jnp.where(place < half, 2 * place, 2 * (place - half) + 1)

    rows_first = jnp.dot(one_hot(size, frequency), amps[...], preferred_element_type=f32)
    ordered[...] = jnp.dot(
        rows_first.astype(bf16),
        one_hot(size, lambda row, col: frequency(col, row)),
        preferred_element_type=f32,
    ).astype(bf16)


def rolled(pieces, amp_pieces, far_rows, far_cols, meta, size):
    whole = pl.BlockSpec(memory_space=pltpu.VMEM)
    return pl.pallas_call(
        functools.partial(roll_kernel, size, len(pieces)),
        out_shape=[
            jax.ShapeDtypeStruct((2, size, size), bf16),
            jax.ShapeDtypeStruct((3, size, size // 2), bf16),
            jax.ShapeDtypeStruct((3, size // 2, size), bf16),
            jax.ShapeDtypeStruct((size, size), bf16),
        ],
        in_specs=[pl.BlockSpec(memory_space=pltpu.SMEM)]
        + [whole] * (2 + len(pieces) + len(amp_pieces)),
        out_specs=[whole] * 4,
        scratch_shapes=[pltpu.VMEM((size, size), bf16)],
        compiler_params=pltpu.CompilerParams(vmem_limit_bytes=24 * 1024 * 1024),
        cost_estimate=pl.CostEstimate(
            flops=64 * size**3, bytes_accessed=24 * size * size, transcendentals=0
        ),
        name="rolled",
    )(meta, far_rows, far_cols, *pieces, *amp_pieces)


def wave_kernel(
    size, span, tile_rows,
    meta, mine, theirs, far_rows_hbm, far_cols_hbm, near_hbm, probe, far_near, far_far, amps,
    keep, send, wave, last, far_rows, far_cols, near, rows_buf, cols_buf, psi2, zero, sems,
):
    offset, live, core = meta[0], meta[1], meta[3]
    parts = mine.shape[1]
    width = size // parts
    half = size // 2
    low, high = slice(0, half), slice(half, size)

    def chunk(same, other, k):
        return same.at[k // 2] if k % 2 == 0 else other.at[k // 2 + core]

    @pl.when(live == 1)
    def _():
        loads = [
            pltpu.make_async_copy(chunk(mine, theirs, span), last, sems.at[0]),
            pltpu.make_async_copy(near_hbm, near, sems.at[1]),
            pltpu.make_async_copy(far_cols_hbm.at[:, pl.ds(0, half)], far_cols, sems.at[2]),
            pltpu.make_async_copy(far_rows_hbm.at[:, :, pl.ds(0, half)], far_rows, sems.at[3]),
        ]
        chunks = []
        for k in range(span):
            for h in range(parts):
                chunks.append(
                    pltpu.make_async_copy(
                        chunk(mine, theirs, k).at[h],
                        wave.at[:, :, pl.ds(k * tile_rows, tile_rows), pl.ds(h * width, width)],
                        sems.at[4 + parts * k + h],
                    )
                )
        for one in loads[:1] + chunks + loads[1:]:
            one.start()
        for one in loads[:1] + chunks:
            one.wait()
        early = lax.broadcasted_iota(jnp.int32, (tile_rows, width), 0) < offset
        for s in range(2):
            for c in range(2):
                for h in range(parts):
                    cols = pl.ds(h * width, width)
                    wave[s, c, 0:tile_rows, cols] = jnp.where(
                        early, last[h, s, c].astype(f32), wave[s, c, 0:tile_rows, cols].astype(f32)
                    ).astype(bf16)

        def put_rows(pair):
            rows_buf[0:size, :] = pair[0].astype(bf16)
            rows_buf[size : 2 * size, :] = pair[1].astype(bf16)

        def put_cols(pair):
            cols_buf[:, 0:size] = pair[0].astype(bf16)
            cols_buf[:, size : 2 * size] = pair[1].astype(bf16)

        def pair_of(ref):
            return ref[0].astype(f32), ref[1].astype(f32)

        def parts_of(ref, rows, cols):
            return ref[0, rows, cols], ref[1, rows, cols], ref[2, rows, cols]

        def put_row_halves(first, second):
            for number, wave_half in enumerate((first, second)):
                for c in range(2):
                    at = number * size + c * half
                    rows_buf[at : at + half, :] = wave_half[c].astype(bf16)

        def put_col_halves(first, second):
            for number, wave_half in enumerate((first, second)):
                for c in range(2):
                    at = number * size + c * half
                    cols_buf[:, at : at + half] = wave_half[c].astype(bf16)

        def both(first, second, axis):
            return [jnp.concatenate([a, b], axis=axis) for a, b in zip(first, second)]

        def plus(first, second):
            return [a + b for a, b in zip(first, second)]

        def less(first, second):
            return [a - b for a, b in zip(first, second)]

        everything = slice(None)
        loads[1].wait()
        near_parts = parts_of(near, everything, everything)
        pr, pi = pair_of(probe)
        ar, ai = pair_of(wave.at[0])
        put_rows((pr * ar - pi * ai, pr * ai + pi * ar))
        put_cols(left(near_parts, False, rows_buf[...]))
        two = right(near_parts, False, cols_buf[...])
        psi2[0] = two[0].astype(bf16)
        psi2[1] = two[1].astype(bf16)
        wr, wi = pair_of(psi2)
        br, bi = pair_of(wave.at[1])
        wave_exit = (wr * br - wi * bi, wr * bi + wi * br)
        top, bottom = [x[low] for x in wave_exit], [x[high] for x in wave_exit]
        put_row_halves(plus(top, bottom), less(top, bottom))
        half2 = both(
            left(parts_of(far_near, low, everything), False, rows_buf[0:size, :]),
            left(parts_of(far_near, high, everything), False, rows_buf[size : 2 * size, :]),
            0,
        )
        top, bottom = [x[:, low] for x in half2], [x[:, high] for x in half2]
        put_col_halves(plus(top, bottom), less(top, bottom))
        loads[2].wait()
        fields = [
            right(parts_of(far_cols, everything, low), False, cols_buf[:, 0:size]),
            right(parts_of(far_cols, everything, high), False, cols_buf[:, size : 2 * size]),
        ]
        chis = []
        for (fr, fi), cols in zip(fields, (low, high)):
            keeping = 1.0 - amps[:, cols].astype(f32) * lax.rsqrt(fr * fr + fi * fi + smooth)
            chis.append((fr * keeping, fi * keeping))
        put_col_halves(*chis)
        loads[3].wait()
        even = right(parts_of(far_rows, low, everything), True, cols_buf[:, 0:size])
        odd = right(parts_of(far_rows, high, everything), True, cols_buf[:, size : 2 * size])
        back1 = both(plus(even, odd), less(even, odd), 1)
        put_row_halves([x[low] for x in back1], [x[high] for x in back1])
        even = left(parts_of(far_far, everything, low), True, rows_buf[0:size, :])
        odd = left(parts_of(far_far, everything, high), True, rows_buf[size : 2 * size, :])
        er, ei = both(plus(even, odd), less(even, odd), 0)
        br, bi = pair_of(wave.at[1])
        put_cols((br * er + bi * ei, br * ei - bi * er))
        wr, wi = pair_of(psi2)
        wave[1, 0] = (wr * er + wi * ei).astype(bf16)
        wave[1, 1] = (wr * ei - wi * er).astype(bf16)
        near_parts = parts_of(near, everything, everything)
        put_rows(right(near_parts, True, cols_buf[...]))
        gr, gi = left(near_parts, True, rows_buf[...])
        pr, pi = pair_of(probe)
        wave[0, 0] = (pr * gr + pi * gi).astype(bf16)
        wave[0, 1] = (pr * gi - pi * gr).astype(bf16)
        zero[...] = jnp.zeros(zero.shape, bf16)
        for s in range(2):
            for c in range(2):
                for h in range(parts):
                    cols = pl.ds(h * width, width)
                    mixed = wave[s, c, 0:tile_rows, cols].astype(f32)
                    last[h, s, c] = jnp.where(early, mixed, 0.0).astype(bf16)
                    wave[s, c, 0:tile_rows, cols] = jnp.where(early, 0.0, mixed).astype(bf16)
        stores = [
            pltpu.make_async_copy(last, chunk(keep, send, span), sems.at[0]),
            pltpu.make_async_copy(zero, send.at[(1 - core) * (span // 2)], sems.at[1]),
        ]
        for k in range(span):
            for h in range(parts):
                stores.append(
                    pltpu.make_async_copy(
                        wave.at[:, :, pl.ds(k * tile_rows, tile_rows), pl.ds(h * width, width)],
                        chunk(keep, send, k).at[h],
                        sems.at[4 + parts * k + h],
                    )
                )
        for one in stores:
            one.start()
        for one in stores:
            one.wait()

    @pl.when(live == 0)
    def _():
        zero[...] = jnp.zeros(zero.shape, bf16)
        stores = []
        for k in range(span // 2 + 1):
            stores.append(pltpu.make_async_copy(zero, keep.at[k], sems.at[2 * k]))
            stores.append(pltpu.make_async_copy(zero, send.at[k], sems.at[2 * k + 1]))
        for one in stores:
            one.start()
        for one in stores:
            one.wait()


def waves(mine, theirs, consts, turned, meta, size):
    parts, _, _, tile_rows, _ = mine.shape[1:]
    span = size // tile_rows
    anywhere = pl.BlockSpec(memory_space=pl.ANY)
    inside = pl.BlockSpec(memory_space=pltpu.VMEM)
    return pl.pallas_call(
        functools.partial(wave_kernel, size, span, tile_rows),
        out_shape=[jax.ShapeDtypeStruct(mine.shape, bf16)] * 2,
        in_specs=[pl.BlockSpec(memory_space=pltpu.SMEM)]
        + [anywhere] * 5
        + [inside] * 4,
        out_specs=[anywhere] * 2,
        scratch_shapes=[
            pltpu.VMEM((2, 2, size, size), bf16),
            pltpu.VMEM(mine.shape[1:], bf16),
            pltpu.VMEM((3, size, size // 2), bf16),
            pltpu.VMEM((3, size // 2, size), bf16),
            pltpu.VMEM((3, size, size), bf16),
            pltpu.VMEM((2 * size, size), bf16),
            pltpu.VMEM((size, 2 * size), bf16),
            pltpu.VMEM((2, size, size), bf16),
            pltpu.VMEM(mine.shape[1:], bf16),
            pltpu.SemaphoreType.DMA((4 + parts * span,)),
        ],
        compiler_params=pltpu.CompilerParams(vmem_limit_bytes=48 * 1024 * 1024),
        cost_estimate=pl.CostEstimate(
            flops=64 * size**3, bytes_accessed=24 * size * size, transcendentals=size * size
        ),
        name="waves",
    )(meta, mine, theirs, *consts, *turned)


def shards(size, object_slab, probe_wave, amplitudes, row_offsets, position_counts):
    tile_rows = object_slab.shape[2]
    span = size // tile_rows
    count = lax.axis_size("tile")
    parts = lax.axis_size("scan")
    slots = amplitudes.shape[0]
    paired = parts == slots == 2
    slot = lax.axis_index("scan")
    ahead = span // 2
    homes = range(ahead, count - ahead)
    swap = [(0, 1), (1, 0)]

    def brought(value, steps):
        return lax.ppermute(value, "tile", [(home + steps, home) for home in homes])

    def returned(value, steps):
        return lax.ppermute(value, "tile", [(home, home + steps) for home in homes])

    def to_partner(value):
        return lax.ppermute(value, "tile", [(home, home ^ 1) for home in homes])

    def by_slot(first, second):
        return jnp.where(slot == 0, first, second)

    own = object_slab.astype(bf16)
    if paired:
        beside = lax.ppermute(own, "scan", swap)
        whole = jnp.stack([by_slot(own, beside), by_slot(beside, own)])
        probe_pieces = [probe_wave, lax.ppermute(probe_wave, "scan", swap)]
    else:
        whole = lax.all_gather(own, "scan")
        every = lax.all_gather(probe_wave, "scan")
        probe_pieces = [every[number] for number in range(parts)]
    notes = brought(jnp.concatenate([row_offsets, position_counts]), -ahead)
    live = (slot < notes[slots]).astype(jnp.int32)
    core = lax.rem(lax.axis_index("tile"), 2)
    meta = jnp.stack(
        [notes[jnp.minimum(slot, slots - 1)], live, slot.astype(jnp.int32), core.astype(jnp.int32)]
    )
    if paired:
        amp_pieces = [
            lax.ppermute(
                by_slot(amplitudes[which], amplitudes[1 - which]).astype(bf16),
                ("tile", "scan"),
                [
                    ((home - ahead) * 2 + x, home * 2 + (x + which) % 2)
                    for home in homes
                    for x in range(2)
                ],
            )
            for which in range(2)
        ]
    else:
        every = lax.all_gather(brought(amplitudes.astype(bf16), -ahead), "scan")
        amp_pieces = [every[:, jnp.minimum(slot, slots - 1)].reshape((size, size))]
    far_rows, far_cols, near = tables(size)
    whole, meta = lax.optimization_barrier((whole, meta))
    turned = rolled(probe_pieces, amp_pieces, far_rows, far_cols, meta, size)
    steps = range(-ahead, ahead + 1, 2)
    kept, turned = lax.optimization_barrier((whole, turned))
    mine = jnp.stack([brought(whole, step) if step else kept for step in steps])
    theirs = to_partner(mine)
    keep, send = waves(mine, theirs, (far_rows, far_cols, near), turned, meta, size)
    merged = (keep.astype(f32) + to_partner(send).astype(f32)).astype(bf16)
    total = sum(
        (returned(merged[i], step) if step else merged[i]).astype(f32)
        for i, step in enumerate(steps)
    )
    if paired:
        away = lax.ppermute(by_slot(total[1], total[0]).astype(bf16), "scan", swap)
        return by_slot(total[0], total[1]) + away.astype(f32)
    return lax.psum_scatter(total, "scan", scatter_dimension=0, tiled=False)


def solution(mesh):
    in_specs = (
        P(None, None, "tile", "scan"),
        P(None, None, "scan"),
        P("tile", "scan", None),
        P("tile"),
        P("tile"),
    )
    out_specs = P(None, None, "tile", "scan")

    def run(object_slab, *rest):
        return jax.shard_map(
            functools.partial(shards, object_slab.shape[3]),
            mesh=mesh, in_specs=in_specs, out_specs=out_specs, check_vma=False,
        )(object_slab, *rest)

    return run
```

```python
import functools
import math

import jax
import jax.numpy as jnp
import ml_dtypes
import numpy as np
from jax import lax
from jax.experimental import pallas as pl
from jax.experimental.pallas import tpu as pltpu
from jax.sharding import PartitionSpec as P

fresnel = 0.5
smooth = 1.0
bf16 = jnp.bfloat16
f32 = jnp.float32


def tables(size):
    index = np.arange(size)
    angles = 2.0 * np.pi / size * (index[:, None] * index[None, :] % size)
    base = np.exp(1j * angles)
    far = np.conj(base) / math.sqrt(size)
    centred = np.where(index < size // 2, index, index - size).astype(np.float64)
    kernel = np.exp(-1j * np.pi * fresnel / size * centred * centred)
    near = (base * kernel[None, :]) @ np.conj(base).T / size

    def parts(table):
        stacked = np.stack([table.real, table.imag, -table.imag])
        return jnp.asarray(stacked.astype(ml_dtypes.bfloat16))

    order = np.concatenate([index[0::2], index[1::2]])
    return parts(far[order]), parts(far[:, order]), parts(near)


def left(table, conjugate, wave):
    real, plus, minus = table if not conjugate else (table[0], table[2], table[1])
    top = jnp.concatenate([real, minus], axis=1)
    bottom = jnp.concatenate([plus, real], axis=1)
    return (
        jnp.dot(top, wave, preferred_element_type=f32),
        jnp.dot(bottom, wave, preferred_element_type=f32),
    )


def right(table, conjugate, wave):
    real, plus, minus = table if not conjugate else (table[0], table[2], table[1])
    real_side = jnp.concatenate([real, minus], axis=0)
    imag_side = jnp.concatenate([plus, real], axis=0)
    return (
        jnp.dot(wave, real_side, preferred_element_type=f32),
        jnp.dot(wave, imag_side, preferred_element_type=f32),
    )


def one_hot(size, hit):
    row = lax.broadcasted_iota(jnp.int32, (size, size), 0)
    col = lax.broadcasted_iota(jnp.int32, (size, size), 1)
    return jnp.where(hit(row, col), 1.0, 0.0).astype(bf16)


def order_kernel(size, slot, *refs):
    measured, (ordered, amps) = refs[:-2], refs[-2:]
    half = size // 2
    for number, piece in enumerate(measured):
        rows = piece.shape[0]
        at = pl.multiple_of(jnp.where(slot[0] == number, 0, size - rows), rows)
        amps[pl.ds(at, rows), :] = piece[...]

    def frequency(place, natural):
        return natural == jnp.where(place < half, 2 * place, 2 * (place - half) + 1)

    rows_first = jnp.dot(one_hot(size, frequency), amps[...], preferred_element_type=f32)
    ordered[...] = jnp.dot(
        rows_first.astype(bf16),
        one_hot(size, lambda row, col: frequency(col, row)),
        preferred_element_type=f32,
    ).astype(bf16)


def in_order(amp_pieces, slot, size):
    whole = pl.BlockSpec(memory_space=pltpu.VMEM)
    return pl.pallas_call(
        functools.partial(order_kernel, size),
        out_shape=jax.ShapeDtypeStruct((size, size), bf16),
        in_specs=[pl.BlockSpec(memory_space=pltpu.SMEM)] + [whole] * len(amp_pieces),
        out_specs=whole,
        scratch_shapes=[pltpu.VMEM((size, size), bf16)],
        compiler_params=pltpu.CompilerParams(vmem_limit_bytes=16 * 1024 * 1024),
        cost_estimate=pl.CostEstimate(
            flops=4 * size**3, bytes_accessed=4 * size * size, transcendentals=0
        ),
        name="in_order",
    )(slot, *amp_pieces)


def roll_kernel(size, meta, far_rows, far_cols, *refs):
    pieces, (probe_out, near_side, far_side) = refs[:-3], refs[-3:]
    offset, slot = meta[0], meta[2]
    half = size // 2

    def moved(to, source):
        gap = to - source - offset
        return (gap == 0) | (gap == -size)

    down = one_hot(size, moved)
    across = one_hot(size, lambda row, col: moved(col, row))
    for c in range(3):
        near_side[c] = jnp.dot(
            far_rows[c], across[:, :half], preferred_element_type=f32
        ).astype(bf16)
        far_side[c] = jnp.dot(down[:half], far_cols[c], preferred_element_type=f32).astype(bf16)
    for c in range(2):
        done = 0
        for piece in pieces:
            turned = jnp.dot(down, piece[c], preferred_element_type=f32).astype(bf16)
            width = turned.shape[1]
            if len(pieces) == 2:
                at = pl.multiple_of(jnp.where(slot == done, 0, width), width)
                probe_out[c, :, pl.ds(at, width)] = turned
                done += 1
            else:
                probe_out[c, :, done : done + width] = turned
                done += width


def rolled(pieces, far_rows, far_cols, meta, size):
    whole = pl.BlockSpec(memory_space=pltpu.VMEM)
    return pl.pallas_call(
        functools.partial(roll_kernel, size),
        out_shape=[
            jax.ShapeDtypeStruct((2, size, size), bf16),
            jax.ShapeDtypeStruct((3, size, size // 2), bf16),
            jax.ShapeDtypeStruct((3, size // 2, size), bf16),
        ],
        in_specs=[pl.BlockSpec(memory_space=pltpu.SMEM)] + [whole] * (2 + len(pieces)),
        out_specs=[whole] * 3,
        compiler_params=pltpu.CompilerParams(vmem_limit_bytes=24 * 1024 * 1024),
        cost_estimate=pl.CostEstimate(
            flops=64 * size**3, bytes_accessed=24 * size * size, transcendentals=0
        ),
        name="rolled",
    )(meta, far_rows, far_cols, *pieces)


def wave_kernel(
    size, span, tile_rows,
    meta, mine, theirs, far_rows, far_cols, near, probe, far_near, far_far, amps,
    keep, send, rows_buf, cols_buf, psi2,
):
    offset, live, core = meta[0], meta[1], meta[3]
    parts = mine.shape[1]
    width = size // parts
    half = size // 2
    low, high = slice(0, half), slice(half, size)

    @pl.when(live == 1)
    def _():
        early = lax.broadcasted_iota(jnp.int32, (tile_rows, width), 0) < offset

        def place(k):
            return k // 2 if k % 2 == 0 else k // 2 + core

        def piece(k, h, s, c):
            source = mine if k % 2 == 0 else theirs
            return source[place(k), h, s, c].astype(f32)

        def patch(s, c):
            rows = []
            for k in range(span):
                blocks = [piece(k, h, s, c) for h in range(parts)]
                if k == 0:
                    blocks = [
                        jnp.where(early, piece(span, h, s, c), blocks[h]) for h in range(parts)
                    ]
                rows.append(jnp.concatenate(blocks, axis=1))
            return jnp.concatenate(rows, axis=0)

        def put_term(s, c, term):
            for k in range(span):
                for h in range(parts):
                    block = term[
                        k * tile_rows : (k + 1) * tile_rows, h * width : (h + 1) * width
                    ]
                    if k == 0:
                        keep[place(span), h, s, c] = jnp.where(early, block, 0.0).astype(bf16)
                        block = jnp.where(early, 0.0, block)
                    target = keep if k % 2 == 0 else send
                    target[place(k), h, s, c] = block.astype(bf16)

        def put_rows(pair):
            rows_buf[0:size, :] = pair[0].astype(bf16)
            rows_buf[size : 2 * size, :] = pair[1].astype(bf16)

        def put_cols(pair):
            cols_buf[:, 0:size] = pair[0].astype(bf16)
            cols_buf[:, size : 2 * size] = pair[1].astype(bf16)

        def pair_of(ref):
            return ref[0].astype(f32), ref[1].astype(f32)

        def parts_of(ref, rows, cols):
            return ref[0, rows, cols], ref[1, rows, cols], ref[2, rows, cols]

        def put_row_halves(first, second):
            for number, wave_half in enumerate((first, second)):
                for c in range(2):
                    at = number * size + c * half
                    rows_buf[at : at + half, :] = wave_half[c].astype(bf16)

        def put_col_halves(first, second):
            for number, wave_half in enumerate((first, second)):
                for c in range(2):
                    at = number * size + c * half
                    cols_buf[:, at : at + half] = wave_half[c].astype(bf16)

        def both(first, second, axis):
            return [jnp.concatenate([a, b], axis=axis) for a, b in zip(first, second)]

        def plus(first, second):
            return [a + b for a, b in zip(first, second)]

        def less(first, second):
            return [a - b for a, b in zip(first, second)]

        everything = slice(None)
        near_parts = parts_of(near, everything, everything)
        pr, pi = pair_of(probe)
        ar, ai = patch(0, 0), patch(0, 1)
        put_rows((pr * ar - pi * ai, pr * ai + pi * ar))
        put_cols(left(near_parts, False, rows_buf[...]))
        two = right(near_parts, False, cols_buf[...])
        psi2[0] = two[0].astype(bf16)
        psi2[1] = two[1].astype(bf16)
        wr, wi = pair_of(psi2)
        br, bi = patch(1, 0), patch(1, 1)
        wave_exit = (wr * br - wi * bi, wr * bi + wi * br)
        top, bottom = [x[low] for x in wave_exit], [x[high] for x in wave_exit]
        put_row_halves(plus(top, bottom), less(top, bottom))
        half2 = both(
            left(parts_of(far_near, low, everything), False, rows_buf[0:size, :]),
            left(parts_of(far_near, high, everything), False, rows_buf[size : 2 * size, :]),
            0,
        )
        top, bottom = [x[:, low] for x in half2], [x[:, high] for x in half2]
        put_col_halves(plus(top, bottom), less(top, bottom))
        fields = [
            right(parts_of(far_cols, low, low), False, cols_buf[:, 0:size]),
            right(parts_of(far_cols, low, high), False, cols_buf[:, size : 2 * size]),
        ]
        chis = []
        for (fr, fi), cols in zip(fields, (low, high)):
            keeping = 1.0 - amps[:, cols].astype(f32) * lax.rsqrt(fr * fr + fi * fi + smooth)
            chis.append((fr * keeping, fi * keeping))
        put_col_halves(*chis)
        even = right(parts_of(far_rows, low, low), True, cols_buf[:, 0:size])
        odd = right(parts_of(far_rows, high, low), True, cols_buf[:, size : 2 * size])
        back1 = both(plus(even, odd), less(even, odd), 1)
        put_row_halves([x[low] for x in back1], [x[high] for x in back1])
        even = left(parts_of(far_far, everything, low), True, rows_buf[0:size, :])
        odd = left(parts_of(far_far, everything, high), True, rows_buf[size : 2 * size, :])
        er, ei = both(plus(even, odd), less(even, odd), 0)
        br, bi = patch(1, 0), patch(1, 1)
        put_cols((br * er + bi * ei, br * ei - bi * er))
        wr, wi = pair_of(psi2)
        put_term(1, 0, wr * er + wi * ei)
        put_term(1, 1, wr * ei - wi * er)
        near_parts = parts_of(near, everything, everything)
        put_rows(right(near_parts, True, cols_buf[...]))
        gr, gi = left(near_parts, True, rows_buf[...])
        pr, pi = pair_of(probe)
        put_term(0, 0, pr * gr + pi * gi)
        put_term(0, 1, pr * gi - pi * gr)
        send[(1 - core) * (span // 2)] = jnp.zeros(send.shape[1:], bf16)

    @pl.when(live == 0)
    def _():
        keep[...] = jnp.zeros(keep.shape, bf16)
        send[...] = jnp.zeros(send.shape, bf16)


def waves(mine, theirs, consts, turned, meta, size):
    parts, _, _, tile_rows, _ = mine.shape[1:]
    span = size // tile_rows
    inside = pl.BlockSpec(memory_space=pltpu.VMEM)
    return pl.pallas_call(
        functools.partial(wave_kernel, size, span, tile_rows),
        out_shape=[jax.ShapeDtypeStruct(mine.shape, bf16)] * 2,
        in_specs=[pl.BlockSpec(memory_space=pltpu.SMEM)] + [inside] * 9,
        out_specs=[inside] * 2,
        scratch_shapes=[
            pltpu.VMEM((2 * size, size), bf16),
            pltpu.VMEM((size, 2 * size), bf16),
            pltpu.VMEM((2, size, size), bf16),
        ],
        compiler_params=pltpu.CompilerParams(vmem_limit_bytes=40 * 1024 * 1024),
        cost_estimate=pl.CostEstimate(
            flops=64 * size**3, bytes_accessed=24 * size * size, transcendentals=size * size
        ),
        name="waves",
    )(meta, mine, theirs, *consts, *turned)


def shards(size, object_slab, probe_wave, amplitudes, row_offsets, position_counts):
    tile_rows = object_slab.shape[2]
    span = size // tile_rows
    count = lax.axis_size("tile")
    parts = lax.axis_size("scan")
    slots = amplitudes.shape[0]
    paired = parts == slots == 2
    slot = lax.axis_index("scan")
    ahead = span // 2
    homes = range(ahead, count - ahead)
    swap = [(0, 1), (1, 0)]

    def brought(value, steps):
        return lax.ppermute(value, "tile", [(home + steps, home) for home in homes])

    def returned(value, steps):
        return lax.ppermute(value, "tile", [(home, home + steps) for home in homes])

    def to_partner(value):
        return lax.ppermute(value, "tile", [(home, home ^ 1) for home in homes])

    def by_slot(first, second):
        return jnp.where(slot == 0, first, second)

    own = object_slab.astype(bf16)
    notes = jnp.concatenate([row_offsets, position_counts])
    if paired:
        beside = lax.ppermute(own, "scan", swap)
        whole = jnp.stack([by_slot(own, beside), by_slot(beside, own)])
        whole, notes = lax.optimization_barrier((whole, notes))
        probe_pieces = [probe_wave, lax.ppermute(probe_wave, "scan", swap)]
    else:
        whole = lax.all_gather(own, "scan")
        every = lax.all_gather(probe_wave, "scan")
        probe_pieces = [every[number] for number in range(parts)]
    notes = brought(notes, -ahead)
    live = (slot < notes[slots]).astype(jnp.int32)
    core = lax.rem(lax.axis_index("tile"), 2)
    meta = jnp.stack(
        [notes[jnp.minimum(slot, slots - 1)], live, slot.astype(jnp.int32), core.astype(jnp.int32)]
    )
    if paired:
        amp_pieces = [
            lax.ppermute(
                by_slot(amplitudes[which], amplitudes[1 - which]).astype(bf16),
                ("tile", "scan"),
                [
                    ((home - ahead) * 2 + x, home * 2 + (x + which) % 2)
                    for home in homes
                    for x in range(2)
                ],
            )
            for which in range(2)
        ]
    else:
        every = lax.all_gather(brought(amplitudes.astype(bf16), -ahead), "scan")
        amp_pieces = [every[:, jnp.minimum(slot, slots - 1)].reshape((size, size))]
    far_rows, far_cols, near = tables(size)
    amps = in_order(amp_pieces, slot.astype(jnp.int32)[None], size)
    turned = rolled(probe_pieces, far_rows, far_cols, meta, size)
    steps = range(-ahead, ahead + 1, 2)
    arrived = {step: brought(whole, step) for step in steps if 0 < abs(step) < ahead}
    later, amp_pieces = lax.optimization_barrier((whole, amp_pieces))
    arrived.update({step: brought(later, step) for step in (-ahead, ahead)})
    arrived[0], turned = lax.optimization_barrier((whole, turned))
    mine = jnp.stack([arrived[step] for step in steps])
    theirs = to_partner(mine)
    keep, send = waves(mine, theirs, (far_rows, far_cols, near), (*turned, amps), meta, size)
    merged = (keep.astype(f32) + to_partner(send).astype(f32)).astype(bf16)
    total = sum(
        (returned(merged[steps.index(step)], step) if step else merged[ahead // 2]).astype(f32)
        for step in (2, -ahead, ahead, -2, 0)
    )
    if paired:
        away = lax.ppermute(by_slot(total[1], total[0]).astype(bf16), "scan", swap)
        return by_slot(total[0], total[1]) + away.astype(f32)
    return lax.psum_scatter(total, "scan", scatter_dimension=0, tiled=False)


def solution(mesh):
    in_specs = (
        P(None, None, "tile", "scan"),
        P(None, None, "scan"),
        P("tile", "scan", None),
        P("tile"),
        P("tile"),
    )
    out_specs = P(None, None, "tile", "scan")

    def run(object_slab, *rest):
        return jax.shard_map(
            functools.partial(shards, object_slab.shape[3]),
            mesh=mesh, in_specs=in_specs, out_specs=out_specs, check_vma=False,
        )(object_slab, *rest)

    return run
```

```python
import functools
import math

import jax
import jax.numpy as jnp
import ml_dtypes
import numpy as np
from jax import lax
from jax.experimental import pallas as pl
from jax.experimental.pallas import tpu as pltpu
from jax.sharding import PartitionSpec as P

fresnel = 0.5
smooth = 1.0
bf16 = jnp.bfloat16
f32 = jnp.float32


def tables(size):
    index = np.arange(size)
    angles = 2.0 * np.pi / size * (index[:, None] * index[None, :] % size)
    base = np.exp(1j * angles)
    far = np.conj(base) / math.sqrt(size)
    centred = np.where(index < size // 2, index, index - size).astype(np.float64)
    kernel = np.exp(-1j * np.pi * fresnel / size * centred * centred)
    near = (base * kernel[None, :]) @ np.conj(base).T / size

    def parts(table):
        stacked = np.stack([table.real, table.imag, -table.imag])
        return jnp.asarray(stacked.astype(ml_dtypes.bfloat16))

    order = np.concatenate([index[0::2], index[1::2]])
    return parts(far[order]), parts(far[:, order]), parts(near)


def left(table, conjugate, wave):
    real, plus, minus = table if not conjugate else (table[0], table[2], table[1])
    top = jnp.concatenate([real, minus], axis=1)
    bottom = jnp.concatenate([plus, real], axis=1)
    return (
        jnp.dot(top, wave, preferred_element_type=f32),
        jnp.dot(bottom, wave, preferred_element_type=f32),
    )


def right(table, conjugate, wave):
    real, plus, minus = table if not conjugate else (table[0], table[2], table[1])
    real_side = jnp.concatenate([real, minus], axis=0)
    imag_side = jnp.concatenate([plus, real], axis=0)
    return (
        jnp.dot(wave, real_side, preferred_element_type=f32),
        jnp.dot(wave, imag_side, preferred_element_type=f32),
    )


def one_hot(size, hit):
    row = lax.broadcasted_iota(jnp.int32, (size, size), 0)
    col = lax.broadcasted_iota(jnp.int32, (size, size), 1)
    return jnp.where(hit(row, col), 1.0, 0.0).astype(bf16)


def order_kernel(size, slot, measured, ordered, amps):
    half = size // 2
    if len(measured.shape) == 2:
        amps[...] = measured[...]
    else:
        for number in range(2):
            at = pl.multiple_of(jnp.where(slot[0] == number, 0, half), half)
            for side in range(2):
                cols = pl.ds(side * half, half)
                amps[pl.ds(at, half), cols] = measured[number, side]

    def frequency(place, natural):
        return natural == jnp.where(place < half, 2 * place, 2 * (place - half) + 1)

    rows_first = jnp.dot(one_hot(size, frequency), amps[...], preferred_element_type=f32)
    ordered[...] = jnp.dot(
        rows_first.astype(bf16),
        one_hot(size, lambda row, col: frequency(col, row)),
        preferred_element_type=f32,
    ).astype(bf16)


def in_order(measured, slot, size):
    whole = pl.BlockSpec(memory_space=pltpu.VMEM)
    return pl.pallas_call(
        functools.partial(order_kernel, size),
        out_shape=jax.ShapeDtypeStruct((size, size), bf16),
        in_specs=[pl.BlockSpec(memory_space=pltpu.SMEM), whole],
        out_specs=whole,
        scratch_shapes=[pltpu.VMEM((size, size), bf16)],
        compiler_params=pltpu.CompilerParams(vmem_limit_bytes=16 * 1024 * 1024),
        cost_estimate=pl.CostEstimate(
            flops=4 * size**3, bytes_accessed=4 * size * size, transcendentals=0
        ),
        name="in_order",
    )(slot, measured)


def roll_kernel(size, meta, far_rows, far_cols, *refs):
    pieces, (probe_out, near_side, far_side) = refs[:-3], refs[-3:]
    offset, slot = meta[0], meta[2]
    half = size // 2

    def moved(to, source):
        gap = to - source - offset
        return (gap == 0) | (gap == -size)

    down = one_hot(size, moved)
    across = one_hot(size, lambda row, col: moved(col, row))
    for c in range(3):
        near_side[c] = jnp.dot(
            far_rows[c], across[:, :half], preferred_element_type=f32
        ).astype(bf16)
        far_side[c] = jnp.dot(down[:half], far_cols[c], preferred_element_type=f32).astype(bf16)
    for c in range(2):
        done = 0
        for piece in pieces:
            turned = jnp.dot(down, piece[c, 0:size, :], preferred_element_type=f32).astype(bf16)
            width = turned.shape[1]
            if len(pieces) == 2:
                at = pl.multiple_of(jnp.where(slot == done, 0, width), width)
                probe_out[c, :, pl.ds(at, width)] = turned
                done += 1
            else:
                probe_out[c, :, done : done + width] = turned
                done += width


def rolled(pieces, far_rows, far_cols, meta, size):
    whole = pl.BlockSpec(memory_space=pltpu.VMEM)
    return pl.pallas_call(
        functools.partial(roll_kernel, size),
        out_shape=[
            jax.ShapeDtypeStruct((2, size, size), bf16),
            jax.ShapeDtypeStruct((3, size, size // 2), bf16),
            jax.ShapeDtypeStruct((3, size // 2, size), bf16),
        ],
        in_specs=[pl.BlockSpec(memory_space=pltpu.SMEM)] + [whole] * (2 + len(pieces)),
        out_specs=[whole] * 3,
        compiler_params=pltpu.CompilerParams(vmem_limit_bytes=24 * 1024 * 1024),
        cost_estimate=pl.CostEstimate(
            flops=64 * size**3, bytes_accessed=24 * size * size, transcendentals=0
        ),
        name="rolled",
    )(meta, far_rows, far_cols, *pieces)


def tile_access(size, span, tile_rows, meta, mine, theirs):
    offset, core = meta[0], meta[3]
    parts, _, width = mine.shape[1:]
    early = lax.broadcasted_iota(jnp.int32, (tile_rows, width), 0) < offset

    def place(k):
        return k // 2 if k % 2 == 0 else k // 2 + core

    def piece(k, h, s, c):
        source = mine if k % 2 == 0 else theirs
        at = (2 * s + c) * tile_rows
        return source[place(k), h, at : at + tile_rows, :].astype(f32)

    def patch(s, c):
        rows = []
        for k in range(span):
            blocks = [piece(k, h, s, c) for h in range(parts)]
            if k == 0:
                blocks = [jnp.where(early, piece(span, h, s, c), blocks[h]) for h in range(parts)]
            rows.append(jnp.concatenate(blocks, axis=1))
        return jnp.concatenate(rows, axis=0)

    return early, place, patch


def put_rows(rows_buf, pair):
    size = rows_buf.shape[1]
    for c in range(2):
        rows_buf[c * size : (c + 1) * size, :] = pair[c].astype(bf16)


def put_cols(cols_buf, pair):
    size = cols_buf.shape[0]
    for c in range(2):
        cols_buf[:, c * size : (c + 1) * size] = pair[c].astype(bf16)


def put_row_halves(rows_buf, first, second):
    half = rows_buf.shape[1] // 2
    for number, wave in enumerate((*first, *second)):
        rows_buf[number * half : (number + 1) * half, :] = wave.astype(bf16)


def put_col_halves(cols_buf, first, second):
    half = cols_buf.shape[0] // 2
    for number, wave in enumerate((*first, *second)):
        cols_buf[:, number * half : (number + 1) * half] = wave.astype(bf16)


def pair_of(ref):
    return ref[0].astype(f32), ref[1].astype(f32)


def parts_of(ref, rows, cols):
    return ref[0, rows, cols], ref[1, rows, cols], ref[2, rows, cols]


def both(first, second, axis):
    return [jnp.concatenate([a, b], axis=axis) for a, b in zip(first, second)]


def plus(first, second):
    return [a + b for a, b in zip(first, second)]


def less(first, second):
    return [a - b for a, b in zip(first, second)]


def forth_kernel(
    size, span, tile_rows, meta, mine, theirs, far_cols, near, probe, far_near,
    psi2, field, rows_buf, cols_buf,
):
    half = size // 2
    low, high, everything = slice(0, half), slice(half, size), slice(None)

    @pl.when(meta[1] == 1)
    def _():
        _, _, patch = tile_access(size, span, tile_rows, meta, mine, theirs)
        near_parts = parts_of(near, everything, everything)
        pr, pi = pair_of(probe)
        ar, ai = patch(0, 0), patch(0, 1)
        put_rows(rows_buf, (pr * ar - pi * ai, pr * ai + pi * ar))
        put_cols(cols_buf, left(near_parts, False, rows_buf[...]))
        two = right(near_parts, False, cols_buf[...])
        psi2[0] = two[0].astype(bf16)
        psi2[1] = two[1].astype(bf16)
        wr, wi = pair_of(psi2)
        br, bi = patch(1, 0), patch(1, 1)
        wave_exit = (wr * br - wi * bi, wr * bi + wi * br)
        top, bottom = [x[low] for x in wave_exit], [x[high] for x in wave_exit]
        put_row_halves(rows_buf, plus(top, bottom), less(top, bottom))
        half2 = both(
            left(parts_of(far_near, low, everything), False, rows_buf[0:size, :]),
            left(parts_of(far_near, high, everything), False, rows_buf[size : 2 * size, :]),
            0,
        )
        top, bottom = [x[:, low] for x in half2], [x[:, high] for x in half2]
        put_col_halves(cols_buf, plus(top, bottom), less(top, bottom))
        for cols, source in ((low, cols_buf[:, 0:size]), (high, cols_buf[:, size : 2 * size])):
            fr, fi = right(parts_of(far_cols, low, cols), False, source)
            field[0, :, cols] = fr
            field[1, :, cols] = fi


def back_kernel(
    size, span, tile_rows, meta, mine, theirs, far_rows, near, probe, far_far, amps, psi2, field,
    keep, send, rows_buf, cols_buf,
):
    core = meta[3]
    parts, _, _, _, width = keep.shape[1:]
    half = size // 2
    low, high, everything = slice(0, half), slice(half, size), slice(None)

    @pl.when(meta[1] == 1)
    def _():
        early, place, patch = tile_access(size, span, tile_rows, meta, mine, theirs)

        def put_term(s, c, term):
            for k in range(span):
                for h in range(parts):
                    block = term[
                        k * tile_rows : (k + 1) * tile_rows, h * width : (h + 1) * width
                    ]
                    if k == 0:
                        keep[place(span), h, s, c] = jnp.where(early, block, 0.0).astype(bf16)
                        block = jnp.where(early, 0.0, block)
                    target = keep if k % 2 == 0 else send
                    target[place(k), h, s, c] = block.astype(bf16)

        chis = []
        for cols in (low, high):
            fr, fi = field[0, :, cols], field[1, :, cols]
            keeping = 1.0 - amps[:, cols].astype(f32) * lax.rsqrt(fr * fr + fi * fi + smooth)
            chis.append((fr * keeping, fi * keeping))
        put_col_halves(cols_buf, *chis)
        even = right(parts_of(far_rows, low, low), True, cols_buf[:, 0:size])
        odd = right(parts_of(far_rows, high, low), True, cols_buf[:, size : 2 * size])
        back1 = both(plus(even, odd), less(even, odd), 1)
        put_row_halves(rows_buf, [x[low] for x in back1], [x[high] for x in back1])
        even = left(parts_of(far_far, everything, low), True, rows_buf[0:size, :])
        odd = left(parts_of(far_far, everything, high), True, rows_buf[size : 2 * size, :])
        er, ei = both(plus(even, odd), less(even, odd), 0)
        br, bi = patch(1, 0), patch(1, 1)
        put_cols(cols_buf, (br * er + bi * ei, br * ei - bi * er))
        wr, wi = pair_of(psi2)
        put_term(1, 0, wr * er + wi * ei)
        put_term(1, 1, wr * ei - wi * er)
        near_parts = parts_of(near, everything, everything)
        put_rows(rows_buf, right(near_parts, True, cols_buf[...]))
        gr, gi = left(near_parts, True, rows_buf[...])
        pr, pi = pair_of(probe)
        put_term(0, 0, pr * gr + pi * gi)
        put_term(0, 1, pr * gi - pi * gr)
        send[(1 - core) * (span // 2)] = jnp.zeros(send.shape[1:], bf16)

    @pl.when(meta[1] == 0)
    def _():
        keep[...] = jnp.zeros(keep.shape, bf16)
        send[...] = jnp.zeros(send.shape, bf16)


def kernel_call(kernel, size, tile_rows, name, flops, out_shape, meta, *inputs):
    inside = pl.BlockSpec(memory_space=pltpu.VMEM)
    return pl.pallas_call(
        functools.partial(kernel, size, size // tile_rows, tile_rows),
        out_shape=out_shape,
        in_specs=[pl.BlockSpec(memory_space=pltpu.SMEM)] + [inside] * len(inputs),
        out_specs=[inside] * len(out_shape),
        scratch_shapes=[
            pltpu.VMEM((2 * size, size), bf16),
            pltpu.VMEM((size, 2 * size), bf16),
        ],
        compiler_params=pltpu.CompilerParams(vmem_limit_bytes=36 * 1024 * 1024),
        cost_estimate=pl.CostEstimate(
            flops=flops, bytes_accessed=size * size, transcendentals=0
        ),
        name=name,
    )(meta, *inputs)


def shards(size, object_slab, probe_wave, amplitudes, row_offsets, position_counts):
    tile_rows = object_slab.shape[2]
    span = size // tile_rows
    count = lax.axis_size("tile")
    parts = lax.axis_size("scan")
    slots = amplitudes.shape[0]
    paired = parts == slots == 2
    slot = lax.axis_index("scan")
    ahead = span // 2
    homes = range(ahead, count - ahead)
    swap = [(0, 1), (1, 0)]

    def brought(value, steps):
        return lax.ppermute(value, "tile", [(home + steps, home) for home in homes])

    def returned(value, steps):
        return lax.ppermute(value, "tile", [(home, home + steps) for home in homes])

    def to_partner(value):
        return lax.ppermute(value, "tile", [(one, one ^ 1) for one in range(count)])

    def by_slot(first, second):
        return jnp.where(slot == 0, first, second)

    own = object_slab.astype(bf16)
    width = own.shape[-1]
    notes = jnp.concatenate([row_offsets, position_counts]).astype(bf16)
    notes = jnp.pad(notes[None], ((0, 15), (0, width - slots - 1)))

    def below(tile):
        return jnp.concatenate([tile.reshape((-1, width)), notes])

    if paired:
        beside = lax.ppermute(own, "scan", swap)
        whole = jnp.stack([below(by_slot(own, beside)), below(by_slot(beside, own))])

        def in_halves(value):
            return jnp.stack(jnp.split(value.astype(bf16), 2, axis=1))

        other = in_halves(by_slot(amplitudes[1], amplitudes[0]))
        got = lax.ppermute(jnp.concatenate([probe_wave, other], axis=1), "scan", swap)
        probe_pieces = [probe_wave, got]
        mine_amps = in_halves(by_slot(amplitudes[0], amplitudes[1]))
        measured = brought(jnp.stack([mine_amps, got[:, size:]]), -ahead)
    else:
        gathered = lax.all_gather(own, "scan")
        whole = jnp.stack([below(gathered[number]) for number in range(parts)])
        every = lax.all_gather(probe_wave, "scan")
        probe_pieces = [every[number] for number in range(parts)]
        every = lax.all_gather(brought(amplitudes.astype(bf16), -ahead), "scan")
        measured = every[:, jnp.minimum(slot, slots - 1)].reshape((size, size))
    far_rows, far_cols, near = tables(size)
    steps = range(-ahead, ahead + 1, 2)
    arrived = {0: whole}
    for step in sorted(steps, key=abs)[1:]:
        arrived[step] = brought(whole, step)
    notes = arrived[-ahead][0, -16, : slots + 1].astype(jnp.int32)
    live = (slot < notes[slots]).astype(jnp.int32)
    core = lax.rem(lax.axis_index("tile"), 2)
    meta = jnp.stack(
        [notes[jnp.minimum(slot, slots - 1)], live, slot.astype(jnp.int32), core.astype(jnp.int32)]
    )
    turned, far_near, far_far = rolled(probe_pieces, far_rows, far_cols, meta, size)
    mine = jnp.stack([arrived[step] for step in steps])
    theirs = to_partner(mine)
    shape = jax.ShapeDtypeStruct
    psi2, field = kernel_call(
        forth_kernel, size, tile_rows, "forth", 24 * size**3,
        [shape((2, size, size), bf16), shape((2, size, size), f32)],
        meta, mine, theirs, far_cols, near, turned, far_near,
    )
    measured, field = lax.optimization_barrier((measured, field))
    amps = in_order(measured, slot.astype(jnp.int32)[None], size)
    keep, send = kernel_call(
        back_kernel, size, tile_rows, "back", 24 * size**3,
        [shape((len(steps), parts, 2, 2, tile_rows, width), bf16)] * 2,
        meta, mine, theirs, far_rows, near, turned, far_far, amps, psi2, field,
    )
    merged = (keep.astype(f32) + to_partner(send).astype(f32)).astype(bf16)
    total = sum(
        (returned(merged[steps.index(step)], step) if step else merged[ahead // 2]).astype(f32)
        for step in (2, -ahead, ahead, -2, 0)
    )
    if paired:
        away = lax.ppermute(by_slot(total[1], total[0]).astype(bf16), "scan", swap)
        return by_slot(total[0], total[1]) + away.astype(f32)
    return lax.psum_scatter(total, "scan", scatter_dimension=0, tiled=False)


def solution(mesh):
    in_specs = (
        P(None, None, "tile", "scan"),
        P(None, None, "scan"),
        P("tile", "scan", None),
        P("tile"),
        P("tile"),
    )
    out_specs = P(None, None, "tile", "scan")

    def run(object_slab, *rest):
        return jax.shard_map(
            functools.partial(shards, object_slab.shape[3]),
            mesh=mesh, in_specs=in_specs, out_specs=out_specs, check_vma=False,
        )(object_slab, *rest)

    return run
```

```python
import functools
import math

import jax
import jax.numpy as jnp
import ml_dtypes
import numpy as np
from jax import lax
from jax.experimental import pallas as pl
from jax.experimental.pallas import tpu as pltpu
from jax.sharding import PartitionSpec as P

fresnel = 0.5
smooth = 1.0
bf16 = jnp.bfloat16
f32 = jnp.float32


def tables(size):
    index = np.arange(size)
    angles = 2.0 * np.pi / size * (index[:, None] * index[None, :] % size)
    base = np.exp(1j * angles)
    far = np.conj(base) / math.sqrt(size)
    centred = np.where(index < size // 2, index, index - size).astype(np.float64)
    kernel = np.exp(-1j * np.pi * fresnel / size * centred * centred)
    near = (base * kernel[None, :]) @ np.conj(base).T / size

    def parts(table):
        stacked = np.stack([table.real, table.imag, -table.imag])
        return jnp.asarray(stacked.astype(ml_dtypes.bfloat16))

    order = np.concatenate([index[0::2], index[1::2]])
    return parts(far[order]), parts(far[:, order]), parts(near)


def left(table, conjugate, wave):
    real, plus, minus = table if not conjugate else (table[0], table[2], table[1])
    top = jnp.concatenate([real, minus], axis=1)
    bottom = jnp.concatenate([plus, real], axis=1)
    return (
        jnp.dot(top, wave, preferred_element_type=f32),
        jnp.dot(bottom, wave, preferred_element_type=f32),
    )


def right(table, conjugate, wave):
    real, plus, minus = table if not conjugate else (table[0], table[2], table[1])
    real_side = jnp.concatenate([real, minus], axis=0)
    imag_side = jnp.concatenate([plus, real], axis=0)
    return (
        jnp.dot(wave, real_side, preferred_element_type=f32),
        jnp.dot(wave, imag_side, preferred_element_type=f32),
    )


def one_hot(size, hit):
    row = lax.broadcasted_iota(jnp.int32, (size, size), 0)
    col = lax.broadcasted_iota(jnp.int32, (size, size), 1)
    return jnp.where(hit(row, col), 1.0, 0.0).astype(bf16)


def order_kernel(size, slot, *refs):
    measured, (ordered, amps) = refs[:-2], refs[-2:]
    half = size // 2
    for number, piece in enumerate(measured):
        rows = piece.shape[0]
        at = pl.multiple_of(jnp.where(slot[0] == number, 0, size - rows), rows)
        amps[pl.ds(at, rows), :] = piece[...]

    def frequency(place, natural):
        return natural == jnp.where(place < half, 2 * place, 2 * (place - half) + 1)

    rows_first = jnp.dot(one_hot(size, frequency), amps[...], preferred_element_type=f32)
    ordered[...] = jnp.dot(
        rows_first.astype(bf16),
        one_hot(size, lambda row, col: frequency(col, row)),
        preferred_element_type=f32,
    ).astype(bf16)


def in_order(measured, slot, size):
    whole = pl.BlockSpec(memory_space=pltpu.VMEM)
    return pl.pallas_call(
        functools.partial(order_kernel, size),
        out_shape=jax.ShapeDtypeStruct((size, size), bf16),
        in_specs=[pl.BlockSpec(memory_space=pltpu.SMEM)] + [whole] * len(measured),
        out_specs=whole,
        scratch_shapes=[pltpu.VMEM((size, size), bf16)],
        compiler_params=pltpu.CompilerParams(vmem_limit_bytes=16 * 1024 * 1024),
        cost_estimate=pl.CostEstimate(
            flops=4 * size**3, bytes_accessed=4 * size * size, transcendentals=0
        ),
        name="in_order",
    )(slot, *measured)


def roll_kernel(size, meta, far_rows, far_cols, *refs):
    pieces, (probe_out, near_side, far_side) = refs[:-3], refs[-3:]
    offset, slot = meta[0], meta[2]
    half = size // 2

    def moved(to, source):
        gap = to - source - offset
        return (gap == 0) | (gap == -size)

    down = one_hot(size, moved)
    across = one_hot(size, lambda row, col: moved(col, row))
    for c in range(3):
        near_side[c] = jnp.dot(
            far_rows[c], across[:, :half], preferred_element_type=f32
        ).astype(bf16)
        far_side[c] = jnp.dot(down[:half], far_cols[c], preferred_element_type=f32).astype(bf16)
    for c in range(2):
        done = 0
        for piece in pieces:
            turned = jnp.dot(down, piece[c], preferred_element_type=f32).astype(bf16)
            width = turned.shape[1]
            if len(pieces) == 2:
                at = pl.multiple_of(jnp.where(slot == done, 0, width), width)
                probe_out[c, :, pl.ds(at, width)] = turned
                done += 1
            else:
                probe_out[c, :, done : done + width] = turned
                done += width


def rolled(pieces, far_rows, far_cols, meta, size):
    whole = pl.BlockSpec(memory_space=pltpu.VMEM)
    return pl.pallas_call(
        functools.partial(roll_kernel, size),
        out_shape=[
            jax.ShapeDtypeStruct((2, size, size), bf16),
            jax.ShapeDtypeStruct((3, size, size // 2), bf16),
            jax.ShapeDtypeStruct((3, size // 2, size), bf16),
        ],
        in_specs=[pl.BlockSpec(memory_space=pltpu.SMEM)] + [whole] * (2 + len(pieces)),
        out_specs=[whole] * 3,
        compiler_params=pltpu.CompilerParams(vmem_limit_bytes=24 * 1024 * 1024),
        cost_estimate=pl.CostEstimate(
            flops=64 * size**3, bytes_accessed=24 * size * size, transcendentals=0
        ),
        name="rolled",
    )(meta, far_rows, far_cols, *pieces)


def tile_access(size, span, tile_rows, meta, mine, theirs):
    offset, core = meta[0], meta[3]
    parts, _, width = mine.shape[1:]
    early = lax.broadcasted_iota(jnp.int32, (tile_rows, width), 0) < offset

    def place(k):
        return k // 2 if k % 2 == 0 else k // 2 + core

    def piece(k, h, s, c):
        source = mine if k % 2 == 0 else theirs
        at = (2 * s + c) * tile_rows
        return source[place(k), h, at : at + tile_rows, :].astype(f32)

    def patch(s, c):
        rows = []
        for k in range(span):
            blocks = [piece(k, h, s, c) for h in range(parts)]
            if k == 0:
                blocks = [jnp.where(early, piece(span, h, s, c), blocks[h]) for h in range(parts)]
            rows.append(jnp.concatenate(blocks, axis=1))
        return jnp.concatenate(rows, axis=0)

    return early, place, patch


def put_rows(rows_buf, pair):
    size = rows_buf.shape[1]
    for c in range(2):
        rows_buf[c * size : (c + 1) * size, :] = pair[c].astype(bf16)


def put_cols(cols_buf, pair):
    size = cols_buf.shape[0]
    for c in range(2):
        cols_buf[:, c * size : (c + 1) * size] = pair[c].astype(bf16)


def put_row_halves(rows_buf, first, second):
    half = rows_buf.shape[1] // 2
    for number, wave in enumerate((*first, *second)):
        rows_buf[number * half : (number + 1) * half, :] = wave.astype(bf16)


def put_col_halves(cols_buf, first, second):
    half = cols_buf.shape[0] // 2
    for number, wave in enumerate((*first, *second)):
        cols_buf[:, number * half : (number + 1) * half] = wave.astype(bf16)


def pair_of(ref):
    return ref[0].astype(f32), ref[1].astype(f32)


def parts_of(ref, rows, cols):
    return ref[0, rows, cols], ref[1, rows, cols], ref[2, rows, cols]


def both(first, second, axis):
    return [jnp.concatenate([a, b], axis=axis) for a, b in zip(first, second)]


def plus(first, second):
    return [a + b for a, b in zip(first, second)]


def less(first, second):
    return [a - b for a, b in zip(first, second)]


def forth_kernel(
    size, span, tile_rows, meta, mine, theirs, far_cols, near, probe, far_near,
    psi2, field, rows_buf, cols_buf,
):
    half = size // 2
    low, high, everything = slice(0, half), slice(half, size), slice(None)

    @pl.when(meta[1] == 1)
    def _():
        _, _, patch = tile_access(size, span, tile_rows, meta, mine, theirs)
        near_parts = parts_of(near, everything, everything)
        pr, pi = pair_of(probe)
        ar, ai = patch(0, 0), patch(0, 1)
        put_rows(rows_buf, (pr * ar - pi * ai, pr * ai + pi * ar))
        put_cols(cols_buf, left(near_parts, False, rows_buf[...]))
        two = right(near_parts, False, cols_buf[...])
        psi2[0] = two[0].astype(bf16)
        psi2[1] = two[1].astype(bf16)
        wr, wi = pair_of(psi2)
        br, bi = patch(1, 0), patch(1, 1)
        wave_exit = (wr * br - wi * bi, wr * bi + wi * br)
        top, bottom = [x[low] for x in wave_exit], [x[high] for x in wave_exit]
        put_row_halves(rows_buf, plus(top, bottom), less(top, bottom))
        half2 = both(
            left(parts_of(far_near, low, everything), False, rows_buf[0:size, :]),
            left(parts_of(far_near, high, everything), False, rows_buf[size : 2 * size, :]),
            0,
        )
        top, bottom = [x[:, low] for x in half2], [x[:, high] for x in half2]
        put_col_halves(cols_buf, plus(top, bottom), less(top, bottom))
        for cols, source in ((low, cols_buf[:, 0:size]), (high, cols_buf[:, size : 2 * size])):
            fr, fi = right(parts_of(far_cols, low, cols), False, source)
            field[0, :, cols] = fr
            field[1, :, cols] = fi


def back_kernel(
    size, span, tile_rows, meta, mine, theirs, far_rows, near, probe, far_far, amps, psi2, field,
    keep, send, rows_buf, cols_buf,
):
    core = meta[3]
    parts, _, _, _, width = keep.shape[1:]
    half = size // 2
    low, high, everything = slice(0, half), slice(half, size), slice(None)

    @pl.when(meta[1] == 1)
    def _():
        early, place, patch = tile_access(size, span, tile_rows, meta, mine, theirs)

        def put_term(s, c, term):
            for k in range(span):
                for h in range(parts):
                    block = term[
                        k * tile_rows : (k + 1) * tile_rows, h * width : (h + 1) * width
                    ]
                    if k == 0:
                        keep[place(span), h, s, c] = jnp.where(early, block, 0.0).astype(bf16)
                        block = jnp.where(early, 0.0, block)
                    target = keep if k % 2 == 0 else send
                    target[place(k), h, s, c] = block.astype(bf16)

        chis = []
        for cols in (low, high):
            fr, fi = field[0, :, cols], field[1, :, cols]
            keeping = 1.0 - amps[:, cols].astype(f32) * lax.rsqrt(fr * fr + fi * fi + smooth)
            chis.append((fr * keeping, fi * keeping))
        put_col_halves(cols_buf, *chis)
        even = right(parts_of(far_rows, low, low), True, cols_buf[:, 0:size])
        odd = right(parts_of(far_rows, high, low), True, cols_buf[:, size : 2 * size])
        back1 = both(plus(even, odd), less(even, odd), 1)
        put_row_halves(rows_buf, [x[low] for x in back1], [x[high] for x in back1])
        even = left(parts_of(far_far, everything, low), True, rows_buf[0:size, :])
        odd = left(parts_of(far_far, everything, high), True, rows_buf[size : 2 * size, :])
        er, ei = both(plus(even, odd), less(even, odd), 0)
        br, bi = patch(1, 0), patch(1, 1)
        put_cols(cols_buf, (br * er + bi * ei, br * ei - bi * er))
        wr, wi = pair_of(psi2)
        put_term(1, 0, wr * er + wi * ei)
        put_term(1, 1, wr * ei - wi * er)
        near_parts = parts_of(near, everything, everything)
        put_rows(rows_buf, right(near_parts, True, cols_buf[...]))
        gr, gi = left(near_parts, True, rows_buf[...])
        pr, pi = pair_of(probe)
        put_term(0, 0, pr * gr + pi * gi)
        put_term(0, 1, pr * gi - pi * gr)
        send[(1 - core) * (span // 2)] = jnp.zeros(send.shape[1:], bf16)

    @pl.when(meta[1] == 0)
    def _():
        keep[...] = jnp.zeros(keep.shape, bf16)
        send[...] = jnp.zeros(send.shape, bf16)


def kernel_call(kernel, size, tile_rows, name, flops, out_shape, meta, *inputs):
    inside = pl.BlockSpec(memory_space=pltpu.VMEM)
    return pl.pallas_call(
        functools.partial(kernel, size, size // tile_rows, tile_rows),
        out_shape=out_shape,
        in_specs=[pl.BlockSpec(memory_space=pltpu.SMEM)] + [inside] * len(inputs),
        out_specs=[inside] * len(out_shape),
        scratch_shapes=[
            pltpu.VMEM((2 * size, size), bf16),
            pltpu.VMEM((size, 2 * size), bf16),
        ],
        compiler_params=pltpu.CompilerParams(vmem_limit_bytes=36 * 1024 * 1024),
        cost_estimate=pl.CostEstimate(
            flops=flops, bytes_accessed=size * size, transcendentals=0
        ),
        name=name,
    )(meta, *inputs)


def shards(size, object_slab, probe_wave, amplitudes, row_offsets, position_counts):
    tile_rows = object_slab.shape[2]
    span = size // tile_rows
    count = lax.axis_size("tile")
    parts = lax.axis_size("scan")
    slots = amplitudes.shape[0]
    paired = parts == slots == 2
    slot = lax.axis_index("scan")
    ahead = span // 2
    homes = range(ahead, count - ahead)
    swap = [(0, 1), (1, 0)]

    def brought(value, steps):
        return lax.ppermute(value, "tile", [(home + steps, home) for home in homes])

    def paired_with(value, unit):
        return lax.ppermute(value, "tile", [(one, one ^ unit) for one in range(count)])

    def paired_across(value, unit):
        pairs = []
        for one in range(unit, count - unit):
            step = unit if (one // unit) % 2 else -unit
            pairs.append((one, one + step))
        return lax.ppermute(value, "tile", pairs)

    def by_slot(first, second):
        return jnp.where(slot == 0, first, second)

    tile = lax.axis_index("tile")

    def by_place(unit, if_odd, if_even):
        return jnp.where((tile // unit) % 2 == 1, if_odd, if_even)

    own = object_slab.astype(bf16)
    width = own.shape[-1]
    notes = jnp.concatenate([row_offsets, position_counts]).astype(bf16)
    notes = jnp.pad(notes[None], ((0, 15), (0, width - slots - 1)))

    def below(tile):
        return jnp.concatenate([tile.reshape((-1, width)), notes])

    if paired:
        beside = lax.ppermute(own, "scan", swap)
        whole = jnp.stack([below(by_slot(own, beside)), below(by_slot(beside, own))])

        probe_pieces = [probe_wave, lax.ppermute(probe_wave, "scan", swap)]
        straight = brought(by_slot(amplitudes[0], amplitudes[1]).astype(bf16), -ahead)
        crossed = lax.ppermute(
            by_slot(amplitudes[1], amplitudes[0]).astype(bf16),
            ("tile", "scan"),
            [((home - ahead) * 2 + x, home * 2 + 1 - x) for home in homes for x in range(2)],
        )
        measured = [straight, crossed]
    else:
        gathered = lax.all_gather(own, "scan")
        whole = jnp.stack([below(gathered[number]) for number in range(parts)])
        every = lax.all_gather(probe_wave, "scan")
        probe_pieces = [every[number] for number in range(parts)]
        every = lax.all_gather(brought(amplitudes.astype(bf16), -ahead), "scan")
        measured = [every[:, jnp.minimum(slot, slots - 1)].reshape((size, size))]
    far_rows, far_cols, near = tables(size)
    next_across, next_with = paired_across(whole, 4), paired_with(whole, 4)
    near_across, near_with = paired_across(whole, 2), paired_with(whole, 2)
    measured[0], next_across, next_with, near_across, near_with, probe_pieces = (
        lax.optimization_barrier(
            (measured[0], next_across, next_with, near_across, near_with, probe_pieces)
        )
    )
    arrived = [
        by_place(4, next_with, next_across),
        by_place(2, near_with, near_across),
        whole,
        by_place(2, near_across, near_with),
        by_place(4, next_across, next_with),
    ]
    notes = arrived[0][0, -16, : slots + 1].astype(jnp.int32)
    live = (slot < notes[slots]).astype(jnp.int32)
    core = lax.rem(tile, 2)
    meta = jnp.stack(
        [notes[jnp.minimum(slot, slots - 1)], live, slot.astype(jnp.int32), core.astype(jnp.int32)]
    )
    turned, far_near, far_far = rolled(probe_pieces, far_rows, far_cols, meta, size)
    mine = jnp.stack(arrived)
    theirs = paired_with(mine, 1)
    shape = jax.ShapeDtypeStruct
    psi2, field = kernel_call(
        forth_kernel, size, tile_rows, "forth", 24 * size**3,
        [shape((2, size, size), bf16), shape((2, size, size), f32)],
        meta, mine, theirs, far_cols, near, turned, far_near,
    )
    measured[-1], field = lax.optimization_barrier((measured[-1], field))
    amps = in_order(measured, slot.astype(jnp.int32)[None], size)
    keep, send = kernel_call(
        back_kernel, size, tile_rows, "back", 24 * size**3,
        [shape((len(arrived), parts, 2, 2, tile_rows, width), bf16)] * 2,
        meta, mine, theirs, far_rows, near, turned, far_far, amps, psi2, field,
    )
    merged = (keep.astype(f32) + paired_with(send, 1).astype(f32)).astype(bf16)
    total = sum(
        value.astype(f32)
        for value in (
            paired_with(by_place(2, merged[1], merged[3]), 2),
            paired_across(by_place(4, merged[4], merged[0]), 4),
            paired_across(by_place(2, merged[3], merged[1]), 2),
            paired_with(by_place(4, merged[0], merged[4]), 4),
            merged[2],
        )
    )
    if paired:
        away = lax.ppermute(by_slot(total[1], total[0]).astype(bf16), "scan", swap)
        return by_slot(total[0], total[1]) + away.astype(f32)
    return lax.psum_scatter(total, "scan", scatter_dimension=0, tiled=False)


def solution(mesh):
    in_specs = (
        P(None, None, "tile", "scan"),
        P(None, None, "scan"),
        P("tile", "scan", None),
        P("tile"),
        P("tile"),
    )
    out_specs = P(None, None, "tile", "scan")

    def run(object_slab, *rest):
        return jax.shard_map(
            functools.partial(shards, object_slab.shape[3]),
            mesh=mesh, in_specs=in_specs, out_specs=out_specs, check_vma=False,
        )(object_slab, *rest)

    return run
```

```python
import functools
import math

import jax
import jax.numpy as jnp
import ml_dtypes
import numpy as np
from jax import lax
from jax.experimental import pallas as pl
from jax.experimental.pallas import tpu as pltpu
from jax.sharding import PartitionSpec as P

fresnel = 0.5
smooth = 1.0
bf16 = jnp.bfloat16
f32 = jnp.float32


def tables(size):
    index = np.arange(size)
    angles = 2.0 * np.pi / size * (index[:, None] * index[None, :] % size)
    base = np.exp(1j * angles)
    far = np.conj(base) / math.sqrt(size)
    centred = np.where(index < size // 2, index, index - size).astype(np.float64)
    kernel = np.exp(-1j * np.pi * fresnel / size * centred * centred)
    near = (base * kernel[None, :]) @ np.conj(base).T / size

    def parts(table):
        stacked = np.stack([table.real, table.imag])
        return jnp.asarray(stacked.astype(ml_dtypes.bfloat16))

    order = np.concatenate([index[0::2], index[1::2]])
    return parts(far[order]), parts(far[:, order]), parts(near)


def three(table, conjugate):
    real, imag = table
    return (real, -imag, imag) if conjugate else (real, imag, -imag)


def left(table, conjugate, wave):
    real, plus, minus = three(table, conjugate)
    top = jnp.concatenate([real, minus], axis=1)
    bottom = jnp.concatenate([plus, real], axis=1)
    return (
        jnp.dot(top, wave, preferred_element_type=f32),
        jnp.dot(bottom, wave, preferred_element_type=f32),
    )


def right(table, conjugate, wave):
    real, plus, minus = three(table, conjugate)
    real_side = jnp.concatenate([real, minus], axis=0)
    imag_side = jnp.concatenate([plus, real], axis=0)
    return (
        jnp.dot(wave, real_side, preferred_element_type=f32),
        jnp.dot(wave, imag_side, preferred_element_type=f32),
    )


def one_hot(size, hit):
    row = lax.broadcasted_iota(jnp.int32, (size, size), 0)
    col = lax.broadcasted_iota(jnp.int32, (size, size), 1)
    return jnp.where(hit(row, col), 1.0, 0.0).astype(bf16)


def in_order(size, slot, measured, amps):
    half = size // 2
    for number, piece in enumerate(measured):
        rows = size // len(measured)
        at = pl.multiple_of(jnp.where(slot == number, 0, size - rows), rows)
        amps[pl.ds(at, rows), :] = piece[0:rows, :]

    def frequency(place, natural):
        return natural == jnp.where(place < half, 2 * place, 2 * (place - half) + 1)

    rows_first = jnp.dot(one_hot(size, frequency), amps[...], preferred_element_type=f32)
    return jnp.dot(
        rows_first.astype(bf16),
        one_hot(size, lambda row, col: frequency(col, row)),
        preferred_element_type=f32,
    )


def roll_kernel(size, meta, far_rows, far_cols, *refs):
    pieces, (probe_out, near_side, far_side) = refs[:-3], refs[-3:]
    offset, slot = meta[0], meta[2]
    half = size // 2

    def moved(to, source):
        gap = to - source - offset
        return (gap == 0) | (gap == -size)

    down = one_hot(size, moved)
    across = one_hot(size, lambda row, col: moved(col, row))
    for c in range(2):
        near_side[c] = jnp.dot(
            far_rows[c], across[:, :half], preferred_element_type=f32
        ).astype(bf16)
        far_side[c] = jnp.dot(down[:half], far_cols[c], preferred_element_type=f32).astype(bf16)
    for c in range(2):
        done = 0
        for piece in pieces:
            turned = jnp.dot(down, piece[c], preferred_element_type=f32).astype(bf16)
            width = turned.shape[1]
            if len(pieces) == 2:
                at = pl.multiple_of(jnp.where(slot == done, 0, width), width)
                probe_out[c, :, pl.ds(at, width)] = turned
                done += 1
            else:
                probe_out[c, :, done : done + width] = turned
                done += width


def rolled(pieces, far_rows, far_cols, meta, size):
    whole = pl.BlockSpec(memory_space=pltpu.VMEM)
    return pl.pallas_call(
        functools.partial(roll_kernel, size),
        out_shape=[
            jax.ShapeDtypeStruct((2, size, size), bf16),
            jax.ShapeDtypeStruct((2, size, size // 2), bf16),
            jax.ShapeDtypeStruct((2, size // 2, size), bf16),
        ],
        in_specs=[pl.BlockSpec(memory_space=pltpu.SMEM)] + [whole] * (2 + len(pieces)),
        out_specs=[whole] * 3,
        compiler_params=pltpu.CompilerParams(vmem_limit_bytes=16 * 1024 * 1024),
        cost_estimate=pl.CostEstimate(
            flops=64 * size**3, bytes_accessed=24 * size * size, transcendentals=0
        ),
        name="rolled",
    )(meta, far_rows, far_cols, *pieces)


def tile_access(size, span, tile_rows, meta, mine, theirs):
    offset, core = meta[0], meta[3]
    parts, _, _, _, width = mine.shape[1:]
    early = lax.broadcasted_iota(jnp.int32, (tile_rows, width), 0) < offset

    def place(k):
        return k // 2 if k % 2 == 0 else k // 2 + core

    def piece(k, h, s, c):
        source = mine if k % 2 == 0 else theirs
        return source[place(k), h, s, c].astype(f32)

    def patch(s, c):
        rows = []
        for k in range(span):
            blocks = [piece(k, h, s, c) for h in range(parts)]
            if k == 0:
                blocks = [jnp.where(early, piece(span, h, s, c), blocks[h]) for h in range(parts)]
            rows.append(jnp.concatenate(blocks, axis=1))
        return jnp.concatenate(rows, axis=0)

    return early, place, patch


def put_rows(rows_buf, pair):
    size = rows_buf.shape[1]
    for c in range(2):
        rows_buf[c * size : (c + 1) * size, :] = pair[c].astype(bf16)


def put_cols(cols_buf, pair):
    size = cols_buf.shape[0]
    for c in range(2):
        cols_buf[:, c * size : (c + 1) * size] = pair[c].astype(bf16)


def put_row_halves(rows_buf, first, second):
    half = rows_buf.shape[1] // 2
    for number, wave in enumerate((*first, *second)):
        rows_buf[number * half : (number + 1) * half, :] = wave.astype(bf16)


def put_col_halves(cols_buf, first, second):
    half = cols_buf.shape[0] // 2
    for number, wave in enumerate((*first, *second)):
        cols_buf[:, number * half : (number + 1) * half] = wave.astype(bf16)


def pair_of(ref):
    return ref[0].astype(f32), ref[1].astype(f32)


def parts_of(ref, rows, cols):
    return ref[0, rows, cols], ref[1, rows, cols]


def both(first, second, axis):
    return [jnp.concatenate([a, b], axis=axis) for a, b in zip(first, second)]


def plus(first, second):
    return [a + b for a, b in zip(first, second)]


def less(first, second):
    return [a - b for a, b in zip(first, second)]


def forth_kernel(
    size, span, tile_rows, meta, mine, theirs, far_cols, near, probe, far_near,
    psi2, field, rows_buf, cols_buf,
):
    half = size // 2
    low, high, everything = slice(0, half), slice(half, size), slice(None)

    @pl.when(meta[1] == 1)
    def _():
        _, _, patch = tile_access(size, span, tile_rows, meta, mine, theirs)
        near_parts = parts_of(near, everything, everything)
        pr, pi = pair_of(probe)
        ar, ai = patch(0, 0), patch(0, 1)
        put_rows(rows_buf, (pr * ar - pi * ai, pr * ai + pi * ar))
        put_cols(cols_buf, left(near_parts, False, rows_buf[...]))
        two = right(near_parts, False, cols_buf[...])
        psi2[0] = two[0].astype(bf16)
        psi2[1] = two[1].astype(bf16)
        wr, wi = pair_of(psi2)
        br, bi = patch(1, 0), patch(1, 1)
        wave_exit = (wr * br - wi * bi, wr * bi + wi * br)
        top, bottom = [x[low] for x in wave_exit], [x[high] for x in wave_exit]
        put_row_halves(rows_buf, plus(top, bottom), less(top, bottom))
        half2 = both(
            left(parts_of(far_near, low, everything), False, rows_buf[0:size, :]),
            left(parts_of(far_near, high, everything), False, rows_buf[size : 2 * size, :]),
            0,
        )
        top, bottom = [x[:, low] for x in half2], [x[:, high] for x in half2]
        put_col_halves(cols_buf, plus(top, bottom), less(top, bottom))
        for cols, source in ((low, cols_buf[:, 0:size]), (high, cols_buf[:, size : 2 * size])):
            fr, fi = right(parts_of(far_cols, low, cols), False, source)
            field[0, :, cols] = fr
            field[1, :, cols] = fi


def back_kernel(
    size, span, tile_rows, meta, mine, theirs, far_rows, near, probe, far_far, psi2, field, *refs,
):
    measured, (keep, send, rows_buf, cols_buf) = refs[:-4], refs[-4:]
    core = meta[3]
    parts, _, _, _, width = keep.shape[1:]
    half = size // 2
    low, high, everything = slice(0, half), slice(half, size), slice(None)

    @pl.when(meta[1] == 1)
    def _():
        early, place, patch = tile_access(size, span, tile_rows, meta, mine, theirs)

        def put_term(s, c, term):
            for k in range(span):
                for h in range(parts):
                    block = term[
                        k * tile_rows : (k + 1) * tile_rows, h * width : (h + 1) * width
                    ]
                    if k == 0:
                        keep[place(span), h, s, c] = jnp.where(early, block, 0.0).astype(bf16)
                        block = jnp.where(early, 0.0, block)
                    target = keep if k % 2 == 0 else send
                    target[place(k), h, s, c] = block.astype(bf16)

        amps = in_order(size, meta[2], measured, cols_buf.at[:, 0:size])
        chis = []
        for cols in (low, high):
            fr, fi = field[0, :, cols], field[1, :, cols]
            keeping = 1.0 - amps[:, cols] * lax.rsqrt(fr * fr + fi * fi + smooth)
            chis.append((fr * keeping, fi * keeping))
        put_col_halves(cols_buf, *chis)
        even = right(parts_of(far_rows, low, low), True, cols_buf[:, 0:size])
        odd = right(parts_of(far_rows, high, low), True, cols_buf[:, size : 2 * size])
        back1 = both(plus(even, odd), less(even, odd), 1)
        put_row_halves(rows_buf, [x[low] for x in back1], [x[high] for x in back1])
        even = left(parts_of(far_far, everything, low), True, rows_buf[0:size, :])
        odd = left(parts_of(far_far, everything, high), True, rows_buf[size : 2 * size, :])
        er, ei = both(plus(even, odd), less(even, odd), 0)
        br, bi = patch(1, 0), patch(1, 1)
        put_cols(cols_buf, (br * er + bi * ei, br * ei - bi * er))
        wr, wi = pair_of(psi2)
        put_term(1, 0, wr * er + wi * ei)
        put_term(1, 1, wr * ei - wi * er)
        near_parts = parts_of(near, everything, everything)
        put_rows(rows_buf, right(near_parts, True, cols_buf[...]))
        gr, gi = left(near_parts, True, rows_buf[...])
        pr, pi = pair_of(probe)
        put_term(0, 0, pr * gr + pi * gi)
        put_term(0, 1, pr * gi - pi * gr)
        send[(1 - core) * (span // 2)] = jnp.zeros(send.shape[1:], bf16)

    @pl.when(meta[1] == 0)
    def _():
        keep[...] = jnp.zeros(keep.shape, bf16)
        send[...] = jnp.zeros(send.shape, bf16)


def kernel_call(kernel, size, tile_rows, name, flops, out_shape, meta, *inputs):
    inside = pl.BlockSpec(memory_space=pltpu.VMEM)
    return pl.pallas_call(
        functools.partial(kernel, size, size // tile_rows, tile_rows),
        out_shape=out_shape,
        in_specs=[pl.BlockSpec(memory_space=pltpu.SMEM)] + [inside] * len(inputs),
        out_specs=[inside] * len(out_shape),
        scratch_shapes=[
            pltpu.VMEM((2 * size, size), bf16),
            pltpu.VMEM((size, 2 * size), bf16),
        ],
        compiler_params=pltpu.CompilerParams(vmem_limit_bytes=28 * 1024 * 1024),
        cost_estimate=pl.CostEstimate(
            flops=flops, bytes_accessed=size * size, transcendentals=0
        ),
        name=name,
    )(meta, *inputs)


def shards(size, object_slab, probe_wave, amplitudes, row_offsets, position_counts):
    tile_rows = object_slab.shape[2]
    span = size // tile_rows
    count = lax.axis_size("tile")
    parts = lax.axis_size("scan")
    slots = amplitudes.shape[0]
    paired = parts == slots == 2
    slot = lax.axis_index("scan")
    ahead = span // 2
    swap = [(0, 1), (1, 0)]
    ahead_pairs = [(one, (one + ahead) % count) for one in range(count)]

    def brought(value):
        return lax.ppermute(value, "tile", ahead_pairs)

    def paired_with(value, unit):
        return lax.ppermute(value, "tile", [(one, one ^ unit) for one in range(count)])

    def paired_across(value, unit):
        pairs = []
        for one in range(count):
            step = unit if (one // unit) % 2 else -unit
            pairs.append((one, one + step if unit <= one < count - unit else one))
        return lax.ppermute(value, "tile", pairs)

    def by_slot(first, second):
        return jnp.where(slot == 0, first, second)

    tile = lax.axis_index("tile")

    def by_place(unit, if_odd, if_even):
        return jnp.where((tile // unit) % 2 == 1, if_odd, if_even)

    own = object_slab.astype(bf16)
    width = own.shape[-1]
    notes = jnp.concatenate([row_offsets, position_counts]).astype(bf16)
    notes = jnp.pad(notes[None], ((0, 15), (0, size - slots - 1)))
    if paired:
        beside = lax.ppermute(own, "scan", swap)
        whole = jnp.stack([by_slot(own, beside), by_slot(beside, own)])

        probe_pieces = [probe_wave, lax.ppermute(probe_wave, "scan", swap)]
        straight, crossed = (by_slot(amplitudes[a], amplitudes[1 - a]).astype(bf16) for a in (0, 1))
        straight = brought(jnp.concatenate([straight, notes]))
        crossed = lax.ppermute(
            crossed,
            ("tile", "scan"),
            [(2 * a + x, 2 * b + 1 - x) for a, b in ahead_pairs for x in range(2)],
        )
        notes = straight[-16]
        measured = [straight, crossed]
    else:
        whole = lax.all_gather(own, "scan")
        every = lax.all_gather(probe_wave, "scan")
        probe_pieces = [every[number] for number in range(parts)]
        notes = brought(notes)[0]
        every = lax.all_gather(brought(amplitudes.astype(bf16)), "scan")
        measured = [every[:, jnp.minimum(slot, slots - 1)].reshape((size, size))]
    far_rows, far_cols, near = tables(size)
    core = lax.rem(tile, 2)
    notes = notes[: slots + 1].astype(jnp.int32)
    home = (tile >= ahead) & (tile < count - ahead)
    live = (home & (slot < notes[slots])).astype(jnp.int32)
    meta = jnp.stack(
        [notes[jnp.minimum(slot, slots - 1)], live, slot.astype(jnp.int32), core.astype(jnp.int32)]
    )
    turned, far_near, far_far = rolled(probe_pieces, far_rows, far_cols, meta, size)
    next_across, next_with = paired_across(whole, 4), paired_with(whole, 4)
    near_across, near_with = paired_across(whole, 2), paired_with(whole, 2)
    middle, turned = lax.optimization_barrier((whole, turned))
    arrived = [
        by_place(4, next_with, next_across),
        by_place(2, near_with, near_across),
        middle,
        by_place(2, near_across, near_with),
        by_place(4, next_across, next_with),
    ]
    mine = jnp.stack(arrived)
    theirs = paired_with(mine, 1)
    shape = jax.ShapeDtypeStruct
    psi2, field = kernel_call(
        forth_kernel, size, tile_rows, "forth", 24 * size**3,
        [shape((2, size, size), bf16), shape((2, size, size), f32)],
        meta, mine, theirs, far_cols, near, turned, far_near,
    )
    measured[-1], field = lax.optimization_barrier((measured[-1], field))
    keep, send = kernel_call(
        back_kernel, size, tile_rows, "back", 24 * size**3,
        [shape((len(arrived), parts, 2, 2, tile_rows, width), bf16)] * 2,
        meta, mine, theirs, far_rows, near, turned, far_far, psi2, field, *measured,
    )
    merged = (keep.astype(f32) + paired_with(send, 1).astype(f32)).astype(bf16)
    total = sum(
        value.astype(f32)
        for value in (
            paired_with(by_place(4, merged[0], merged[4]), 4),
            paired_across(by_place(4, merged[4], merged[0]), 4),
            paired_with(by_place(2, merged[1], merged[3]), 2),
            paired_across(by_place(2, merged[3], merged[1]), 2),
            merged[2],
        )
    )
    if paired:
        away = lax.ppermute(by_slot(total[1], total[0]).astype(bf16), "scan", swap)
        return by_slot(total[0], total[1]) + away.astype(f32)
    return lax.psum_scatter(total, "scan", scatter_dimension=0, tiled=False)


def solution(mesh):
    in_specs = (
        P(None, None, "tile", "scan"),
        P(None, None, "scan"),
        P("tile", "scan", None),
        P("tile"),
        P("tile"),
    )
    out_specs = P(None, None, "tile", "scan")

    def run(object_slab, *rest):
        return jax.shard_map(
            functools.partial(shards, object_slab.shape[3]),
            mesh=mesh, in_specs=in_specs, out_specs=out_specs, check_vma=False,
        )(object_slab, *rest)

    return run
```

```python
import functools
import math

import jax
import jax.numpy as jnp
import ml_dtypes
import numpy as np
from jax import lax
from jax.experimental import pallas as pl
from jax.experimental.pallas import tpu as pltpu
from jax.sharding import PartitionSpec as P

fresnel = 0.5
smooth = 1.0
bf16 = jnp.bfloat16
f32 = jnp.float32


def tables(size):
    index = np.arange(size)
    angles = 2.0 * np.pi / size * (index[:, None] * index[None, :] % size)
    base = np.exp(1j * angles)
    far = np.conj(base) / math.sqrt(size)
    centred = np.where(index < size // 2, index, index - size).astype(np.float64)
    kernel = np.exp(-1j * np.pi * fresnel / size * centred * centred)
    near = (base * kernel[None, :]) @ np.conj(base).T / size

    def parts(table):
        stacked = np.stack([table.real, table.imag])
        return jnp.asarray(stacked.astype(ml_dtypes.bfloat16))

    order = np.concatenate([index[0::2], index[1::2]])
    return parts(far[order]), parts(far[:, order]), parts(near)


def three(table, conjugate):
    real, imag = table
    return (real, -imag, imag) if conjugate else (real, imag, -imag)


def left(table, conjugate, wave):
    real, plus, minus = three(table, conjugate)
    top = jnp.concatenate([real, minus], axis=1)
    bottom = jnp.concatenate([plus, real], axis=1)
    return (
        jnp.dot(top, wave, preferred_element_type=f32),
        jnp.dot(bottom, wave, preferred_element_type=f32),
    )


def right(table, conjugate, wave):
    real, plus, minus = three(table, conjugate)
    real_side = jnp.concatenate([real, minus], axis=0)
    imag_side = jnp.concatenate([plus, real], axis=0)
    return (
        jnp.dot(wave, real_side, preferred_element_type=f32),
        jnp.dot(wave, imag_side, preferred_element_type=f32),
    )


def one_hot(size, hit):
    row = lax.broadcasted_iota(jnp.int32, (size, size), 0)
    col = lax.broadcasted_iota(jnp.int32, (size, size), 1)
    return jnp.where(hit(row, col), 1.0, 0.0).astype(bf16)


def in_order(size, slot, measured, amps):
    half = size // 2
    for number, piece in enumerate(measured):
        rows = size // len(measured)
        at = pl.multiple_of(jnp.where(slot == number, 0, size - rows), rows)
        amps[pl.ds(at, rows), :] = piece[0:rows, :]

    def frequency(place, natural):
        return natural == jnp.where(place < half, 2 * place, 2 * (place - half) + 1)

    rows_first = jnp.dot(one_hot(size, frequency), amps[...], preferred_element_type=f32)
    return jnp.dot(
        rows_first.astype(bf16),
        one_hot(size, lambda row, col: frequency(col, row)),
        preferred_element_type=f32,
    )


def roll_kernel(size, meta, far_rows, far_cols, *refs):
    pieces, (probe_out, near_side, far_side) = refs[:-3], refs[-3:]
    offset, slot = meta[0], meta[2]
    half = size // 2

    def moved(to, source):
        gap = to - source - offset
        return (gap == 0) | (gap == -size)

    down = one_hot(size, moved)
    across = one_hot(size, lambda row, col: moved(col, row))
    for c in range(2):
        near_side[c] = jnp.dot(
            far_rows[c], across[:, :half], preferred_element_type=f32
        ).astype(bf16)
        far_side[c] = jnp.dot(down[:half], far_cols[c], preferred_element_type=f32).astype(bf16)
    for c in range(2):
        done = 0
        for piece in pieces:
            turned = jnp.dot(down, piece[c], preferred_element_type=f32).astype(bf16)
            width = turned.shape[1]
            if len(pieces) == 2:
                at = pl.multiple_of(jnp.where(slot == done, 0, width), width)
                probe_out[c, :, pl.ds(at, width)] = turned
                done += 1
            else:
                probe_out[c, :, done : done + width] = turned
                done += width


def rolled(pieces, far_rows, far_cols, meta, size):
    whole = pl.BlockSpec(memory_space=pltpu.VMEM)
    return pl.pallas_call(
        functools.partial(roll_kernel, size),
        out_shape=[
            jax.ShapeDtypeStruct((2, size, size), bf16),
            jax.ShapeDtypeStruct((2, size, size // 2), bf16),
            jax.ShapeDtypeStruct((2, size // 2, size), bf16),
        ],
        in_specs=[pl.BlockSpec(memory_space=pltpu.SMEM)] + [whole] * (2 + len(pieces)),
        out_specs=[whole] * 3,
        compiler_params=pltpu.CompilerParams(vmem_limit_bytes=16 * 1024 * 1024),
        cost_estimate=pl.CostEstimate(
            flops=64 * size**3, bytes_accessed=24 * size * size, transcendentals=0
        ),
        name="rolled",
    )(meta, far_rows, far_cols, *pieces)


def tile_access(size, span, tile_rows, meta, mine, theirs):
    offset, core = meta[0], meta[3]
    parts, _, _, _, width = mine.shape[1:]
    early = lax.broadcasted_iota(jnp.int32, (tile_rows, width), 0) < offset

    def place(k):
        return k // 2 if k % 2 == 0 else k // 2 + core

    def piece(k, h, s, c):
        source = mine if k % 2 == 0 else theirs
        return source[place(k), h, s, c].astype(f32)

    def patch(s, c):
        rows = []
        for k in range(span):
            blocks = [piece(k, h, s, c) for h in range(parts)]
            if k == 0:
                blocks = [jnp.where(early, piece(span, h, s, c), blocks[h]) for h in range(parts)]
            rows.append(jnp.concatenate(blocks, axis=1))
        return jnp.concatenate(rows, axis=0)

    return early, place, patch


def put_rows(rows_buf, pair):
    size = rows_buf.shape[1]
    for c in range(2):
        rows_buf[c * size : (c + 1) * size, :] = pair[c].astype(bf16)


def put_cols(cols_buf, pair):
    size = cols_buf.shape[0]
    for c in range(2):
        cols_buf[:, c * size : (c + 1) * size] = pair[c].astype(bf16)


def put_row_halves(rows_buf, first, second):
    half = rows_buf.shape[1] // 2
    for number, wave in enumerate((*first, *second)):
        rows_buf[number * half : (number + 1) * half, :] = wave.astype(bf16)


def put_col_halves(cols_buf, first, second):
    half = cols_buf.shape[0] // 2
    for number, wave in enumerate((*first, *second)):
        cols_buf[:, number * half : (number + 1) * half] = wave.astype(bf16)


def pair_of(ref):
    return ref[0].astype(f32), ref[1].astype(f32)


def parts_of(ref, rows, cols):
    return ref[0, rows, cols], ref[1, rows, cols]


def both(first, second, axis):
    return [jnp.concatenate([a, b], axis=axis) for a, b in zip(first, second)]


def plus(first, second):
    return [a + b for a, b in zip(first, second)]


def less(first, second):
    return [a - b for a, b in zip(first, second)]


def forth_kernel(
    size, span, tile_rows, meta, mine, theirs, far_cols, near, probe, far_near,
    psi2, field, rows_buf, cols_buf,
):
    half = size // 2
    low, high, everything = slice(0, half), slice(half, size), slice(None)

    @pl.when(meta[1] == 1)
    def _():
        _, _, patch = tile_access(size, span, tile_rows, meta, mine, theirs)
        near_parts = parts_of(near, everything, everything)
        pr, pi = pair_of(probe)
        ar, ai = patch(0, 0), patch(0, 1)
        put_rows(rows_buf, (pr * ar - pi * ai, pr * ai + pi * ar))
        put_cols(cols_buf, left(near_parts, False, rows_buf[...]))
        two = right(near_parts, False, cols_buf[...])
        psi2[0] = two[0].astype(bf16)
        psi2[1] = two[1].astype(bf16)
        wr, wi = pair_of(psi2)
        br, bi = patch(1, 0), patch(1, 1)
        wave_exit = (wr * br - wi * bi, wr * bi + wi * br)
        top, bottom = [x[low] for x in wave_exit], [x[high] for x in wave_exit]
        put_row_halves(rows_buf, plus(top, bottom), less(top, bottom))
        half2 = both(
            left(parts_of(far_near, low, everything), False, rows_buf[0:size, :]),
            left(parts_of(far_near, high, everything), False, rows_buf[size : 2 * size, :]),
            0,
        )
        top, bottom = [x[:, low] for x in half2], [x[:, high] for x in half2]
        put_col_halves(cols_buf, plus(top, bottom), less(top, bottom))
        for cols, source in ((low, cols_buf[:, 0:size]), (high, cols_buf[:, size : 2 * size])):
            fr, fi = right(parts_of(far_cols, low, cols), False, source)
            field[0, :, cols] = fr
            field[1, :, cols] = fi


def back_kernel(
    size, span, tile_rows, meta, mine, theirs, far_rows, near, probe, far_far, psi2, field, *refs,
):
    measured, (keep, send, rows_buf, cols_buf) = refs[:-4], refs[-4:]
    core = meta[3]
    parts, _, _, _, width = keep.shape[1:]
    half = size // 2
    low, high, everything = slice(0, half), slice(half, size), slice(None)

    @pl.when(meta[1] == 1)
    def _():
        early, place, patch = tile_access(size, span, tile_rows, meta, mine, theirs)

        def put_term(s, c, term):
            for k in range(span):
                for h in range(parts):
                    block = term[
                        k * tile_rows : (k + 1) * tile_rows, h * width : (h + 1) * width
                    ]
                    if k == 0:
                        keep[place(span), h, s, c] = jnp.where(early, block, 0.0).astype(bf16)
                        block = jnp.where(early, 0.0, block)
                    target = keep if k % 2 == 0 else send
                    target[place(k), h, s, c] = block.astype(bf16)

        amps = in_order(size, meta[2], measured, cols_buf.at[:, 0:size])
        chis = []
        for cols in (low, high):
            fr, fi = field[0, :, cols], field[1, :, cols]
            keeping = 1.0 - amps[:, cols] * lax.rsqrt(fr * fr + fi * fi + smooth)
            chis.append((fr * keeping, fi * keeping))
        put_col_halves(cols_buf, *chis)
        even = right(parts_of(far_rows, low, low), True, cols_buf[:, 0:size])
        odd = right(parts_of(far_rows, high, low), True, cols_buf[:, size : 2 * size])
        back1 = both(plus(even, odd), less(even, odd), 1)
        put_row_halves(rows_buf, [x[low] for x in back1], [x[high] for x in back1])
        even = left(parts_of(far_far, everything, low), True, rows_buf[0:size, :])
        odd = left(parts_of(far_far, everything, high), True, rows_buf[size : 2 * size, :])
        er, ei = both(plus(even, odd), less(even, odd), 0)
        br, bi = patch(1, 0), patch(1, 1)
        put_cols(cols_buf, (br * er + bi * ei, br * ei - bi * er))
        wr, wi = pair_of(psi2)
        put_term(1, 0, wr * er + wi * ei)
        put_term(1, 1, wr * ei - wi * er)
        near_parts = parts_of(near, everything, everything)
        put_rows(rows_buf, right(near_parts, True, cols_buf[...]))
        gr, gi = left(near_parts, True, rows_buf[...])
        pr, pi = pair_of(probe)
        put_term(0, 0, pr * gr + pi * gi)
        put_term(0, 1, pr * gi - pi * gr)
        send[(1 - core) * (span // 2)] = jnp.zeros(send.shape[1:], bf16)

    @pl.when(meta[1] == 0)
    def _():
        keep[...] = jnp.zeros(keep.shape, bf16)
        send[...] = jnp.zeros(send.shape, bf16)


def small_call(kernel, out_shape, scalars, values, name):
    inside = pl.BlockSpec(memory_space=pltpu.VMEM)
    return pl.pallas_call(
        kernel,
        out_shape=out_shape,
        in_specs=[pl.BlockSpec(memory_space=pltpu.SMEM)] * len(scalars) + [inside] * len(values),
        out_specs=jax.tree.map(lambda _: inside, out_shape),
        compiler_params=pltpu.CompilerParams(vmem_limit_bytes=12 * 1024 * 1024),
        cost_estimate=pl.CostEstimate(flops=0, bytes_accessed=1 << 20, transcendentals=0),
        name=name,
    )(*scalars, *values)


def placed(values, place_of, name):
    def kernel(*refs):
        for number, value in enumerate(refs[:-1]):
            refs[-1][place_of(number)] = value[...]

    shape = jax.ShapeDtypeStruct((len(values),) + values[0].shape, values[0].dtype)
    return small_call(kernel, shape, [], values, name)


def amplitude_messages(amplitudes, row_offsets, position_counts):
    slots, rows, size = amplitudes.shape

    def kernel(offsets, counts, amps, straight, crossed):
        slot = lax.axis_index("scan")
        straight[0:rows, :] = amps[slot].astype(bf16)
        crossed[...] = amps[1 - slot].astype(bf16)
        at = lax.broadcasted_iota(jnp.int32, (16, size), 1)
        notes = jnp.where(at == slots, counts[0].astype(f32), 0.0)
        for number in range(slots):
            notes = jnp.where(at == number, offsets[number].astype(f32), notes)
        straight[rows : rows + 16, :] = notes.astype(bf16)

    shapes = [jax.ShapeDtypeStruct((n, size), bf16) for n in (rows + 16, rows)]
    return small_call(kernel, shapes, [row_offsets, position_counts], [amplitudes], "messages")


def kernel_call(kernel, size, tile_rows, name, flops, out_shape, meta, *inputs):
    inside = pl.BlockSpec(memory_space=pltpu.VMEM)
    return pl.pallas_call(
        functools.partial(kernel, size, size // tile_rows, tile_rows),
        out_shape=out_shape,
        in_specs=[pl.BlockSpec(memory_space=pltpu.SMEM)] + [inside] * len(inputs),
        out_specs=[inside] * len(out_shape),
        scratch_shapes=[
            pltpu.VMEM((2 * size, size), bf16),
            pltpu.VMEM((size, 2 * size), bf16),
        ],
        compiler_params=pltpu.CompilerParams(vmem_limit_bytes=28 * 1024 * 1024),
        cost_estimate=pl.CostEstimate(
            flops=flops, bytes_accessed=size * size, transcendentals=0
        ),
        name=name,
    )(meta, *inputs)


def shards(size, object_slab, probe_wave, amplitudes, row_offsets, position_counts):
    tile_rows = object_slab.shape[2]
    span = size // tile_rows
    count = lax.axis_size("tile")
    parts = lax.axis_size("scan")
    slots = amplitudes.shape[0]
    paired = parts == slots == 2
    slot = lax.axis_index("scan")
    ahead = span // 2
    swap = [(0, 1), (1, 0)]
    ahead_pairs = [(one, (one + ahead) % count) for one in range(count)]

    def brought(value):
        return lax.ppermute(value, "tile", ahead_pairs)

    def paired_with(value, unit):
        return lax.ppermute(value, "tile", [(one, one ^ unit) for one in range(count)])

    def paired_across(value, unit):
        pairs = []
        for one in range(count):
            step = unit if (one // unit) % 2 else -unit
            pairs.append((one, one + step if unit <= one < count - unit else one ^ 1))
        return lax.ppermute(value, "tile", pairs)

    def by_slot(first, second):
        return jnp.where(slot == 0, first, second)

    tile = lax.axis_index("tile")

    def by_place(unit, if_odd, if_even):
        return jnp.where((tile // unit) % 2 == 1, if_odd, if_even)

    own = object_slab.astype(bf16)
    width = own.shape[-1]
    if paired:
        beside = lax.ppermute(own, "scan", swap)
        beside, probe_wave = lax.optimization_barrier((beside, probe_wave))
        whole = placed([own, beside], lambda n: jnp.bitwise_xor(lax.axis_index("scan"), n), "halves")
        probe_pieces = [probe_wave, lax.ppermute(probe_wave, "scan", swap)]
        straight, crossed = amplitude_messages(amplitudes, row_offsets, position_counts)
        straight = brought(straight)
        crossed = lax.ppermute(
            crossed,
            ("tile", "scan"),
            [(2 * a + x, 2 * b + 1 - x) for a, b in ahead_pairs for x in range(2)],
        )
        notes = straight[-16]
        measured = [straight, crossed]
    else:
        whole = lax.all_gather(own, "scan")
        every = lax.all_gather(probe_wave, "scan")
        probe_pieces = [every[number] for number in range(parts)]
        notes = brought(jnp.concatenate([row_offsets, position_counts]))
        every = lax.all_gather(brought(amplitudes.astype(bf16)), "scan")
        measured = [every[:, jnp.minimum(slot, slots - 1)].reshape((size, size))]
    next_across, next_with = paired_across(whole, 4), paired_with(whole, 4)
    near_across, near_with = paired_across(whole, 2), paired_with(whole, 2)
    middle, probe_pieces, notes = lax.optimization_barrier((whole, probe_pieces, notes))
    far_rows, far_cols, near = tables(size)
    core = lax.rem(tile, 2)
    notes = notes[: slots + 1].astype(jnp.int32)
    home = (tile >= ahead) & (tile < count - ahead)
    live = (home & (slot < notes[slots])).astype(jnp.int32)
    meta = jnp.stack(
        [notes[jnp.minimum(slot, slots - 1)], live, slot.astype(jnp.int32), core.astype(jnp.int32)]
    )
    turned, far_near, far_far = rolled(probe_pieces, far_rows, far_cols, meta, size)
    def group(number):
        unit, flip = ((4, 0), (2, 1), (2, 2), (2, 3), (4, 4))[number]
        odd = lax.rem(lax.axis_index("tile") // unit, 2) == 1
        return jnp.where(odd, flip, 4 - flip)

    arrived = [next_with, near_with, middle, near_across, next_across]
    mine = placed(arrived, group, "groups")
    theirs = paired_with(mine, 1)
    shape = jax.ShapeDtypeStruct
    psi2, field = kernel_call(
        forth_kernel, size, tile_rows, "forth", 24 * size**3,
        [shape((2, size, size), bf16), shape((2, size, size), f32)],
        meta, mine, theirs, far_cols, near, turned, far_near,
    )
    measured[-1], field = lax.optimization_barrier((measured[-1], field))
    keep, send = kernel_call(
        back_kernel, size, tile_rows, "back", 24 * size**3,
        [shape((len(arrived), parts, 2, 2, tile_rows, width), bf16)] * 2,
        meta, mine, theirs, far_rows, near, turned, far_far, psi2, field, *measured,
    )
    merged = (keep.astype(f32) + paired_with(send, 1).astype(f32)).astype(bf16)
    total = sum(
        value.astype(f32)
        for value in (
            paired_with(by_place(4, merged[0], merged[4]), 4),
            paired_across(by_place(4, merged[4], merged[0]), 4),
            paired_with(by_place(2, merged[1], merged[3]), 2),
            paired_across(by_place(2, merged[3], merged[1]), 2),
            merged[2],
        )
    )
    if paired:
        away = lax.ppermute(by_slot(total[1], total[0]).astype(bf16), "scan", swap)
        return by_slot(total[0], total[1]) + away.astype(f32)
    return lax.psum_scatter(total, "scan", scatter_dimension=0, tiled=False)


def solution(mesh):
    in_specs = (
        P(None, None, "tile", "scan"),
        P(None, None, "scan"),
        P("tile", "scan", None),
        P("tile"),
        P("tile"),
    )
    out_specs = P(None, None, "tile", "scan")

    def run(object_slab, *rest):
        return jax.shard_map(
            functools.partial(shards, object_slab.shape[3]),
            mesh=mesh, in_specs=in_specs, out_specs=out_specs, check_vma=False,
        )(object_slab, *rest)

    return run
```

```python
import functools
import math

import jax
import jax.numpy as jnp
import ml_dtypes
import numpy as np
from jax import lax
from jax.experimental import pallas as pl
from jax.experimental.pallas import tpu as pltpu
from jax.sharding import PartitionSpec as P

fresnel = 0.5
smooth = 1.0
bf16 = jnp.bfloat16
f32 = jnp.float32


def tables(size):
    index = np.arange(size)
    angles = 2.0 * np.pi / size * (index[:, None] * index[None, :] % size)
    base = np.exp(1j * angles)
    far = np.conj(base) / math.sqrt(size)
    centred = np.where(index < size // 2, index, index - size).astype(np.float64)
    kernel = np.exp(-1j * np.pi * fresnel / size * centred * centred)
    near = (base * kernel[None, :]) @ np.conj(base).T / size

    def parts(table):
        stacked = np.stack([table.real, table.imag])
        return jnp.asarray(stacked.astype(ml_dtypes.bfloat16))

    order = np.concatenate([index[0::2], index[1::2]])
    return parts(far[order]), parts(far[:, order]), parts(near)


def three(table, conjugate):
    real, imag = table
    return (real, -imag, imag) if conjugate else (real, imag, -imag)


def left(table, conjugate, wave):
    real, plus, minus = three(table, conjugate)
    top = jnp.concatenate([real, minus], axis=1)
    bottom = jnp.concatenate([plus, real], axis=1)
    return (
        jnp.dot(top, wave, preferred_element_type=f32),
        jnp.dot(bottom, wave, preferred_element_type=f32),
    )


def right(table, conjugate, wave):
    real, plus, minus = three(table, conjugate)
    real_side = jnp.concatenate([real, minus], axis=0)
    imag_side = jnp.concatenate([plus, real], axis=0)
    return (
        jnp.dot(wave, real_side, preferred_element_type=f32),
        jnp.dot(wave, imag_side, preferred_element_type=f32),
    )


def one_hot(size, hit):
    row = lax.broadcasted_iota(jnp.int32, (size, size), 0)
    col = lax.broadcasted_iota(jnp.int32, (size, size), 1)
    return jnp.where(hit(row, col), 1.0, 0.0).astype(bf16)


def notes_of(span, slots, ref):
    rows = ref.shape[0]
    values = ref[rows - 16 : rows, 0:128].astype(f32)
    row = lax.broadcasted_iota(jnp.int32, values.shape, 0)
    col = lax.broadcasted_iota(jnp.int32, values.shape, 1)

    def note(at):
        return jnp.sum(jnp.where((row == 0) & (col == at), values, 0.0)).astype(jnp.int32)

    tile, slot = lax.axis_index("tile"), lax.axis_index("scan")
    ahead = span // 2
    home = (tile >= ahead) & (tile < lax.axis_size("tile") - ahead)
    live = home & (slot < note(slots))
    return note(jnp.minimum(slot, slots - 1)), live, slot, lax.rem(tile, 2)


def in_order(size, slot, measured, amps):
    half = size // 2
    for number, piece in enumerate(measured):
        rows = size // len(measured)
        at = pl.multiple_of(jnp.where(slot == number, 0, size - rows), rows)
        amps[pl.ds(at, rows), :] = piece[0:rows, :]

    def frequency(place, natural):
        return natural == jnp.where(place < half, 2 * place, 2 * (place - half) + 1)

    rows_first = jnp.dot(one_hot(size, frequency), amps[...], preferred_element_type=f32)
    return jnp.dot(
        rows_first.astype(bf16),
        one_hot(size, lambda row, col: frequency(col, row)),
        preferred_element_type=f32,
    )


def roll_kernel(size, span, slots, notes, far_rows, far_cols, *refs):
    pieces, (probe_out, near_side, far_side) = refs[:-3], refs[-3:]
    offset, _, slot, _ = notes_of(span, slots, notes)
    half = size // 2

    def moved(to, source):
        gap = to - source - offset
        return (gap == 0) | (gap == -size)

    down = one_hot(size, moved)
    across = one_hot(size, lambda row, col: moved(col, row))
    for c in range(2):
        near_side[c] = jnp.dot(
            far_rows[c], across[:, :half], preferred_element_type=f32
        ).astype(bf16)
        far_side[c] = jnp.dot(down[:half], far_cols[c], preferred_element_type=f32).astype(bf16)
    for c in range(2):
        done = 0
        for piece in pieces:
            turned = jnp.dot(down, piece[c], preferred_element_type=f32).astype(bf16)
            width = turned.shape[1]
            if len(pieces) == 2:
                at = pl.multiple_of(jnp.where(slot == done, 0, width), width)
                probe_out[c, :, pl.ds(at, width)] = turned
                done += 1
            else:
                probe_out[c, :, done : done + width] = turned
                done += width


def rolled(pieces, far_rows, far_cols, notes, size, span, slots):
    whole = pl.BlockSpec(memory_space=pltpu.VMEM)
    return pl.pallas_call(
        functools.partial(roll_kernel, size, span, slots),
        out_shape=[
            jax.ShapeDtypeStruct((2, size, size), bf16),
            jax.ShapeDtypeStruct((2, size, size // 2), bf16),
            jax.ShapeDtypeStruct((2, size // 2, size), bf16),
        ],
        in_specs=[whole] * (3 + len(pieces)),
        out_specs=[whole] * 3,
        compiler_params=pltpu.CompilerParams(vmem_limit_bytes=16 * 1024 * 1024),
        cost_estimate=pl.CostEstimate(
            flops=64 * size**3, bytes_accessed=24 * size * size, transcendentals=0
        ),
        name="rolled",
    )(notes, far_rows, far_cols, *pieces)


def tile_access(span, tile_rows, offset, core, mine, theirs):
    parts, _, _, _, width = mine.shape[1:]
    early = lax.broadcasted_iota(jnp.int32, (tile_rows, width), 0) < offset

    def place(k):
        return k // 2 if k % 2 == 0 else k // 2 + core

    def piece(k, h, s, c):
        source = mine if k % 2 == 0 else theirs
        return source[place(k), h, s, c].astype(f32)

    def patch(s, c):
        rows = []
        for k in range(span):
            blocks = [piece(k, h, s, c) for h in range(parts)]
            if k == 0:
                blocks = [jnp.where(early, piece(span, h, s, c), blocks[h]) for h in range(parts)]
            rows.append(jnp.concatenate(blocks, axis=1))
        return jnp.concatenate(rows, axis=0)

    return early, place, patch


def put_rows(rows_buf, pair):
    size = rows_buf.shape[1]
    for c in range(2):
        rows_buf[c * size : (c + 1) * size, :] = pair[c].astype(bf16)


def put_cols(cols_buf, pair):
    size = cols_buf.shape[0]
    for c in range(2):
        cols_buf[:, c * size : (c + 1) * size] = pair[c].astype(bf16)


def put_row_halves(rows_buf, first, second):
    half = rows_buf.shape[1] // 2
    for number, wave in enumerate((*first, *second)):
        rows_buf[number * half : (number + 1) * half, :] = wave.astype(bf16)


def put_col_halves(cols_buf, first, second):
    half = cols_buf.shape[0] // 2
    for number, wave in enumerate((*first, *second)):
        cols_buf[:, number * half : (number + 1) * half] = wave.astype(bf16)


def pair_of(ref):
    return ref[0].astype(f32), ref[1].astype(f32)


def parts_of(ref, rows, cols):
    return ref[0, rows, cols], ref[1, rows, cols]


def both(first, second, axis):
    return [jnp.concatenate([a, b], axis=axis) for a, b in zip(first, second)]


def plus(first, second):
    return [a + b for a, b in zip(first, second)]


def less(first, second):
    return [a - b for a, b in zip(first, second)]


def forth_kernel(
    size, span, slots, tile_rows, notes, mine, theirs, far_cols, near, probe, far_near,
    psi2, field, rows_buf, cols_buf,
):
    half = size // 2
    low, high, everything = slice(0, half), slice(half, size), slice(None)
    offset, live, _, core = notes_of(span, slots, notes)

    @pl.when(live)
    def _():
        _, _, patch = tile_access(span, tile_rows, offset, core, mine, theirs)
        near_parts = parts_of(near, everything, everything)
        pr, pi = pair_of(probe)
        ar, ai = patch(0, 0), patch(0, 1)
        put_rows(rows_buf, (pr * ar - pi * ai, pr * ai + pi * ar))
        put_cols(cols_buf, left(near_parts, False, rows_buf[...]))
        two = right(near_parts, False, cols_buf[...])
        psi2[0] = two[0].astype(bf16)
        psi2[1] = two[1].astype(bf16)
        wr, wi = pair_of(psi2)
        br, bi = patch(1, 0), patch(1, 1)
        wave_exit = (wr * br - wi * bi, wr * bi + wi * br)
        top, bottom = [x[low] for x in wave_exit], [x[high] for x in wave_exit]
        put_row_halves(rows_buf, plus(top, bottom), less(top, bottom))
        half2 = both(
            left(parts_of(far_near, low, everything), False, rows_buf[0:size, :]),
            left(parts_of(far_near, high, everything), False, rows_buf[size : 2 * size, :]),
            0,
        )
        top, bottom = [x[:, low] for x in half2], [x[:, high] for x in half2]
        put_col_halves(cols_buf, plus(top, bottom), less(top, bottom))
        for cols, source in ((low, cols_buf[:, 0:size]), (high, cols_buf[:, size : 2 * size])):
            fr, fi = right(parts_of(far_cols, low, cols), False, source)
            field[0, :, cols] = fr
            field[1, :, cols] = fi


def back_kernel(
    size, span, slots, tile_rows, notes, mine, theirs, far_rows, near, probe, far_far, psi2, field, *refs,
):
    measured, (keep, send, rows_buf, cols_buf) = refs[:-4], refs[-4:]
    offset, live, slot, core = notes_of(span, slots, notes)
    parts, _, _, _, width = keep.shape[1:]
    half = size // 2
    low, high, everything = slice(0, half), slice(half, size), slice(None)

    @pl.when(live)
    def _():
        early, place, patch = tile_access(span, tile_rows, offset, core, mine, theirs)

        def put_term(s, c, term):
            for k in range(span):
                for h in range(parts):
                    block = term[
                        k * tile_rows : (k + 1) * tile_rows, h * width : (h + 1) * width
                    ]
                    if k == 0:
                        keep[place(span), h, s, c] = jnp.where(early, block, 0.0).astype(bf16)
                        block = jnp.where(early, 0.0, block)
                    target = keep if k % 2 == 0 else send
                    target[place(k), h, s, c] = block.astype(bf16)

        amps = in_order(size, slot, measured, cols_buf.at[:, 0:size])
        chis = []
        for cols in (low, high):
            fr, fi = field[0, :, cols], field[1, :, cols]
            keeping = 1.0 - amps[:, cols] * lax.rsqrt(fr * fr + fi * fi + smooth)
            chis.append((fr * keeping, fi * keeping))
        put_col_halves(cols_buf, *chis)
        even = right(parts_of(far_rows, low, low), True, cols_buf[:, 0:size])
        odd = right(parts_of(far_rows, high, low), True, cols_buf[:, size : 2 * size])
        back1 = both(plus(even, odd), less(even, odd), 1)
        put_row_halves(rows_buf, [x[low] for x in back1], [x[high] for x in back1])
        even = left(parts_of(far_far, everything, low), True, rows_buf[0:size, :])
        odd = left(parts_of(far_far, everything, high), True, rows_buf[size : 2 * size, :])
        er, ei = both(plus(even, odd), less(even, odd), 0)
        br, bi = patch(1, 0), patch(1, 1)
        put_cols(cols_buf, (br * er + bi * ei, br * ei - bi * er))
        wr, wi = pair_of(psi2)
        put_term(1, 0, wr * er + wi * ei)
        put_term(1, 1, wr * ei - wi * er)
        near_parts = parts_of(near, everything, everything)
        put_rows(rows_buf, right(near_parts, True, cols_buf[...]))
        gr, gi = left(near_parts, True, rows_buf[...])
        pr, pi = pair_of(probe)
        put_term(0, 0, pr * gr + pi * gi)
        put_term(0, 1, pr * gi - pi * gr)
        send[(1 - core) * (span // 2)] = jnp.zeros(send.shape[1:], bf16)

    @pl.when(jnp.logical_not(live))
    def _():
        keep[...] = jnp.zeros(keep.shape, bf16)
        send[...] = jnp.zeros(send.shape, bf16)


def small_call(kernel, out_shape, scalars, values, name):
    inside = pl.BlockSpec(memory_space=pltpu.VMEM)
    return pl.pallas_call(
        kernel,
        out_shape=out_shape,
        in_specs=[pl.BlockSpec(memory_space=pltpu.SMEM)] * len(scalars) + [inside] * len(values),
        out_specs=jax.tree.map(lambda _: inside, out_shape),
        compiler_params=pltpu.CompilerParams(vmem_limit_bytes=12 * 1024 * 1024),
        cost_estimate=pl.CostEstimate(flops=0, bytes_accessed=1 << 20, transcendentals=0),
        name=name,
    )(*scalars, *values)


def placed(values, place_of, name):
    def kernel(*refs):
        for number, value in enumerate(refs[:-1]):
            refs[-1][place_of(number)] = value[...]

    shape = jax.ShapeDtypeStruct((len(values),) + values[0].shape, values[0].dtype)
    return small_call(kernel, shape, [], values, name)


def amplitude_messages(amplitudes, row_offsets, position_counts):
    slots, rows, size = amplitudes.shape

    def kernel(offsets, counts, amps, straight, crossed):
        slot = lax.axis_index("scan")
        straight[0:rows, :] = amps[slot].astype(bf16)
        crossed[...] = amps[1 - slot].astype(bf16)
        at = lax.broadcasted_iota(jnp.int32, (16, size), 1)
        notes = jnp.where(at == slots, counts[0].astype(f32), 0.0)
        for number in range(slots):
            notes = jnp.where(at == number, offsets[number].astype(f32), notes)
        straight[rows : rows + 16, :] = notes.astype(bf16)

    shapes = [jax.ShapeDtypeStruct((n, size), bf16) for n in (rows + 16, rows)]
    return small_call(kernel, shapes, [row_offsets, position_counts], [amplitudes], "messages")


def group(number):
    unit, flip = ((4, 0), (2, 1), (2, 2), (2, 3), (4, 4))[number]
    odd = lax.rem(lax.axis_index("tile") // unit, 2) == 1
    return jnp.where(odd, flip, 4 - flip)


def merged_messages(keep, got):
    def kernel(keep, got, *outs):
        for number, out in enumerate(outs):
            at = group(number)
            out[...] = (keep[at].astype(f32) + got[at].astype(f32)).astype(bf16)

    return small_call(kernel, [jax.ShapeDtypeStruct(keep.shape[1:], bf16)] * 5, [], [keep, got], "merge")


def halves_of_sum(values):
    def kernel(*refs):
        (own, away), slot = refs[-2:], lax.axis_index("scan")

        def half(h):
            return sum(ref[h].astype(f32) for ref in refs[:-2])

        own[...] = half(slot)
        away[...] = half(1 - slot).astype(bf16)

    shape = values[0].shape[1:]
    shapes = [jax.ShapeDtypeStruct(shape, f32), jax.ShapeDtypeStruct(shape, bf16)]
    return small_call(kernel, shapes, [], values, "sums")


def kernel_call(kernel, size, slots, tile_rows, name, out_shape, *inputs):
    inside = pl.BlockSpec(memory_space=pltpu.VMEM)
    return pl.pallas_call(
        functools.partial(kernel, size, size // tile_rows, slots, tile_rows),
        out_shape=out_shape,
        in_specs=[inside] * len(inputs),
        out_specs=[inside] * len(out_shape),
        scratch_shapes=[
            pltpu.VMEM((2 * size, size), bf16),
            pltpu.VMEM((size, 2 * size), bf16),
        ],
        compiler_params=pltpu.CompilerParams(vmem_limit_bytes=28 * 1024 * 1024),
        cost_estimate=pl.CostEstimate(
            flops=24 * size**3, bytes_accessed=size * size, transcendentals=0
        ),
        name=name,
    )(*inputs)


def shards(size, object_slab, probe_wave, amplitudes, row_offsets, position_counts):
    tile_rows = object_slab.shape[2]
    span = size // tile_rows
    count = lax.axis_size("tile")
    parts = lax.axis_size("scan")
    slots = amplitudes.shape[0]
    paired = parts == slots == 2
    ahead = span // 2
    swap = [(0, 1), (1, 0)]
    ahead_pairs = [(one, (one + ahead) % count) for one in range(count)]

    def brought(value):
        return lax.ppermute(value, "tile", ahead_pairs)

    def paired_with(value, unit):
        return lax.ppermute(value, "tile", [(one, one ^ unit) for one in range(count)])

    def paired_across(value, unit):
        pairs = []
        for one in range(count):
            step = unit if (one // unit) % 2 else -unit
            pairs.append((one, one + step if unit <= one < count - unit else one ^ 1))
        return lax.ppermute(value, "tile", pairs)

    own = object_slab.astype(bf16)
    width = own.shape[-1]
    if paired:
        beside = lax.ppermute(own, "scan", swap)
        beside, probe_wave = lax.optimization_barrier((beside, probe_wave))
        whole = placed([own, beside], lambda n: jnp.bitwise_xor(lax.axis_index("scan"), n), "halves")
        probe_pieces = [probe_wave, lax.ppermute(probe_wave, "scan", swap)]
        straight, crossed = amplitude_messages(amplitudes, row_offsets, position_counts)
        straight = brought(straight)
        crossed = lax.ppermute(
            crossed,
            ("tile", "scan"),
            [(2 * a + x, 2 * b + 1 - x) for a, b in ahead_pairs for x in range(2)],
        )
        notes = straight
        measured = [straight, crossed]
    else:
        whole = lax.all_gather(own, "scan")
        every = lax.all_gather(probe_wave, "scan")
        probe_pieces = [every[number] for number in range(parts)]
        notes = jnp.concatenate([row_offsets, position_counts]).astype(bf16)
        notes = brought(jnp.pad(notes[None], ((0, 15), (0, size - slots - 1))))
        every = lax.all_gather(brought(amplitudes.astype(bf16)), "scan")
        slot = lax.axis_index("scan")
        measured = [every[:, jnp.minimum(slot, slots - 1)].reshape((size, size))]
    next_across, next_with = paired_across(whole, 4), paired_with(whole, 4)
    near_across, near_with = paired_across(whole, 2), paired_with(whole, 2)
    middle, probe_pieces, notes = lax.optimization_barrier((whole, probe_pieces, notes))
    far_rows, far_cols, near = tables(size)
    turned, far_near, far_far = rolled(
        probe_pieces, far_rows, far_cols, notes, size, span, slots
    )
    arrived = [next_with, near_with, middle, near_across, next_across]
    mine = placed(arrived, group, "groups")
    theirs = paired_with(mine, 1)
    shape = jax.ShapeDtypeStruct
    psi2, field = kernel_call(
        forth_kernel, size, slots, tile_rows, "forth",
        [shape((2, size, size), bf16), shape((2, size, size), f32)],
        notes, mine, theirs, far_cols, near, turned, far_near,
    )
    measured[-1], field = lax.optimization_barrier((measured[-1], field))
    keep, send = kernel_call(
        back_kernel, size, slots, tile_rows, "back",
        [shape((len(arrived), parts, 2, 2, tile_rows, width), bf16)] * 2,
        notes, mine, theirs, far_rows, near, turned, far_far, psi2, field, *measured,
    )
    next_with, near_with, middle, near_across, next_across = merged_messages(
        keep, paired_with(send, 1)
    )
    returned = [
        paired_with(near_with, 2),
        paired_across(near_across, 2),
        paired_with(next_with, 4),
        paired_across(next_across, 4),
        middle,
    ]
    if paired:
        kept, away = halves_of_sum(returned)
        return kept + lax.ppermute(away, "scan", swap).astype(f32)
    total = sum(value.astype(f32) for value in returned)
    return lax.psum_scatter(total, "scan", scatter_dimension=0, tiled=False)


def solution(mesh):
    in_specs = (
        P(None, None, "tile", "scan"),
        P(None, None, "scan"),
        P("tile", "scan", None),
        P("tile"),
        P("tile"),
    )
    out_specs = P(None, None, "tile", "scan")

    def run(object_slab, *rest):
        return jax.shard_map(
            functools.partial(shards, object_slab.shape[3]),
            mesh=mesh, in_specs=in_specs, out_specs=out_specs, check_vma=False,
        )(object_slab, *rest)

    return run
```

```python
import functools
import math

import jax
import jax.numpy as jnp
import ml_dtypes
import numpy as np
from jax import lax
from jax.experimental import pallas as pl
from jax.experimental.pallas import tpu as pltpu
from jax.sharding import PartitionSpec as P

fresnel = 0.5
smooth = 1.0
bf16 = jnp.bfloat16
f32 = jnp.float32


def tables(size):
    index = np.arange(size)
    angles = 2.0 * np.pi / size * (index[:, None] * index[None, :] % size)
    base = np.exp(1j * angles)
    far = np.conj(base) / math.sqrt(size)
    centred = np.where(index < size // 2, index, index - size).astype(np.float64)
    kernel = np.exp(-1j * np.pi * fresnel / size * centred * centred)
    near = (base * kernel[None, :]) @ np.conj(base).T / size

    def parts(table):
        stacked = np.stack([table.real, table.imag])
        return jnp.asarray(stacked.astype(ml_dtypes.bfloat16))

    order = np.concatenate([index[0::2], index[1::2]])
    return parts(far[order]), parts(far[:, order]), parts(near)


def three(table, conjugate):
    real, imag = table
    return (real, -imag, imag) if conjugate else (real, imag, -imag)


def left(table, conjugate, wave):
    real, plus, minus = three(table, conjugate)
    top = jnp.concatenate([real, minus], axis=1)
    bottom = jnp.concatenate([plus, real], axis=1)
    return (
        jnp.dot(top, wave, preferred_element_type=f32),
        jnp.dot(bottom, wave, preferred_element_type=f32),
    )


def right(table, conjugate, wave):
    real, plus, minus = three(table, conjugate)
    real_side = jnp.concatenate([real, minus], axis=0)
    imag_side = jnp.concatenate([plus, real], axis=0)
    return (
        jnp.dot(wave, real_side, preferred_element_type=f32),
        jnp.dot(wave, imag_side, preferred_element_type=f32),
    )


def one_hot(size, hit):
    row = lax.broadcasted_iota(jnp.int32, (size, size), 0)
    col = lax.broadcasted_iota(jnp.int32, (size, size), 1)
    return jnp.where(hit(row, col), 1.0, 0.0).astype(bf16)


def notes_of(span, slots, ref):
    rows = ref.shape[0]
    values = ref[rows - 16 : rows, 0:128].astype(f32)
    row = lax.broadcasted_iota(jnp.int32, values.shape, 0)
    col = lax.broadcasted_iota(jnp.int32, values.shape, 1)

    def note(at):
        return jnp.sum(jnp.where((row == 0) & (col == at), values, 0.0)).astype(jnp.int32)

    tile, slot = lax.axis_index("tile"), lax.axis_index("scan")
    ahead = span // 2
    home = (tile >= ahead) & (tile < lax.axis_size("tile") - ahead)
    live = home & (slot < note(slots))
    return note(jnp.minimum(slot, slots - 1)), live, slot, lax.rem(tile, 2)


def in_order(size, slot, measured, amps):
    half = size // 2
    for number, piece in enumerate(measured):
        rows = size // len(measured)
        at = pl.multiple_of(jnp.where(slot == number, 0, size - rows), rows)
        amps[pl.ds(at, rows), :] = piece[0:rows, :]

    def frequency(place, natural):
        return natural == jnp.where(place < half, 2 * place, 2 * (place - half) + 1)

    rows_first = jnp.dot(one_hot(size, frequency), amps[...], preferred_element_type=f32)
    return jnp.dot(
        rows_first.astype(bf16),
        one_hot(size, lambda row, col: frequency(col, row)),
        preferred_element_type=f32,
    )


def roll_kernel(size, span, slots, notes, far_rows, far_cols, *refs):
    pieces, (probe_out, near_side, far_side) = refs[:-3], refs[-3:]
    offset, _, slot, _ = notes_of(span, slots, notes)
    half = size // 2

    def moved(to, source):
        gap = to - source - offset
        return (gap == 0) | (gap == -size)

    down = one_hot(size, moved)
    across = one_hot(size, lambda row, col: moved(col, row))
    for c in range(2):
        near_side[c] = jnp.dot(
            far_rows[c], across[:, :half], preferred_element_type=f32
        ).astype(bf16)
        far_side[c] = jnp.dot(down[:half], far_cols[c], preferred_element_type=f32).astype(bf16)
    for c in range(2):
        done = 0
        for piece in pieces:
            turned = jnp.dot(down, piece[c], preferred_element_type=f32).astype(bf16)
            width = turned.shape[1]
            if len(pieces) == 2:
                at = pl.multiple_of(jnp.where(slot == done, 0, width), width)
                probe_out[c, :, pl.ds(at, width)] = turned
                done += 1
            else:
                probe_out[c, :, done : done + width] = turned
                done += width


def rolled(pieces, far_rows, far_cols, notes, size, span, slots):
    whole = pl.BlockSpec(memory_space=pltpu.VMEM)
    return pl.pallas_call(
        functools.partial(roll_kernel, size, span, slots),
        out_shape=[
            jax.ShapeDtypeStruct((2, size, size), bf16),
            jax.ShapeDtypeStruct((2, size, size // 2), bf16),
            jax.ShapeDtypeStruct((2, size // 2, size), bf16),
        ],
        in_specs=[whole] * (3 + len(pieces)),
        out_specs=[whole] * 3,
        compiler_params=pltpu.CompilerParams(vmem_limit_bytes=16 * 1024 * 1024),
        cost_estimate=pl.CostEstimate(
            flops=64 * size**3, bytes_accessed=24 * size * size, transcendentals=0
        ),
        name="rolled",
    )(notes, far_rows, far_cols, *pieces)


def tile_access(span, tile_rows, offset, core, mine, theirs):
    parts, _, _, _, width = mine.shape[1:]
    early = lax.broadcasted_iota(jnp.int32, (tile_rows, width), 0) < offset

    def place(k):
        return k // 2 if k % 2 == 0 else k // 2 + core

    def piece(k, h, s, c):
        source = mine if k % 2 == 0 else theirs
        return source[place(k), h, s, c].astype(f32)

    def patch(s, c):
        rows = []
        for k in range(span):
            blocks = [piece(k, h, s, c) for h in range(parts)]
            if k == 0:
                blocks = [jnp.where(early, piece(span, h, s, c), blocks[h]) for h in range(parts)]
            rows.append(jnp.concatenate(blocks, axis=1))
        return jnp.concatenate(rows, axis=0)

    return early, place, patch


def put_rows(rows_buf, pair):
    size = rows_buf.shape[1]
    for c in range(2):
        rows_buf[c * size : (c + 1) * size, :] = pair[c].astype(bf16)


def put_cols(cols_buf, pair):
    size = cols_buf.shape[0]
    for c in range(2):
        cols_buf[:, c * size : (c + 1) * size] = pair[c].astype(bf16)


def put_row_halves(rows_buf, first, second):
    half = rows_buf.shape[1] // 2
    for number, wave in enumerate((*first, *second)):
        rows_buf[number * half : (number + 1) * half, :] = wave.astype(bf16)


def put_col_halves(cols_buf, first, second):
    half = cols_buf.shape[0] // 2
    for number, wave in enumerate((*first, *second)):
        cols_buf[:, number * half : (number + 1) * half] = wave.astype(bf16)


def pair_of(ref):
    return ref[0].astype(f32), ref[1].astype(f32)


def parts_of(ref, rows, cols):
    return ref[0, rows, cols], ref[1, rows, cols]


def both(first, second, axis):
    return [jnp.concatenate([a, b], axis=axis) for a, b in zip(first, second)]


def plus(first, second):
    return [a + b for a, b in zip(first, second)]


def less(first, second):
    return [a - b for a, b in zip(first, second)]


def forth_kernel(
    size, span, slots, tile_rows, notes, mine, theirs, far_cols, near, probe, far_near,
    psi2, field, rows_buf, cols_buf,
):
    half = size // 2
    low, high, everything = slice(0, half), slice(half, size), slice(None)
    offset, live, _, core = notes_of(span, slots, notes)

    @pl.when(live)
    def _():
        _, _, patch = tile_access(span, tile_rows, offset, core, mine, theirs)
        near_parts = parts_of(near, everything, everything)
        pr, pi = pair_of(probe)
        ar, ai = patch(0, 0), patch(0, 1)
        put_rows(rows_buf, (pr * ar - pi * ai, pr * ai + pi * ar))
        put_cols(cols_buf, left(near_parts, False, rows_buf[...]))
        two = right(near_parts, False, cols_buf[...])
        psi2[0] = two[0].astype(bf16)
        psi2[1] = two[1].astype(bf16)
        wr, wi = pair_of(psi2)
        br, bi = patch(1, 0), patch(1, 1)
        wave_exit = (wr * br - wi * bi, wr * bi + wi * br)
        top, bottom = [x[low] for x in wave_exit], [x[high] for x in wave_exit]
        put_row_halves(rows_buf, plus(top, bottom), less(top, bottom))
        half2 = both(
            left(parts_of(far_near, low, everything), False, rows_buf[0:size, :]),
            left(parts_of(far_near, high, everything), False, rows_buf[size : 2 * size, :]),
            0,
        )
        top, bottom = [x[:, low] for x in half2], [x[:, high] for x in half2]
        put_col_halves(cols_buf, plus(top, bottom), less(top, bottom))
        for cols, source in ((low, cols_buf[:, 0:size]), (high, cols_buf[:, size : 2 * size])):
            fr, fi = right(parts_of(far_cols, low, cols), False, source)
            field[0, :, cols] = fr
            field[1, :, cols] = fi


def back_kernel(
    size, span, slots, tile_rows, notes, mine, theirs, far_rows, near, probe, far_far, psi2, field, *refs,
):
    measured, (keep, send, rows_buf, cols_buf) = refs[:-4], refs[-4:]
    offset, live, slot, core = notes_of(span, slots, notes)
    parts, _, _, _, width = keep.shape[1:]
    half = size // 2
    low, high, everything = slice(0, half), slice(half, size), slice(None)

    @pl.when(live)
    def _():
        early, place, patch = tile_access(span, tile_rows, offset, core, mine, theirs)

        def put_term(s, c, term):
            for k in range(span):
                for h in range(parts):
                    block = term[
                        k * tile_rows : (k + 1) * tile_rows, h * width : (h + 1) * width
                    ]
                    if k == 0:
                        keep[place(span), h, s, c] = jnp.where(early, block, 0.0).astype(bf16)
                        block = jnp.where(early, 0.0, block)
                    target = keep if k % 2 == 0 else send
                    target[place(k), h, s, c] = block.astype(bf16)

        amps = in_order(size, slot, measured, cols_buf.at[:, 0:size])
        chis = []
        for cols in (low, high):
            fr, fi = field[0, :, cols], field[1, :, cols]
            keeping = 1.0 - amps[:, cols] * lax.rsqrt(fr * fr + fi * fi + smooth)
            chis.append((fr * keeping, fi * keeping))
        put_col_halves(cols_buf, *chis)
        even = right(parts_of(far_rows, low, low), True, cols_buf[:, 0:size])
        odd = right(parts_of(far_rows, high, low), True, cols_buf[:, size : 2 * size])
        back1 = both(plus(even, odd), less(even, odd), 1)
        put_row_halves(rows_buf, [x[low] for x in back1], [x[high] for x in back1])
        even = left(parts_of(far_far, everything, low), True, rows_buf[0:size, :])
        odd = left(parts_of(far_far, everything, high), True, rows_buf[size : 2 * size, :])
        er, ei = both(plus(even, odd), less(even, odd), 0)
        br, bi = patch(1, 0), patch(1, 1)
        put_cols(cols_buf, (br * er + bi * ei, br * ei - bi * er))
        wr, wi = pair_of(psi2)
        put_term(1, 0, wr * er + wi * ei)
        put_term(1, 1, wr * ei - wi * er)
        near_parts = parts_of(near, everything, everything)
        put_rows(rows_buf, right(near_parts, True, cols_buf[...]))
        gr, gi = left(near_parts, True, rows_buf[...])
        pr, pi = pair_of(probe)
        put_term(0, 0, pr * gr + pi * gi)
        put_term(0, 1, pr * gi - pi * gr)
        send[(1 - core) * (span // 2)] = jnp.zeros(send.shape[1:], bf16)

    @pl.when(jnp.logical_not(live))
    def _():
        keep[...] = jnp.zeros(keep.shape, bf16)
        send[...] = jnp.zeros(send.shape, bf16)


def small_call(kernel, out_shape, scalars, values, name):
    inside = pl.BlockSpec(memory_space=pltpu.VMEM)
    return pl.pallas_call(
        kernel,
        out_shape=out_shape,
        in_specs=[pl.BlockSpec(memory_space=pltpu.SMEM)] * len(scalars) + [inside] * len(values),
        out_specs=jax.tree.map(lambda _: inside, out_shape),
        compiler_params=pltpu.CompilerParams(vmem_limit_bytes=12 * 1024 * 1024),
        cost_estimate=pl.CostEstimate(flops=0, bytes_accessed=1 << 20, transcendentals=0),
        name=name,
    )(*scalars, *values)


def placed(values, place_of, name):
    def kernel(*refs):
        for number, value in enumerate(refs[:-1]):
            refs[-1][place_of(number)] = value[...]

    shape = jax.ShapeDtypeStruct((len(values),) + values[0].shape, values[0].dtype)
    return small_call(kernel, shape, [], values, name)


def amplitude_messages(amplitudes, row_offsets, position_counts):
    slots, rows, size = amplitudes.shape

    def kernel(offsets, counts, amps, straight, crossed):
        slot = lax.axis_index("scan")
        straight[0:rows, :] = amps[slot].astype(bf16)
        crossed[...] = amps[1 - slot].astype(bf16)
        at = lax.broadcasted_iota(jnp.int32, (16, size), 1)
        notes = jnp.where(at == slots, counts[0].astype(f32), 0.0)
        for number in range(slots):
            notes = jnp.where(at == number, offsets[number].astype(f32), notes)
        straight[rows : rows + 16, :] = notes.astype(bf16)

    shapes = [jax.ShapeDtypeStruct((n, size), bf16) for n in (rows + 16, rows)]
    return small_call(kernel, shapes, [row_offsets, position_counts], [amplitudes], "messages")


def group(number):
    unit, flip = ((4, 0), (2, 1), (2, 2), (2, 3), (4, 4))[number]
    odd = lax.rem(lax.axis_index("tile") // unit, 2) == 1
    return jnp.where(odd, flip, 4 - flip)


def merged_messages(keep, got):
    def kernel(keep, got, *outs):
        for number, out in enumerate(outs):
            at = group(number)
            out[...] = (keep[at].astype(f32) + got[at].astype(f32)).astype(bf16)

    return small_call(kernel, [jax.ShapeDtypeStruct(keep.shape[1:], bf16)] * 5, [], [keep, got], "merge")


def merged_in_halves(keep, got):
    def kernel(keep, got, next_with, next_across, middle, near_own, near_away):
        def chunk(number, *half):
            at = (group(number), *half)
            return keep[at].astype(f32) + got[at].astype(f32)

        slot = lax.axis_index("scan")
        for place, number in enumerate((1, 3)):
            near_own[place] = chunk(number, slot).astype(bf16)
            near_away[place] = chunk(number, 1 - slot).astype(bf16)
        for out, number in ((next_with, 0), (next_across, 4), (middle, 2)):
            out[...] = chunk(number).astype(bf16)

    whole = jax.ShapeDtypeStruct(keep.shape[1:], bf16)
    near = jax.ShapeDtypeStruct((2,) + keep.shape[2:], bf16)
    return small_call(kernel, [whole] * 3 + [near] * 2, [], [keep, got], "merge")


def near_messages(own, got):
    def kernel(own, got, *outs):
        for place, out in enumerate(outs):
            out[...] = (own[place].astype(f32) + got[place].astype(f32)).astype(bf16)

    return small_call(kernel, [jax.ShapeDtypeStruct(own.shape[1:], bf16)] * 2, [], [own, got], "near")


def halves_of_sum(values):
    def kernel(*refs):
        (own, away), slot = refs[-2:], lax.axis_index("scan")

        def half(h):
            return sum(ref[h].astype(f32) for ref in refs[:-2])

        own[...] = half(slot)
        away[...] = half(1 - slot).astype(bf16)

    shape = values[0].shape[1:]
    shapes = [jax.ShapeDtypeStruct(shape, f32), jax.ShapeDtypeStruct(shape, bf16)]
    return small_call(kernel, shapes, [], values, "sums")


def kernel_call(kernel, size, slots, tile_rows, name, out_shape, *inputs):
    inside = pl.BlockSpec(memory_space=pltpu.VMEM)
    return pl.pallas_call(
        functools.partial(kernel, size, size // tile_rows, slots, tile_rows),
        out_shape=out_shape,
        in_specs=[inside] * len(inputs),
        out_specs=[inside] * len(out_shape),
        scratch_shapes=[
            pltpu.VMEM((2 * size, size), bf16),
            pltpu.VMEM((size, 2 * size), bf16),
        ],
        compiler_params=pltpu.CompilerParams(vmem_limit_bytes=28 * 1024 * 1024),
        cost_estimate=pl.CostEstimate(
            flops=24 * size**3, bytes_accessed=size * size, transcendentals=0
        ),
        name=name,
    )(*inputs)


def shards(size, object_slab, probe_wave, amplitudes, row_offsets, position_counts):
    tile_rows = object_slab.shape[2]
    span = size // tile_rows
    count = lax.axis_size("tile")
    parts = lax.axis_size("scan")
    slots = amplitudes.shape[0]
    paired = parts == slots == 2
    ahead = span // 2
    swap = [(0, 1), (1, 0)]
    ahead_pairs = [(one, (one + ahead) % count) for one in range(count)]

    def brought(value):
        return lax.ppermute(value, "tile", ahead_pairs)

    def paired_with(value, unit):
        return lax.ppermute(value, "tile", [(one, one ^ unit) for one in range(count)])

    def paired_across(value, unit):
        pairs = []
        for one in range(count):
            step = unit if (one // unit) % 2 else -unit
            pairs.append((one, one + step if unit <= one < count - unit else one ^ 1))
        return lax.ppermute(value, "tile", pairs)

    own = object_slab.astype(bf16)
    width = own.shape[-1]
    if paired:
        beside = lax.ppermute(own, "scan", swap)
        beside, probe_wave = lax.optimization_barrier((beside, probe_wave))
        whole = placed([own, beside], lambda n: jnp.bitwise_xor(lax.axis_index("scan"), n), "halves")
        probe_pieces = [probe_wave, lax.ppermute(probe_wave, "scan", swap)]
        straight, crossed = amplitude_messages(amplitudes, row_offsets, position_counts)
        straight = brought(straight)
        crossed = lax.ppermute(
            crossed,
            ("tile", "scan"),
            [(2 * a + x, 2 * b + 1 - x) for a, b in ahead_pairs for x in range(2)],
        )
        notes = straight
        measured = [straight, crossed]
    else:
        whole = lax.all_gather(own, "scan")
        every = lax.all_gather(probe_wave, "scan")
        probe_pieces = [every[number] for number in range(parts)]
        notes = jnp.concatenate([row_offsets, position_counts]).astype(bf16)
        notes = brought(jnp.pad(notes[None], ((0, 15), (0, size - slots - 1))))
        every = lax.all_gather(brought(amplitudes.astype(bf16)), "scan")
        slot = lax.axis_index("scan")
        measured = [every[:, jnp.minimum(slot, slots - 1)].reshape((size, size))]
    next_across, next_with = paired_across(whole, 4), paired_with(whole, 4)
    near_across, near_with = paired_across(whole, 2), paired_with(whole, 2)
    middle, probe_pieces, notes = lax.optimization_barrier((whole, probe_pieces, notes))
    far_rows, far_cols, near = tables(size)
    turned, far_near, far_far = rolled(
        probe_pieces, far_rows, far_cols, notes, size, span, slots
    )
    arrived = [near_with, next_with, middle, near_across, next_across]
    mine = placed(arrived, lambda n: group((1, 0, 2, 3, 4)[n]), "groups")
    theirs = paired_with(mine, 1)
    shape = jax.ShapeDtypeStruct
    psi2, field = kernel_call(
        forth_kernel, size, slots, tile_rows, "forth",
        [shape((2, size, size), bf16), shape((2, size, size), f32)],
        notes, mine, theirs, far_cols, near, turned, far_near,
    )
    measured[-1], field = lax.optimization_barrier((measured[-1], field))
    keep, send = kernel_call(
        back_kernel, size, slots, tile_rows, "back",
        [shape((len(arrived), parts, 2, 2, tile_rows, width), bf16)] * 2,
        notes, mine, theirs, far_rows, near, turned, far_far, psi2, field, *measured,
    )
    got = paired_with(send, 1)
    if paired:
        next_with, next_across, middle, near_own, near_away = merged_in_halves(keep, got)
        near_got = lax.ppermute(near_away, "scan", swap)
        near_with, near_across = near_messages(near_own, near_got)
        near = [paired_across(near_across, 2), paired_with(near_with, 2)]
        middle, near_with = lax.optimization_barrier((middle, near_with))
        far = [paired_with(next_with, 4), paired_across(next_across, 4), middle]
        kept, away = halves_of_sum(far)
        for value in (lax.ppermute(away, "scan", swap), *near):
            kept = kept + value.astype(f32)
        return kept
    next_with, near_with, middle, near_across, next_across = merged_messages(keep, got)
    returned = [
        paired_with(near_with, 2),
        paired_across(near_across, 2),
        paired_with(next_with, 4),
        paired_across(next_across, 4),
        middle,
    ]
    total = sum(value.astype(f32) for value in returned)
    return lax.psum_scatter(total, "scan", scatter_dimension=0, tiled=False)


def solution(mesh):
    in_specs = (
        P(None, None, "tile", "scan"),
        P(None, None, "scan"),
        P("tile", "scan", None),
        P("tile"),
        P("tile"),
    )
    out_specs = P(None, None, "tile", "scan")

    def run(object_slab, *rest):
        return jax.shard_map(
            functools.partial(shards, object_slab.shape[3]),
            mesh=mesh, in_specs=in_specs, out_specs=out_specs, check_vma=False,
        )(object_slab, *rest)

    return run
```

```python
import functools
import math

import jax
import jax.numpy as jnp
import ml_dtypes
import numpy as np
from jax import lax
from jax.experimental import pallas as pl
from jax.experimental.pallas import tpu as pltpu
from jax.sharding import PartitionSpec as P

fresnel = 0.5
smooth = 1.0
bf16 = jnp.bfloat16
f32 = jnp.float32


def tables(size):
    index = np.arange(size)
    angles = 2.0 * np.pi / size * (index[:, None] * index[None, :] % size)
    base = np.exp(1j * angles)
    far = np.conj(base) / math.sqrt(size)
    centred = np.where(index < size // 2, index, index - size).astype(np.float64)
    kernel = np.exp(-1j * np.pi * fresnel / size * centred * centred)
    near = (base * kernel[None, :]) @ np.conj(base).T / size

    def parts(table):
        stacked = np.stack([table.real, table.imag])
        return jnp.asarray(stacked.astype(ml_dtypes.bfloat16))

    order = np.concatenate([index[0::2], index[1::2]])
    return parts(far[order]), parts(far[:, order]), parts(near)


def three(table, conjugate):
    real, imag = table
    return (real, -imag, imag) if conjugate else (real, imag, -imag)


def left(table, conjugate, wave):
    real, plus, minus = three(table, conjugate)
    top = jnp.concatenate([real, minus], axis=1)
    bottom = jnp.concatenate([plus, real], axis=1)
    return (
        jnp.dot(top, wave, preferred_element_type=f32),
        jnp.dot(bottom, wave, preferred_element_type=f32),
    )


def right(table, conjugate, wave):
    real, plus, minus = three(table, conjugate)
    real_side = jnp.concatenate([real, minus], axis=0)
    imag_side = jnp.concatenate([plus, real], axis=0)
    return (
        jnp.dot(wave, real_side, preferred_element_type=f32),
        jnp.dot(wave, imag_side, preferred_element_type=f32),
    )


def one_hot(size, hit):
    row = lax.broadcasted_iota(jnp.int32, (size, size), 0)
    col = lax.broadcasted_iota(jnp.int32, (size, size), 1)
    return jnp.where(hit(row, col), 1.0, 0.0).astype(bf16)


def notes_of(span, slots, ref):
    rows = ref.shape[0]
    values = ref[rows - 16 : rows, 0:128].astype(f32)
    row = lax.broadcasted_iota(jnp.int32, values.shape, 0)
    col = lax.broadcasted_iota(jnp.int32, values.shape, 1)

    def note(at):
        return jnp.sum(jnp.where((row == 0) & (col == at), values, 0.0)).astype(jnp.int32)

    tile, slot = lax.axis_index("tile"), lax.axis_index("scan")
    ahead = span // 2
    home = (tile >= ahead) & (tile < lax.axis_size("tile") - ahead)
    live = home & (slot < note(slots))
    return note(jnp.minimum(slot, slots - 1)), live, slot, lax.rem(tile, 2)


def in_order(size, slot, measured, amps):
    half = size // 2
    for number, piece in enumerate(measured):
        rows = size // len(measured)
        at = pl.multiple_of(jnp.where(slot == number, 0, size - rows), rows)
        amps[pl.ds(at, rows), :] = piece[0:rows, :]

    def frequency(place, natural):
        return natural == jnp.where(place < half, 2 * place, 2 * (place - half) + 1)

    rows_first = jnp.dot(one_hot(size, frequency), amps[...], preferred_element_type=f32)
    return jnp.dot(
        rows_first.astype(bf16),
        one_hot(size, lambda row, col: frequency(col, row)),
        preferred_element_type=f32,
    )


def roll_kernel(size, span, slots, notes, far_rows, far_cols, *refs):
    pieces, (probe_out, near_side, far_side) = refs[:-3], refs[-3:]
    offset, _, slot, _ = notes_of(span, slots, notes)
    half = size // 2

    def moved(to, source):
        gap = to - source - offset
        return (gap == 0) | (gap == -size)

    down = one_hot(size, moved)
    across = one_hot(size, lambda row, col: moved(col, row))
    for c in range(2):
        near_side[c] = jnp.dot(
            far_rows[c], across[:, :half], preferred_element_type=f32
        ).astype(bf16)
        far_side[c] = jnp.dot(down[:half], far_cols[c], preferred_element_type=f32).astype(bf16)
    for c in range(2):
        done = 0
        for piece in pieces:
            turned = jnp.dot(down, piece[c], preferred_element_type=f32).astype(bf16)
            width = turned.shape[1]
            if len(pieces) == 2:
                at = pl.multiple_of(jnp.where(slot == done, 0, width), width)
                probe_out[c, :, pl.ds(at, width)] = turned
                done += 1
            else:
                probe_out[c, :, done : done + width] = turned
                done += width


def rolled(pieces, far_rows, far_cols, notes, size, span, slots):
    whole = pl.BlockSpec(memory_space=pltpu.VMEM)
    return pl.pallas_call(
        functools.partial(roll_kernel, size, span, slots),
        out_shape=[
            jax.ShapeDtypeStruct((2, size, size), bf16),
            jax.ShapeDtypeStruct((2, size, size // 2), bf16),
            jax.ShapeDtypeStruct((2, size // 2, size), bf16),
        ],
        in_specs=[whole] * (3 + len(pieces)),
        out_specs=[whole] * 3,
        compiler_params=pltpu.CompilerParams(vmem_limit_bytes=16 * 1024 * 1024),
        cost_estimate=pl.CostEstimate(
            flops=64 * size**3, bytes_accessed=24 * size * size, transcendentals=0
        ),
        name="rolled",
    )(notes, far_rows, far_cols, *pieces)


def tile_access(span, tile_rows, offset, core, mine, theirs):
    parts, _, _, _, width = mine.shape[1:]
    early = lax.broadcasted_iota(jnp.int32, (tile_rows, width), 0) < offset

    def place(k):
        return k // 2 if k % 2 == 0 else k // 2 + core

    def piece(k, h, s, c):
        source = mine if k % 2 == 0 else theirs
        return source[place(k), h, s, c].astype(f32)

    def patch(s, c):
        rows = []
        for k in range(span):
            blocks = [piece(k, h, s, c) for h in range(parts)]
            if k == 0:
                blocks = [jnp.where(early, piece(span, h, s, c), blocks[h]) for h in range(parts)]
            rows.append(jnp.concatenate(blocks, axis=1))
        return jnp.concatenate(rows, axis=0)

    return early, place, patch


def put_rows(rows_buf, pair):
    size = rows_buf.shape[1]
    for c in range(2):
        rows_buf[c * size : (c + 1) * size, :] = pair[c].astype(bf16)


def put_cols(cols_buf, pair):
    size = cols_buf.shape[0]
    for c in range(2):
        cols_buf[:, c * size : (c + 1) * size] = pair[c].astype(bf16)


def put_row_halves(rows_buf, first, second):
    half = rows_buf.shape[1] // 2
    for number, wave in enumerate((*first, *second)):
        rows_buf[number * half : (number + 1) * half, :] = wave.astype(bf16)


def put_col_halves(cols_buf, first, second):
    half = cols_buf.shape[0] // 2
    for number, wave in enumerate((*first, *second)):
        cols_buf[:, number * half : (number + 1) * half] = wave.astype(bf16)


def pair_of(ref):
    return ref[0].astype(f32), ref[1].astype(f32)


def parts_of(ref, rows, cols):
    return ref[0, rows, cols], ref[1, rows, cols]


def both(first, second, axis):
    return [jnp.concatenate([a, b], axis=axis) for a, b in zip(first, second)]


def plus(first, second):
    return [a + b for a, b in zip(first, second)]


def less(first, second):
    return [a - b for a, b in zip(first, second)]


def forth_kernel(
    size, span, slots, tile_rows, notes, mine, theirs, far_cols, near, probe, far_near,
    psi2, field, rows_buf, cols_buf,
):
    half = size // 2
    low, high, everything = slice(0, half), slice(half, size), slice(None)
    offset, live, _, core = notes_of(span, slots, notes)

    @pl.when(live)
    def _():
        _, _, patch = tile_access(span, tile_rows, offset, core, mine, theirs)
        near_parts = parts_of(near, everything, everything)
        pr, pi = pair_of(probe)
        ar, ai = patch(0, 0), patch(0, 1)
        put_rows(rows_buf, (pr * ar - pi * ai, pr * ai + pi * ar))
        put_cols(cols_buf, left(near_parts, False, rows_buf[...]))
        two = right(near_parts, False, cols_buf[...])
        psi2[0] = two[0].astype(bf16)
        psi2[1] = two[1].astype(bf16)
        wr, wi = pair_of(psi2)
        br, bi = patch(1, 0), patch(1, 1)
        wave_exit = (wr * br - wi * bi, wr * bi + wi * br)
        top, bottom = [x[low] for x in wave_exit], [x[high] for x in wave_exit]
        put_row_halves(rows_buf, plus(top, bottom), less(top, bottom))
        half2 = both(
            left(parts_of(far_near, low, everything), False, rows_buf[0:size, :]),
            left(parts_of(far_near, high, everything), False, rows_buf[size : 2 * size, :]),
            0,
        )
        top, bottom = [x[:, low] for x in half2], [x[:, high] for x in half2]
        put_col_halves(cols_buf, plus(top, bottom), less(top, bottom))
        for cols, source in ((low, cols_buf[:, 0:size]), (high, cols_buf[:, size : 2 * size])):
            fr, fi = right(parts_of(far_cols, low, cols), False, source)
            field[0, :, cols] = fr
            field[1, :, cols] = fi


def back_kernel(
    size, span, slots, tile_rows, notes, mine, theirs, far_rows, near, probe, far_far, psi2, field, *refs,
):
    measured, (keep, send, rows_buf, cols_buf) = refs[:-4], refs[-4:]
    offset, live, slot, core = notes_of(span, slots, notes)
    parts, _, _, _, width = keep.shape[1:]
    half = size // 2
    low, high, everything = slice(0, half), slice(half, size), slice(None)

    @pl.when(live)
    def _():
        early, place, patch = tile_access(span, tile_rows, offset, core, mine, theirs)

        def put_term(s, c, term):
            for k in range(span):
                for h in range(parts):
                    block = term[
                        k * tile_rows : (k + 1) * tile_rows, h * width : (h + 1) * width
                    ]
                    if k == 0:
                        keep[place(span), h, s, c] = jnp.where(early, block, 0.0).astype(bf16)
                        block = jnp.where(early, 0.0, block)
                    target = keep if k % 2 == 0 else send
                    target[place(k), h, s, c] = block.astype(bf16)

        amps = in_order(size, slot, measured, cols_buf.at[:, 0:size])
        chis = []
        for cols in (low, high):
            fr, fi = field[0, :, cols], field[1, :, cols]
            keeping = 1.0 - amps[:, cols] * lax.rsqrt(fr * fr + fi * fi + smooth)
            chis.append((fr * keeping, fi * keeping))
        put_col_halves(cols_buf, *chis)
        even = right(parts_of(far_rows, low, low), True, cols_buf[:, 0:size])
        odd = right(parts_of(far_rows, high, low), True, cols_buf[:, size : 2 * size])
        back1 = both(plus(even, odd), less(even, odd), 1)
        put_row_halves(rows_buf, [x[low] for x in back1], [x[high] for x in back1])
        even = left(parts_of(far_far, everything, low), True, rows_buf[0:size, :])
        odd = left(parts_of(far_far, everything, high), True, rows_buf[size : 2 * size, :])
        er, ei = both(plus(even, odd), less(even, odd), 0)
        br, bi = patch(1, 0), patch(1, 1)
        put_cols(cols_buf, (br * er + bi * ei, br * ei - bi * er))
        wr, wi = pair_of(psi2)
        put_term(1, 0, wr * er + wi * ei)
        put_term(1, 1, wr * ei - wi * er)
        near_parts = parts_of(near, everything, everything)
        put_rows(rows_buf, right(near_parts, True, cols_buf[...]))
        gr, gi = left(near_parts, True, rows_buf[...])
        pr, pi = pair_of(probe)
        put_term(0, 0, pr * gr + pi * gi)
        put_term(0, 1, pr * gi - pi * gr)
        send[(1 - core) * (span // 2)] = jnp.zeros(send.shape[1:], bf16)

    @pl.when(jnp.logical_not(live))
    def _():
        keep[...] = jnp.zeros(keep.shape, bf16)
        send[...] = jnp.zeros(send.shape, bf16)


def small_call(kernel, out_shape, scalars, values, name):
    inside = pl.BlockSpec(memory_space=pltpu.VMEM)
    return pl.pallas_call(
        kernel,
        out_shape=out_shape,
        in_specs=[pl.BlockSpec(memory_space=pltpu.SMEM)] * len(scalars) + [inside] * len(values),
        out_specs=jax.tree.map(lambda _: inside, out_shape),
        compiler_params=pltpu.CompilerParams(vmem_limit_bytes=12 * 1024 * 1024),
        cost_estimate=pl.CostEstimate(flops=0, bytes_accessed=1 << 20, transcendentals=0),
        name=name,
    )(*scalars, *values)


def placed(values, place_of, name):
    def kernel(*refs):
        for number, value in enumerate(refs[:-1]):
            refs[-1][place_of(number)] = value[...]

    shape = jax.ShapeDtypeStruct((len(values),) + values[0].shape, values[0].dtype)
    return small_call(kernel, shape, [], values, name)


def amplitude_messages(amplitudes, row_offsets, position_counts):
    slots, rows, size = amplitudes.shape

    def kernel(offsets, counts, amps, straight, crossed):
        slot = lax.axis_index("scan")
        straight[0:rows, :] = amps[slot].astype(bf16)
        crossed[...] = amps[1 - slot].astype(bf16)
        at = lax.broadcasted_iota(jnp.int32, (16, size), 1)
        notes = jnp.where(at == slots, counts[0].astype(f32), 0.0)
        for number in range(slots):
            notes = jnp.where(at == number, offsets[number].astype(f32), notes)
        straight[rows : rows + 16, :] = notes.astype(bf16)

    shapes = [jax.ShapeDtypeStruct((n, size), bf16) for n in (rows + 16, rows)]
    return small_call(kernel, shapes, [row_offsets, position_counts], [amplitudes], "messages")


def group(number):
    unit, flip = ((4, 0), (2, 1), (2, 2), (2, 3), (4, 4))[number]
    odd = lax.rem(lax.axis_index("tile") // unit, 2) == 1
    return jnp.where(odd, flip, 4 - flip)


def merged_messages(keep, got):
    def kernel(keep, got, *outs):
        for number, out in enumerate(outs):
            at = group(number)
            out[...] = (keep[at].astype(f32) + got[at].astype(f32)).astype(bf16)

    return small_call(kernel, [jax.ShapeDtypeStruct(keep.shape[1:], bf16)] * 5, [], [keep, got], "merge")


def merged_in_halves(keep, got):
    def kernel(keep, got, near_with, next_with, next_across, middle, half_own, half_away):
        def chunk(number, *half):
            at = (group(number), *half)
            return keep[at].astype(f32) + got[at].astype(f32)

        slot = lax.axis_index("scan")
        half_own[...] = chunk(3, slot)
        half_away[...] = chunk(3, 1 - slot).astype(bf16)
        for out, number in ((near_with, 1), (next_with, 0), (next_across, 4), (middle, 2)):
            out[...] = chunk(number).astype(bf16)

    whole = jax.ShapeDtypeStruct(keep.shape[1:], bf16)
    halves = [jax.ShapeDtypeStruct(keep.shape[2:], kind) for kind in (f32, bf16)]
    return small_call(kernel, [whole] * 4 + halves, [], [keep, got], "merge")


def summed(own, got):
    def kernel(own, got, out):
        out[...] = (own[...] + got[...].astype(f32)).astype(bf16)

    return small_call(kernel, jax.ShapeDtypeStruct(own.shape, bf16), [], [own, got], "near")


def halves_of_sum(values):
    def kernel(*refs):
        (own, away), slot = refs[-2:], lax.axis_index("scan")

        def half(h):
            return sum(ref[h].astype(f32) for ref in refs[:-2])

        own[...] = half(slot)
        away[...] = half(1 - slot).astype(bf16)

    shape = values[0].shape[1:]
    shapes = [jax.ShapeDtypeStruct(shape, f32), jax.ShapeDtypeStruct(shape, bf16)]
    return small_call(kernel, shapes, [], values, "sums")


def kernel_call(kernel, size, slots, tile_rows, name, out_shape, *inputs):
    inside = pl.BlockSpec(memory_space=pltpu.VMEM)
    return pl.pallas_call(
        functools.partial(kernel, size, size // tile_rows, slots, tile_rows),
        out_shape=out_shape,
        in_specs=[inside] * len(inputs),
        out_specs=[inside] * len(out_shape),
        scratch_shapes=[
            pltpu.VMEM((2 * size, size), bf16),
            pltpu.VMEM((size, 2 * size), bf16),
        ],
        compiler_params=pltpu.CompilerParams(vmem_limit_bytes=28 * 1024 * 1024),
        cost_estimate=pl.CostEstimate(
            flops=24 * size**3, bytes_accessed=size * size, transcendentals=0
        ),
        name=name,
    )(*inputs)


def shards(size, object_slab, probe_wave, amplitudes, row_offsets, position_counts):
    tile_rows = object_slab.shape[2]
    span = size // tile_rows
    count = lax.axis_size("tile")
    parts = lax.axis_size("scan")
    slots = amplitudes.shape[0]
    paired = parts == slots == 2
    ahead = span // 2
    swap = [(0, 1), (1, 0)]
    ahead_pairs = [(one, (one + ahead) % count) for one in range(count)]

    def brought(value):
        return lax.ppermute(value, "tile", ahead_pairs)

    def paired_with(value, unit):
        return lax.ppermute(value, "tile", [(one, one ^ unit) for one in range(count)])

    def paired_across(value, unit):
        pairs = []
        for one in range(count):
            step = unit if (one // unit) % 2 else -unit
            pairs.append((one, one + step if unit <= one < count - unit else one ^ 1))
        return lax.ppermute(value, "tile", pairs)

    own = object_slab.astype(bf16)
    width = own.shape[-1]
    if paired:
        beside = lax.ppermute(own, "scan", swap)
        beside, probe_wave = lax.optimization_barrier((beside, probe_wave))
        whole = placed([own, beside], lambda n: jnp.bitwise_xor(lax.axis_index("scan"), n), "halves")
        probe_pieces = [probe_wave, lax.ppermute(probe_wave, "scan", swap)]
        straight, crossed = amplitude_messages(amplitudes, row_offsets, position_counts)
        straight = brought(straight)
        crossed = lax.ppermute(
            crossed,
            ("tile", "scan"),
            [(2 * a + x, 2 * b + 1 - x) for a, b in ahead_pairs for x in range(2)],
        )
        notes = straight
        measured = [straight, crossed]
    else:
        whole = lax.all_gather(own, "scan")
        every = lax.all_gather(probe_wave, "scan")
        probe_pieces = [every[number] for number in range(parts)]
        notes = jnp.concatenate([row_offsets, position_counts]).astype(bf16)
        notes = brought(jnp.pad(notes[None], ((0, 15), (0, size - slots - 1))))
        every = lax.all_gather(brought(amplitudes.astype(bf16)), "scan")
        slot = lax.axis_index("scan")
        measured = [every[:, jnp.minimum(slot, slots - 1)].reshape((size, size))]
    next_across, next_with = paired_across(whole, 4), paired_with(whole, 4)
    near_across, near_with = paired_across(whole, 2), paired_with(whole, 2)
    middle, probe_pieces, notes = lax.optimization_barrier((whole, probe_pieces, notes))
    far_rows, far_cols, near = tables(size)
    turned, far_near, far_far = rolled(
        probe_pieces, far_rows, far_cols, notes, size, span, slots
    )
    arrived = [next_with, near_with, middle, near_across, next_across]
    mine = placed(arrived, group, "groups")
    theirs = paired_with(mine, 1)
    shape = jax.ShapeDtypeStruct
    psi2, field = kernel_call(
        forth_kernel, size, slots, tile_rows, "forth",
        [shape((2, size, size), bf16), shape((2, size, size), f32)],
        notes, mine, theirs, far_cols, near, turned, far_near,
    )
    measured[-1], field = lax.optimization_barrier((measured[-1], field))
    keep, send = kernel_call(
        back_kernel, size, slots, tile_rows, "back",
        [shape((len(arrived), parts, 2, 2, tile_rows, width), bf16)] * 2,
        notes, mine, theirs, far_rows, near, turned, far_far, psi2, field, *measured,
    )
    got = paired_with(send, 1)
    if paired:
        near_with, next_with, next_across, middle, half_own, half_away = merged_in_halves(keep, got)
        half_got = lax.ppermute(half_away, "scan", swap)
        message = summed(half_own, half_got)
        middle, message = lax.optimization_barrier((middle, message))
        kept, away = halves_of_sum(
            [
                paired_with(near_with, 2),
                paired_with(next_with, 4),
                paired_across(next_across, 4),
                middle,
            ]
        )
        for value in (lax.ppermute(away, "scan", swap), paired_across(message, 2)):
            kept = kept + value.astype(f32)
        return kept
    next_with, near_with, middle, near_across, next_across = merged_messages(keep, got)
    returned = [
        paired_with(near_with, 2),
        paired_across(near_across, 2),
        paired_with(next_with, 4),
        paired_across(next_across, 4),
        middle,
    ]
    total = sum(value.astype(f32) for value in returned)
    return lax.psum_scatter(total, "scan", scatter_dimension=0, tiled=False)


def solution(mesh):
    in_specs = (
        P(None, None, "tile", "scan"),
        P(None, None, "scan"),
        P("tile", "scan", None),
        P("tile"),
        P("tile"),
    )
    out_specs = P(None, None, "tile", "scan")

    def run(object_slab, *rest):
        return jax.shard_map(
            functools.partial(shards, object_slab.shape[3]),
            mesh=mesh, in_specs=in_specs, out_specs=out_specs, check_vma=False,
        )(object_slab, *rest)

    return run
```

```python
import functools
import math

import jax
import jax.numpy as jnp
import ml_dtypes
import numpy as np
from jax import lax
from jax.experimental import pallas as pl
from jax.experimental.pallas import tpu as pltpu
from jax.sharding import PartitionSpec as P

fresnel = 0.5
smooth = 1.0
bf16 = jnp.bfloat16
f32 = jnp.float32


def tables(size):
    index = np.arange(size)
    angles = 2.0 * np.pi / size * (index[:, None] * index[None, :] % size)
    base = np.exp(1j * angles)
    far = np.conj(base) / math.sqrt(size)
    centred = np.where(index < size // 2, index, index - size).astype(np.float64)
    kernel = np.exp(-1j * np.pi * fresnel / size * centred * centred)
    near = (base * kernel[None, :]) @ np.conj(base).T / size

    def parts(table):
        stacked = np.stack([table.real, table.imag])
        return jnp.asarray(stacked.astype(ml_dtypes.bfloat16))

    order = np.concatenate([index[0::2], index[1::2]])
    return parts(far[order]), parts(far[:, order]), parts(near)


def three(table, conjugate):
    real, imag = table
    return (real, -imag, imag) if conjugate else (real, imag, -imag)


def left(table, conjugate, wave):
    real, plus, minus = three(table, conjugate)
    top = jnp.concatenate([real, minus], axis=1)
    bottom = jnp.concatenate([plus, real], axis=1)
    return (
        jnp.dot(top, wave, preferred_element_type=f32),
        jnp.dot(bottom, wave, preferred_element_type=f32),
    )


def right(table, conjugate, wave):
    real, plus, minus = three(table, conjugate)
    real_side = jnp.concatenate([real, minus], axis=0)
    imag_side = jnp.concatenate([plus, real], axis=0)
    return (
        jnp.dot(wave, real_side, preferred_element_type=f32),
        jnp.dot(wave, imag_side, preferred_element_type=f32),
    )


def one_hot(size, hit):
    row = lax.broadcasted_iota(jnp.int32, (size, size), 0)
    col = lax.broadcasted_iota(jnp.int32, (size, size), 1)
    return jnp.where(hit(row, col), 1.0, 0.0).astype(bf16)


def notes_of(span, slots, ref):
    rows = ref.shape[0]
    values = ref[rows - 16 : rows, 0:128].astype(f32)
    row = lax.broadcasted_iota(jnp.int32, values.shape, 0)
    col = lax.broadcasted_iota(jnp.int32, values.shape, 1)

    def note(at):
        return jnp.sum(jnp.where((row == 0) & (col == at), values, 0.0)).astype(jnp.int32)

    tile, slot = lax.axis_index("tile"), lax.axis_index("scan")
    ahead = span // 2
    home = (tile >= ahead) & (tile < lax.axis_size("tile") - ahead)
    live = home & (slot < note(slots))
    return note(jnp.minimum(slot, slots - 1)), live, slot, lax.rem(tile, 2)


def in_order(size, slot, measured, amps):
    half = size // 2
    for number, piece in enumerate(measured):
        rows = size // len(measured)
        at = pl.multiple_of(jnp.where(slot == number, 0, size - rows), rows)
        amps[pl.ds(at, rows), :] = piece[0:rows, :]

    def frequency(place, natural):
        return natural == jnp.where(place < half, 2 * place, 2 * (place - half) + 1)

    rows_first = jnp.dot(one_hot(size, frequency), amps[...], preferred_element_type=f32)
    return jnp.dot(
        rows_first.astype(bf16),
        one_hot(size, lambda row, col: frequency(col, row)),
        preferred_element_type=f32,
    )


def roll_kernel(size, span, slots, notes, far_rows, far_cols, *refs):
    pieces, (probe_out, near_side, far_side) = refs[:-3], refs[-3:]
    offset, _, slot, _ = notes_of(span, slots, notes)
    half = size // 2

    def moved(to, source):
        gap = to - source - offset
        return (gap == 0) | (gap == -size)

    down = one_hot(size, moved)
    across = one_hot(size, lambda row, col: moved(col, row))
    for c in range(2):
        near_side[c] = jnp.dot(
            far_rows[c], across[:, :half], preferred_element_type=f32
        ).astype(bf16)
        far_side[c] = jnp.dot(down[:half], far_cols[c], preferred_element_type=f32).astype(bf16)
    for c in range(2):
        done = 0
        for piece in pieces:
            turned = jnp.dot(down, piece[c], preferred_element_type=f32).astype(bf16)
            width = turned.shape[1]
            if len(pieces) == 2:
                at = pl.multiple_of(jnp.where(slot == done, 0, width), width)
                probe_out[c, :, pl.ds(at, width)] = turned
                done += 1
            else:
                probe_out[c, :, done : done + width] = turned
                done += width


def rolled(pieces, far_rows, far_cols, notes, size, span, slots):
    whole = pl.BlockSpec(memory_space=pltpu.VMEM)
    return pl.pallas_call(
        functools.partial(roll_kernel, size, span, slots),
        out_shape=[
            jax.ShapeDtypeStruct((2, size, size), bf16),
            jax.ShapeDtypeStruct((2, size, size // 2), bf16),
            jax.ShapeDtypeStruct((2, size // 2, size), bf16),
        ],
        in_specs=[whole] * (3 + len(pieces)),
        out_specs=[whole] * 3,
        compiler_params=pltpu.CompilerParams(vmem_limit_bytes=16 * 1024 * 1024),
        cost_estimate=pl.CostEstimate(
            flops=64 * size**3, bytes_accessed=24 * size * size, transcendentals=0
        ),
        name="rolled",
    )(notes, far_rows, far_cols, *pieces)


def tile_access(span, tile_rows, offset, core, mine, theirs):
    parts, _, _, _, width = mine.shape[1:]
    early = lax.broadcasted_iota(jnp.int32, (tile_rows, width), 0) < offset

    def place(k):
        return k // 2 if k % 2 == 0 else k // 2 + core

    def piece(k, h, s, c):
        source = mine if k % 2 == 0 else theirs
        return source[place(k), h, s, c].astype(f32)

    def patch(s, c):
        rows = []
        for k in range(span):
            blocks = [piece(k, h, s, c) for h in range(parts)]
            if k == 0:
                blocks = [jnp.where(early, piece(span, h, s, c), blocks[h]) for h in range(parts)]
            rows.append(jnp.concatenate(blocks, axis=1))
        return jnp.concatenate(rows, axis=0)

    return early, place, patch


def put_rows(rows_buf, pair):
    size = rows_buf.shape[1]
    for c in range(2):
        rows_buf[c * size : (c + 1) * size, :] = pair[c].astype(bf16)


def put_cols(cols_buf, pair):
    size = cols_buf.shape[0]
    for c in range(2):
        cols_buf[:, c * size : (c + 1) * size] = pair[c].astype(bf16)


def put_row_halves(rows_buf, first, second):
    half = rows_buf.shape[1] // 2
    for number, wave in enumerate((*first, *second)):
        rows_buf[number * half : (number + 1) * half, :] = wave.astype(bf16)


def put_col_halves(cols_buf, first, second):
    half = cols_buf.shape[0] // 2
    for number, wave in enumerate((*first, *second)):
        cols_buf[:, number * half : (number + 1) * half] = wave.astype(bf16)


def pair_of(ref):
    return ref[0].astype(f32), ref[1].astype(f32)


def parts_of(ref, rows, cols):
    return ref[0, rows, cols], ref[1, rows, cols]


def both(first, second, axis):
    return [jnp.concatenate([a, b], axis=axis) for a, b in zip(first, second)]


def plus(first, second):
    return [a + b for a, b in zip(first, second)]


def less(first, second):
    return [a - b for a, b in zip(first, second)]


def forth_kernel(
    size, span, slots, tile_rows, notes, mine, theirs, far_cols, near, probe, far_near,
    psi2, field, rows_buf, cols_buf,
):
    half = size // 2
    low, high, everything = slice(0, half), slice(half, size), slice(None)
    offset, live, _, core = notes_of(span, slots, notes)

    @pl.when(live)
    def _():
        _, _, patch = tile_access(span, tile_rows, offset, core, mine, theirs)
        near_parts = parts_of(near, everything, everything)
        pr, pi = pair_of(probe)
        ar, ai = patch(0, 0), patch(0, 1)
        put_rows(rows_buf, (pr * ar - pi * ai, pr * ai + pi * ar))
        put_cols(cols_buf, left(near_parts, False, rows_buf[...]))
        two = right(near_parts, False, cols_buf[...])
        psi2[0] = two[0].astype(bf16)
        psi2[1] = two[1].astype(bf16)
        wr, wi = pair_of(psi2)
        br, bi = patch(1, 0), patch(1, 1)
        wave_exit = (wr * br - wi * bi, wr * bi + wi * br)
        top, bottom = [x[low] for x in wave_exit], [x[high] for x in wave_exit]
        put_row_halves(rows_buf, plus(top, bottom), less(top, bottom))
        half2 = both(
            left(parts_of(far_near, low, everything), False, rows_buf[0:size, :]),
            left(parts_of(far_near, high, everything), False, rows_buf[size : 2 * size, :]),
            0,
        )
        top, bottom = [x[:, low] for x in half2], [x[:, high] for x in half2]
        put_col_halves(cols_buf, plus(top, bottom), less(top, bottom))
        for cols, source in ((low, cols_buf[:, 0:size]), (high, cols_buf[:, size : 2 * size])):
            fr, fi = right(parts_of(far_cols, low, cols), False, source)
            field[0, :, cols] = fr
            field[1, :, cols] = fi


def back_kernel(
    size, span, slots, tile_rows, notes, mine, theirs, far_rows, near, probe, far_far, psi2, field, *refs,
):
    measured, (keep, send, rows_buf, cols_buf) = refs[:-4], refs[-4:]
    offset, live, slot, core = notes_of(span, slots, notes)
    parts, _, _, _, width = keep.shape[1:]
    half = size // 2
    low, high, everything = slice(0, half), slice(half, size), slice(None)

    @pl.when(live)
    def _():
        early, place, patch = tile_access(span, tile_rows, offset, core, mine, theirs)

        def put_term(s, c, term):
            for k in range(span):
                for h in range(parts):
                    block = term[
                        k * tile_rows : (k + 1) * tile_rows, h * width : (h + 1) * width
                    ]
                    if k == 0:
                        keep[place(span), h, s, c] = jnp.where(early, block, 0.0).astype(bf16)
                        block = jnp.where(early, 0.0, block)
                    target = keep if k % 2 == 0 else send
                    target[place(k), h, s, c] = block.astype(bf16)

        amps = in_order(size, slot, measured, cols_buf.at[:, 0:size])
        chis = []
        for cols in (low, high):
            fr, fi = field[0, :, cols], field[1, :, cols]
            keeping = 1.0 - amps[:, cols] * lax.rsqrt(fr * fr + fi * fi + smooth)
            chis.append((fr * keeping, fi * keeping))
        put_col_halves(cols_buf, *chis)
        even = right(parts_of(far_rows, low, low), True, cols_buf[:, 0:size])
        odd = right(parts_of(far_rows, high, low), True, cols_buf[:, size : 2 * size])
        back1 = both(plus(even, odd), less(even, odd), 1)
        put_row_halves(rows_buf, [x[low] for x in back1], [x[high] for x in back1])
        even = left(parts_of(far_far, everything, low), True, rows_buf[0:size, :])
        odd = left(parts_of(far_far, everything, high), True, rows_buf[size : 2 * size, :])
        er, ei = both(plus(even, odd), less(even, odd), 0)
        br, bi = patch(1, 0), patch(1, 1)
        put_cols(cols_buf, (br * er + bi * ei, br * ei - bi * er))
        wr, wi = pair_of(psi2)
        put_term(1, 0, wr * er + wi * ei)
        put_term(1, 1, wr * ei - wi * er)
        near_parts = parts_of(near, everything, everything)
        put_rows(rows_buf, right(near_parts, True, cols_buf[...]))
        gr, gi = left(near_parts, True, rows_buf[...])
        pr, pi = pair_of(probe)
        put_term(0, 0, pr * gr + pi * gi)
        put_term(0, 1, pr * gi - pi * gr)
        send[(1 - core) * (span // 2)] = jnp.zeros(send.shape[1:], bf16)

    @pl.when(jnp.logical_not(live))
    def _():
        keep[...] = jnp.zeros(keep.shape, bf16)
        send[...] = jnp.zeros(send.shape, bf16)


def small_call(kernel, out_shape, scalars, values, name):
    inside = pl.BlockSpec(memory_space=pltpu.VMEM)
    return pl.pallas_call(
        kernel,
        out_shape=out_shape,
        in_specs=[pl.BlockSpec(memory_space=pltpu.SMEM)] * len(scalars) + [inside] * len(values),
        out_specs=jax.tree.map(lambda _: inside, out_shape),
        compiler_params=pltpu.CompilerParams(vmem_limit_bytes=12 * 1024 * 1024),
        cost_estimate=pl.CostEstimate(flops=0, bytes_accessed=1 << 20, transcendentals=0),
        name=name,
    )(*scalars, *values)


def placed(values, place_of, name):
    def kernel(*refs):
        for number, value in enumerate(refs[:-1]):
            refs[-1][place_of(number)] = value[...]

    shape = jax.ShapeDtypeStruct((len(values),) + values[0].shape, values[0].dtype)
    return small_call(kernel, shape, [], values, name)


def placed_groups(next_with, near_with, middle, next_across, own_half, other_half):
    def kernel(*refs):
        out, slot = refs[-1], lax.axis_index("scan")
        for number, value in zip((0, 1, 2, 4), refs[:4]):
            out[group(number)] = value[...]
        out[group(3), slot] = refs[4][...]
        out[group(3), 1 - slot] = refs[5][...]

    values = [next_with, near_with, middle, next_across, own_half, other_half]
    return small_call(kernel, jax.ShapeDtypeStruct((5,) + middle.shape, bf16), [], values, "groups")


def amplitude_messages(amplitudes, row_offsets, position_counts):
    slots, rows, size = amplitudes.shape

    def kernel(offsets, counts, amps, straight, crossed):
        slot = lax.axis_index("scan")
        straight[0:rows, :] = amps[slot].astype(bf16)
        crossed[...] = amps[1 - slot].astype(bf16)
        at = lax.broadcasted_iota(jnp.int32, (16, size), 1)
        notes = jnp.where(at == slots, counts[0].astype(f32), 0.0)
        for number in range(slots):
            notes = jnp.where(at == number, offsets[number].astype(f32), notes)
        straight[rows : rows + 16, :] = notes.astype(bf16)

    shapes = [jax.ShapeDtypeStruct((n, size), bf16) for n in (rows + 16, rows)]
    return small_call(kernel, shapes, [row_offsets, position_counts], [amplitudes], "messages")


def group(number):
    unit, flip = ((4, 0), (2, 1), (2, 2), (2, 3), (4, 4))[number]
    odd = lax.rem(lax.axis_index("tile") // unit, 2) == 1
    return jnp.where(odd, flip, 4 - flip)


def merged_messages(keep, got):
    def kernel(keep, got, *outs):
        for number, out in enumerate(outs):
            at = group(number)
            out[...] = (keep[at].astype(f32) + got[at].astype(f32)).astype(bf16)

    return small_call(kernel, [jax.ShapeDtypeStruct(keep.shape[1:], bf16)] * 5, [], [keep, got], "merge")


def merged_in_halves(keep, got):
    def kernel(keep, got, near_with, next_with, next_across, middle, half_own, half_away):
        def chunk(number, *half):
            at = (group(number), *half)
            return keep[at].astype(f32) + got[at].astype(f32)

        slot = lax.axis_index("scan")
        half_own[...] = chunk(3, slot)
        half_away[...] = chunk(3, 1 - slot).astype(bf16)
        for out, number in ((near_with, 1), (next_with, 0), (next_across, 4), (middle, 2)):
            out[...] = chunk(number).astype(bf16)

    whole = jax.ShapeDtypeStruct(keep.shape[1:], bf16)
    halves = [jax.ShapeDtypeStruct(keep.shape[2:], kind) for kind in (f32, bf16)]
    return small_call(kernel, [whole] * 4 + halves, [], [keep, got], "merge")


def summed(own, got):
    def kernel(own, got, out):
        out[...] = (own[...] + got[...].astype(f32)).astype(bf16)

    return small_call(kernel, jax.ShapeDtypeStruct(own.shape, bf16), [], [own, got], "near")


def halves_of_sum(values):
    def kernel(*refs):
        (own, away), slot = refs[-2:], lax.axis_index("scan")

        def half(h):
            return sum(ref[h].astype(f32) for ref in refs[:-2])

        own[...] = half(slot)
        away[...] = half(1 - slot).astype(bf16)

    shape = values[0].shape[1:]
    shapes = [jax.ShapeDtypeStruct(shape, f32), jax.ShapeDtypeStruct(shape, bf16)]
    return small_call(kernel, shapes, [], values, "sums")


def kernel_call(kernel, size, slots, tile_rows, name, out_shape, *inputs):
    inside = pl.BlockSpec(memory_space=pltpu.VMEM)
    return pl.pallas_call(
        functools.partial(kernel, size, size // tile_rows, slots, tile_rows),
        out_shape=out_shape,
        in_specs=[inside] * len(inputs),
        out_specs=[inside] * len(out_shape),
        scratch_shapes=[
            pltpu.VMEM((2 * size, size), bf16),
            pltpu.VMEM((size, 2 * size), bf16),
        ],
        compiler_params=pltpu.CompilerParams(vmem_limit_bytes=28 * 1024 * 1024),
        cost_estimate=pl.CostEstimate(
            flops=24 * size**3, bytes_accessed=size * size, transcendentals=0
        ),
        name=name,
    )(*inputs)


def shards(size, object_slab, probe_wave, amplitudes, row_offsets, position_counts):
    tile_rows = object_slab.shape[2]
    span = size // tile_rows
    count = lax.axis_size("tile")
    parts = lax.axis_size("scan")
    slots = amplitudes.shape[0]
    paired = parts == slots == 2
    ahead = span // 2
    swap = [(0, 1), (1, 0)]
    ahead_pairs = [(one, (one + ahead) % count) for one in range(count)]

    def brought(value):
        return lax.ppermute(value, "tile", ahead_pairs)

    def paired_with(value, unit):
        return lax.ppermute(value, "tile", [(one, one ^ unit) for one in range(count)])

    def paired_across(value, unit):
        pairs = []
        for one in range(count):
            step = unit if (one // unit) % 2 else -unit
            pairs.append((one, one + step if unit <= one < count - unit else one ^ 1))
        return lax.ppermute(value, "tile", pairs)

    own = object_slab.astype(bf16)
    width = own.shape[-1]
    if paired:
        beside = lax.ppermute(own, "scan", swap)
        straight, crossed = amplitude_messages(amplitudes, row_offsets, position_counts)
        beside, probe_wave, own_late, straight = lax.optimization_barrier(
            (beside, probe_wave, own, straight)
        )
        whole = placed([own, beside], lambda n: jnp.bitwise_xor(lax.axis_index("scan"), n), "halves")
        probe_pieces = [probe_wave, lax.ppermute(probe_wave, "scan", swap)]
        straight = brought(straight)
        crossed = lax.ppermute(
            crossed,
            ("tile", "scan"),
            [(2 * a + x, 2 * b + 1 - x) for a, b in ahead_pairs for x in range(2)],
        )
        notes = straight
        measured = [straight, crossed]
    else:
        whole = lax.all_gather(own, "scan")
        every = lax.all_gather(probe_wave, "scan")
        probe_pieces = [every[number] for number in range(parts)]
        notes = jnp.concatenate([row_offsets, position_counts]).astype(bf16)
        notes = brought(jnp.pad(notes[None], ((0, 15), (0, size - slots - 1))))
        every = lax.all_gather(brought(amplitudes.astype(bf16)), "scan")
        slot = lax.axis_index("scan")
        measured = [every[:, jnp.minimum(slot, slots - 1)].reshape((size, size))]
    next_across, next_with = paired_across(whole, 4), paired_with(whole, 4)
    near_with = paired_with(whole, 2)
    near_across = paired_across(own_late if paired else whole, 2)
    if paired:
        near_beside = lax.ppermute(near_across, "scan", swap)
    middle, probe_pieces, notes = lax.optimization_barrier((whole, probe_pieces, notes))
    far_rows, far_cols, near = tables(size)
    turned, far_near, far_far = rolled(
        probe_pieces, far_rows, far_cols, notes, size, span, slots
    )
    if paired:
        mine = placed_groups(
            next_with, near_with, middle, next_across, near_across, near_beside
        )
    else:
        mine = placed([next_with, near_with, middle, near_across, next_across], group, "groups")
    theirs = paired_with(mine, 1)
    shape = jax.ShapeDtypeStruct
    psi2, field = kernel_call(
        forth_kernel, size, slots, tile_rows, "forth",
        [shape((2, size, size), bf16), shape((2, size, size), f32)],
        notes, mine, theirs, far_cols, near, turned, far_near,
    )
    measured[-1], field = lax.optimization_barrier((measured[-1], field))
    keep, send = kernel_call(
        back_kernel, size, slots, tile_rows, "back",
        [shape((5, parts, 2, 2, tile_rows, width), bf16)] * 2,
        notes, mine, theirs, far_rows, near, turned, far_far, psi2, field, *measured,
    )
    got = paired_with(send, 1)
    if paired:
        near_with, next_with, next_across, middle, half_own, half_away = merged_in_halves(keep, got)
        half_got = lax.ppermute(half_away, "scan", swap)
        message = summed(half_own, half_got)
        middle, message = lax.optimization_barrier((middle, message))
        kept, away = halves_of_sum(
            [
                paired_with(near_with, 2),
                paired_with(next_with, 4),
                paired_across(next_across, 4),
                middle,
            ]
        )
        for value in (lax.ppermute(away, "scan", swap), paired_across(message, 2)):
            kept = kept + value.astype(f32)
        return kept
    next_with, near_with, middle, near_across, next_across = merged_messages(keep, got)
    returned = [
        paired_with(near_with, 2),
        paired_across(near_across, 2),
        paired_with(next_with, 4),
        paired_across(next_across, 4),
        middle,
    ]
    total = sum(value.astype(f32) for value in returned)
    return lax.psum_scatter(total, "scan", scatter_dimension=0, tiled=False)


def solution(mesh):
    in_specs = (
        P(None, None, "tile", "scan"),
        P(None, None, "scan"),
        P("tile", "scan", None),
        P("tile"),
        P("tile"),
    )
    out_specs = P(None, None, "tile", "scan")

    def run(object_slab, *rest):
        return jax.shard_map(
            functools.partial(shards, object_slab.shape[3]),
            mesh=mesh, in_specs=in_specs, out_specs=out_specs, check_vma=False,
        )(object_slab, *rest)

    return run
```

```python
import functools
import math

import jax
import jax.numpy as jnp
import ml_dtypes
import numpy as np
from jax import lax
from jax.experimental import pallas as pl
from jax.experimental.pallas import tpu as pltpu
from jax.sharding import PartitionSpec as P

fresnel = 0.5
smooth = 1.0
bf16 = jnp.bfloat16
f32 = jnp.float32


def tables(size):
    index = np.arange(size)
    angles = 2.0 * np.pi / size * (index[:, None] * index[None, :] % size)
    base = np.exp(1j * angles)
    far = np.conj(base) / math.sqrt(size)
    centred = np.where(index < size // 2, index, index - size).astype(np.float64)
    kernel = np.exp(-1j * np.pi * fresnel / size * centred * centred)
    near = (base * kernel[None, :]) @ np.conj(base).T / size

    def parts(table):
        stacked = np.stack([table.real, table.imag])
        return jnp.asarray(stacked.astype(ml_dtypes.bfloat16))

    order = np.concatenate([index[0::2], index[1::2]])
    return parts(far[order]), parts(far[:, order]), parts(near)


def three(table, conjugate):
    real, imag = table
    return (real, -imag, imag) if conjugate else (real, imag, -imag)


def left(table, conjugate, wave):
    real, plus, minus = three(table, conjugate)
    top = jnp.concatenate([real, minus], axis=1)
    bottom = jnp.concatenate([plus, real], axis=1)
    return (
        jnp.dot(top, wave, preferred_element_type=f32),
        jnp.dot(bottom, wave, preferred_element_type=f32),
    )


def right(table, conjugate, wave):
    real, plus, minus = three(table, conjugate)
    real_side = jnp.concatenate([real, minus], axis=0)
    imag_side = jnp.concatenate([plus, real], axis=0)
    return (
        jnp.dot(wave, real_side, preferred_element_type=f32),
        jnp.dot(wave, imag_side, preferred_element_type=f32),
    )


def one_hot(size, hit):
    row = lax.broadcasted_iota(jnp.int32, (size, size), 0)
    col = lax.broadcasted_iota(jnp.int32, (size, size), 1)
    return jnp.where(hit(row, col), 1.0, 0.0).astype(bf16)


def notes_of(span, slots, ref):
    rows = ref.shape[0]
    values = ref[rows - 16 : rows, 0:128].astype(f32)
    row = lax.broadcasted_iota(jnp.int32, values.shape, 0)
    col = lax.broadcasted_iota(jnp.int32, values.shape, 1)

    def note(at):
        return jnp.sum(jnp.where((row == 0) & (col == at), values, 0.0)).astype(jnp.int32)

    tile, slot = lax.axis_index("tile"), lax.axis_index("scan")
    ahead = span // 2
    home = (tile >= ahead) & (tile < lax.axis_size("tile") - ahead)
    live = home & (slot < note(slots))
    return note(jnp.minimum(slot, slots - 1)), live, slot, lax.rem(tile, 2)


def in_order(size, slot, measured, amps):
    half = size // 2
    for number, piece in enumerate(measured):
        rows = size // len(measured)
        at = pl.multiple_of(jnp.where(slot == number, 0, size - rows), rows)
        amps[pl.ds(at, rows), :] = piece[0:rows, :]

    def frequency(place, natural):
        return natural == jnp.where(place < half, 2 * place, 2 * (place - half) + 1)

    rows_first = jnp.dot(one_hot(size, frequency), amps[...], preferred_element_type=f32)
    return jnp.dot(
        rows_first.astype(bf16),
        one_hot(size, lambda row, col: frequency(col, row)),
        preferred_element_type=f32,
    )


def roll_kernel(size, span, slots, notes, far_rows, far_cols, *refs):
    pieces, (probe_out, near_side, far_side) = refs[:-3], refs[-3:]
    offset, _, slot, _ = notes_of(span, slots, notes)
    half = size // 2

    def moved(to, source):
        gap = to - source - offset
        return (gap == 0) | (gap == -size)

    down = one_hot(size, moved)
    across = one_hot(size, lambda row, col: moved(col, row))
    for c in range(2):
        near_side[c] = jnp.dot(
            far_rows[c], across[:, :half], preferred_element_type=f32
        ).astype(bf16)
        far_side[c] = jnp.dot(down[:half], far_cols[c], preferred_element_type=f32).astype(bf16)
    for c in range(2):
        done = 0
        for piece in pieces:
            turned = jnp.dot(down, piece[c], preferred_element_type=f32).astype(bf16)
            width = turned.shape[1]
            if len(pieces) == 2:
                at = pl.multiple_of(jnp.where(slot == done, 0, width), width)
                probe_out[c, :, pl.ds(at, width)] = turned
                done += 1
            else:
                probe_out[c, :, done : done + width] = turned
                done += width


def rolled(pieces, far_rows, far_cols, notes, size, span, slots):
    whole = pl.BlockSpec(memory_space=pltpu.VMEM)
    return pl.pallas_call(
        functools.partial(roll_kernel, size, span, slots),
        out_shape=[
            jax.ShapeDtypeStruct((2, size, size), bf16),
            jax.ShapeDtypeStruct((2, size, size // 2), bf16),
            jax.ShapeDtypeStruct((2, size // 2, size), bf16),
        ],
        in_specs=[whole] * (3 + len(pieces)),
        out_specs=[whole] * 3,
        compiler_params=pltpu.CompilerParams(vmem_limit_bytes=16 * 1024 * 1024),
        cost_estimate=pl.CostEstimate(
            flops=64 * size**3, bytes_accessed=24 * size * size, transcendentals=0
        ),
        name="rolled",
    )(notes, far_rows, far_cols, *pieces)


def tile_access(span, tile_rows, offset, core, mine, theirs):
    parts, _, _, _, width = mine.shape[1:]
    early = lax.broadcasted_iota(jnp.int32, (tile_rows, width), 0) < offset

    def place(k):
        return k // 2 if k % 2 == 0 else k // 2 + core

    def piece(k, h, s, c):
        source = mine if k % 2 == 0 else theirs
        return source[place(k), h, s, c].astype(f32)

    def patch(s, c):
        rows = []
        for k in range(span):
            blocks = [piece(k, h, s, c) for h in range(parts)]
            if k == 0:
                blocks = [jnp.where(early, piece(span, h, s, c), blocks[h]) for h in range(parts)]
            rows.append(jnp.concatenate(blocks, axis=1))
        return jnp.concatenate(rows, axis=0)

    return early, place, patch


def put_rows(rows_buf, pair):
    size = rows_buf.shape[1]
    for c in range(2):
        rows_buf[c * size : (c + 1) * size, :] = pair[c].astype(bf16)


def put_cols(cols_buf, pair):
    size = cols_buf.shape[0]
    for c in range(2):
        cols_buf[:, c * size : (c + 1) * size] = pair[c].astype(bf16)


def put_row_halves(rows_buf, first, second):
    half = rows_buf.shape[1] // 2
    for number, wave in enumerate((*first, *second)):
        rows_buf[number * half : (number + 1) * half, :] = wave.astype(bf16)


def put_col_halves(cols_buf, first, second):
    half = cols_buf.shape[0] // 2
    for number, wave in enumerate((*first, *second)):
        cols_buf[:, number * half : (number + 1) * half] = wave.astype(bf16)


def pair_of(ref):
    return ref[0].astype(f32), ref[1].astype(f32)


def parts_of(ref, rows, cols):
    return ref[0, rows, cols], ref[1, rows, cols]


def both(first, second, axis):
    return [jnp.concatenate([a, b], axis=axis) for a, b in zip(first, second)]


def plus(first, second):
    return [a + b for a, b in zip(first, second)]


def less(first, second):
    return [a - b for a, b in zip(first, second)]


def forth_kernel(
    size, span, slots, tile_rows, notes, mine, theirs, far_cols, near, probe, far_near,
    psi2, field, rows_buf, cols_buf,
):
    half = size // 2
    low, high, everything = slice(0, half), slice(half, size), slice(None)
    offset, live, _, core = notes_of(span, slots, notes)

    @pl.when(live)
    def _():
        _, _, patch = tile_access(span, tile_rows, offset, core, mine, theirs)
        near_parts = parts_of(near, everything, everything)
        pr, pi = pair_of(probe)
        ar, ai = patch(0, 0), patch(0, 1)
        put_rows(rows_buf, (pr * ar - pi * ai, pr * ai + pi * ar))
        put_cols(cols_buf, left(near_parts, False, rows_buf[...]))
        two = right(near_parts, False, cols_buf[...])
        psi2[0] = two[0].astype(bf16)
        psi2[1] = two[1].astype(bf16)
        wr, wi = pair_of(psi2)
        br, bi = patch(1, 0), patch(1, 1)
        wave_exit = (wr * br - wi * bi, wr * bi + wi * br)
        top, bottom = [x[low] for x in wave_exit], [x[high] for x in wave_exit]
        put_row_halves(rows_buf, plus(top, bottom), less(top, bottom))
        half2 = both(
            left(parts_of(far_near, low, everything), False, rows_buf[0:size, :]),
            left(parts_of(far_near, high, everything), False, rows_buf[size : 2 * size, :]),
            0,
        )
        top, bottom = [x[:, low] for x in half2], [x[:, high] for x in half2]
        put_col_halves(cols_buf, plus(top, bottom), less(top, bottom))
        for cols, source in ((low, cols_buf[:, 0:size]), (high, cols_buf[:, size : 2 * size])):
            fr, fi = right(parts_of(far_cols, low, cols), False, source)
            field[0, :, cols] = fr
            field[1, :, cols] = fi


def back_kernel(
    size, span, slots, tile_rows, notes, mine, theirs, far_rows, near, probe, far_far, psi2, field, *refs,
):
    measured, (keep, send, rows_buf, cols_buf) = refs[:-4], refs[-4:]
    offset, live, slot, core = notes_of(span, slots, notes)
    parts, _, _, _, width = keep.shape[1:]
    half = size // 2
    low, high, everything = slice(0, half), slice(half, size), slice(None)

    @pl.when(live)
    def _():
        early, place, patch = tile_access(span, tile_rows, offset, core, mine, theirs)

        def put_term(s, c, term):
            for k in range(span):
                for h in range(parts):
                    block = term[
                        k * tile_rows : (k + 1) * tile_rows, h * width : (h + 1) * width
                    ]
                    if k == 0:
                        keep[place(span), h, s, c] = jnp.where(early, block, 0.0).astype(bf16)
                        block = jnp.where(early, 0.0, block)
                    target = keep if k % 2 == 0 else send
                    target[place(k), h, s, c] = block.astype(bf16)

        amps = in_order(size, slot, measured, cols_buf.at[:, 0:size])
        chis = []
        for cols in (low, high):
            fr, fi = field[0, :, cols], field[1, :, cols]
            keeping = 1.0 - amps[:, cols] * lax.rsqrt(fr * fr + fi * fi + smooth)
            chis.append((fr * keeping, fi * keeping))
        put_col_halves(cols_buf, *chis)
        even = right(parts_of(far_rows, low, low), True, cols_buf[:, 0:size])
        odd = right(parts_of(far_rows, high, low), True, cols_buf[:, size : 2 * size])
        back1 = both(plus(even, odd), less(even, odd), 1)
        put_row_halves(rows_buf, [x[low] for x in back1], [x[high] for x in back1])
        even = left(parts_of(far_far, everything, low), True, rows_buf[0:size, :])
        odd = left(parts_of(far_far, everything, high), True, rows_buf[size : 2 * size, :])
        er, ei = both(plus(even, odd), less(even, odd), 0)
        br, bi = patch(1, 0), patch(1, 1)
        grad = (br * er + bi * ei, br * ei - bi * er)
        wr, wi = pair_of(psi2)
        put_term(1, 0, wr * er + wi * ei)
        put_term(1, 1, wr * ei - wi * er)
        firsts = [near[c, low, low].astype(f32) * 0.5 for c in range(2)]
        seconds = [near[c, low, high].astype(f32) * 0.5 for c in range(2)]
        evens = [x.astype(bf16) for x in plus(firsts, seconds)]
        odds = [x.astype(bf16) for x in less(firsts, seconds)]
        one, two = [x[:, low] for x in grad], [x[:, high] for x in grad]
        put_col_halves(cols_buf, plus(one, two), less(one, two))
        even = right(evens, True, cols_buf[:, 0:size])
        odd = right(odds, True, cols_buf[:, size : 2 * size])
        back2 = both(plus(even, odd), less(even, odd), 1)
        one, two = [x[low] for x in back2], [x[high] for x in back2]
        put_row_halves(rows_buf, plus(one, two), less(one, two))
        even = left(evens, True, rows_buf[0:size, :])
        odd = left(odds, True, rows_buf[size : 2 * size, :])
        gr, gi = both(plus(even, odd), less(even, odd), 0)
        pr, pi = pair_of(probe)
        put_term(0, 0, pr * gr + pi * gi)
        put_term(0, 1, pr * gi - pi * gr)
        send[(1 - core) * (span // 2)] = jnp.zeros(send.shape[1:], bf16)

    @pl.when(jnp.logical_not(live))
    def _():
        keep[...] = jnp.zeros(keep.shape, bf16)
        send[...] = jnp.zeros(send.shape, bf16)


def small_call(kernel, out_shape, scalars, values, name):
    inside = pl.BlockSpec(memory_space=pltpu.VMEM)
    return pl.pallas_call(
        kernel,
        out_shape=out_shape,
        in_specs=[pl.BlockSpec(memory_space=pltpu.SMEM)] * len(scalars) + [inside] * len(values),
        out_specs=jax.tree.map(lambda _: inside, out_shape),
        compiler_params=pltpu.CompilerParams(vmem_limit_bytes=12 * 1024 * 1024),
        cost_estimate=pl.CostEstimate(flops=0, bytes_accessed=1 << 20, transcendentals=0),
        name=name,
    )(*scalars, *values)


def placed(values, place_of, name):
    def kernel(*refs):
        for number, value in enumerate(refs[:-1]):
            refs[-1][place_of(number)] = value[...]

    shape = jax.ShapeDtypeStruct((len(values),) + values[0].shape, values[0].dtype)
    return small_call(kernel, shape, [], values, name)


def amplitude_messages(amplitudes, row_offsets, position_counts):
    slots, rows, size = amplitudes.shape

    def kernel(offsets, counts, amps, straight, crossed):
        slot = lax.axis_index("scan")
        straight[0:rows, :] = amps[slot].astype(bf16)
        crossed[...] = amps[1 - slot].astype(bf16)
        at = lax.broadcasted_iota(jnp.int32, (16, size), 1)
        notes = jnp.where(at == slots, counts[0].astype(f32), 0.0)
        for number in range(slots):
            notes = jnp.where(at == number, offsets[number].astype(f32), notes)
        straight[rows : rows + 16, :] = notes.astype(bf16)

    shapes = [jax.ShapeDtypeStruct((n, size), bf16) for n in (rows + 16, rows)]
    return small_call(kernel, shapes, [row_offsets, position_counts], [amplitudes], "messages")


def group(number):
    unit, flip = ((4, 0), (2, 1), (2, 2), (2, 3), (4, 4))[number]
    odd = lax.rem(lax.axis_index("tile") // unit, 2) == 1
    return jnp.where(odd, flip, 4 - flip)


def merged_messages(keep, got):
    def kernel(keep, got, *outs):
        for number, out in enumerate(outs):
            at = group(number)
            out[...] = (keep[at].astype(f32) + got[at].astype(f32)).astype(bf16)

    return small_call(kernel, [jax.ShapeDtypeStruct(keep.shape[1:], bf16)] * 5, [], [keep, got], "merge")


def merged_in_halves(keep, got):
    def kernel(keep, got, near_with, next_with, next_across, middle, half_own, half_away):
        def chunk(number, *half):
            at = (group(number), *half)
            return keep[at].astype(f32) + got[at].astype(f32)

        slot = lax.axis_index("scan")
        half_own[...] = chunk(3, slot)
        half_away[...] = chunk(3, 1 - slot).astype(bf16)
        for out, number in ((near_with, 1), (next_with, 0), (next_across, 4), (middle, 2)):
            out[...] = chunk(number).astype(bf16)

    whole = jax.ShapeDtypeStruct(keep.shape[1:], bf16)
    halves = [jax.ShapeDtypeStruct(keep.shape[2:], kind) for kind in (f32, bf16)]
    return small_call(kernel, [whole] * 4 + halves, [], [keep, got], "merge")


def summed(own, got):
    def kernel(own, got, out):
        out[...] = (own[...] + got[...].astype(f32)).astype(bf16)

    return small_call(kernel, jax.ShapeDtypeStruct(own.shape, bf16), [], [own, got], "near")


def halves_of_sum(values):
    def kernel(*refs):
        (own, away), slot = refs[-2:], lax.axis_index("scan")

        def half(h):
            return sum(ref[h].astype(f32) for ref in refs[:-2])

        own[...] = half(slot)
        away[...] = half(1 - slot).astype(bf16)

    shape = values[0].shape[1:]
    shapes = [jax.ShapeDtypeStruct(shape, f32), jax.ShapeDtypeStruct(shape, bf16)]
    return small_call(kernel, shapes, [], values, "sums")


def kernel_call(kernel, size, slots, tile_rows, name, out_shape, *inputs):
    inside = pl.BlockSpec(memory_space=pltpu.VMEM)
    return pl.pallas_call(
        functools.partial(kernel, size, size // tile_rows, slots, tile_rows),
        out_shape=out_shape,
        in_specs=[inside] * len(inputs),
        out_specs=[inside] * len(out_shape),
        scratch_shapes=[
            pltpu.VMEM((2 * size, size), bf16),
            pltpu.VMEM((size, 2 * size), bf16),
        ],
        compiler_params=pltpu.CompilerParams(vmem_limit_bytes=28 * 1024 * 1024),
        cost_estimate=pl.CostEstimate(
            flops=24 * size**3, bytes_accessed=size * size, transcendentals=0
        ),
        name=name,
    )(*inputs)


def shards(size, object_slab, probe_wave, amplitudes, row_offsets, position_counts):
    tile_rows = object_slab.shape[2]
    span = size // tile_rows
    count = lax.axis_size("tile")
    parts = lax.axis_size("scan")
    slots = amplitudes.shape[0]
    paired = parts == slots == 2
    ahead = span // 2
    swap = [(0, 1), (1, 0)]
    ahead_pairs = [(one, (one + ahead) % count) for one in range(count)]

    def brought(value):
        return lax.ppermute(value, "tile", ahead_pairs)

    def paired_with(value, unit):
        return lax.ppermute(value, "tile", [(one, one ^ unit) for one in range(count)])

    def paired_across(value, unit):
        pairs = []
        for one in range(count):
            step = unit if (one // unit) % 2 else -unit
            pairs.append((one, one + step if unit <= one < count - unit else one ^ 1))
        return lax.ppermute(value, "tile", pairs)

    own = object_slab.astype(bf16)
    width = own.shape[-1]
    if paired:
        beside = lax.ppermute(own, "scan", swap)
        beside, probe_wave = lax.optimization_barrier((beside, probe_wave))
        whole = placed([own, beside], lambda n: jnp.bitwise_xor(lax.axis_index("scan"), n), "halves")
        probe_pieces = [probe_wave, lax.ppermute(probe_wave, "scan", swap)]
        straight, crossed = amplitude_messages(amplitudes, row_offsets, position_counts)
        straight = brought(straight)
        crossed = lax.ppermute(
            crossed,
            ("tile", "scan"),
            [(2 * a + x, 2 * b + 1 - x) for a, b in ahead_pairs for x in range(2)],
        )
        notes = straight
        measured = [straight, crossed]
    else:
        whole = lax.all_gather(own, "scan")
        every = lax.all_gather(probe_wave, "scan")
        probe_pieces = [every[number] for number in range(parts)]
        notes = jnp.concatenate([row_offsets, position_counts]).astype(bf16)
        notes = brought(jnp.pad(notes[None], ((0, 15), (0, size - slots - 1))))
        every = lax.all_gather(brought(amplitudes.astype(bf16)), "scan")
        slot = lax.axis_index("scan")
        measured = [every[:, jnp.minimum(slot, slots - 1)].reshape((size, size))]
    next_across, next_with = paired_across(whole, 4), paired_with(whole, 4)
    near_across, near_with = paired_across(whole, 2), paired_with(whole, 2)
    middle, probe_pieces, notes = lax.optimization_barrier((whole, probe_pieces, notes))
    far_rows, far_cols, near = tables(size)
    turned, far_near, far_far = rolled(
        probe_pieces, far_rows, far_cols, notes, size, span, slots
    )
    arrived = [next_with, near_with, middle, near_across, next_across]
    mine = placed(arrived, group, "groups")
    theirs = paired_with(mine, 1)
    shape = jax.ShapeDtypeStruct
    psi2, field = kernel_call(
        forth_kernel, size, slots, tile_rows, "forth",
        [shape((2, size, size), bf16), shape((2, size, size), f32)],
        notes, mine, theirs, far_cols, near, turned, far_near,
    )
    measured[-1], field = lax.optimization_barrier((measured[-1], field))
    keep, send = kernel_call(
        back_kernel, size, slots, tile_rows, "back",
        [shape((len(arrived), parts, 2, 2, tile_rows, width), bf16)] * 2,
        notes, mine, theirs, far_rows, near, turned, far_far, psi2, field, *measured,
    )
    got = paired_with(send, 1)
    if paired:
        near_with, next_with, next_across, middle, half_own, half_away = merged_in_halves(keep, got)
        half_got = lax.ppermute(half_away, "scan", swap)
        message = summed(half_own, half_got)
        middle, message = lax.optimization_barrier((middle, message))
        kept, away = halves_of_sum(
            [
                paired_with(near_with, 2),
                paired_with(next_with, 4),
                paired_across(next_across, 4),
                middle,
            ]
        )
        for value in (lax.ppermute(away, "scan", swap), paired_across(message, 2)):
            kept = kept + value.astype(f32)
        return kept
    next_with, near_with, middle, near_across, next_across = merged_messages(keep, got)
    returned = [
        paired_with(near_with, 2),
        paired_across(near_across, 2),
        paired_with(next_with, 4),
        paired_across(next_across, 4),
        middle,
    ]
    total = sum(value.astype(f32) for value in returned)
    return lax.psum_scatter(total, "scan", scatter_dimension=0, tiled=False)


def solution(mesh):
    in_specs = (
        P(None, None, "tile", "scan"),
        P(None, None, "scan"),
        P("tile", "scan", None),
        P("tile"),
        P("tile"),
    )
    out_specs = P(None, None, "tile", "scan")

    def run(object_slab, *rest):
        return jax.shard_map(
            functools.partial(shards, object_slab.shape[3]),
            mesh=mesh, in_specs=in_specs, out_specs=out_specs, check_vma=False,
        )(object_slab, *rest)

    return run
```

```python
import functools
import math

import jax
import jax.numpy as jnp
import ml_dtypes
import numpy as np
from jax import lax
from jax.experimental import pallas as pl
from jax.experimental.pallas import tpu as pltpu
from jax.sharding import PartitionSpec as P

fresnel = 0.5
smooth = 1.0
bf16 = jnp.bfloat16
f32 = jnp.float32


def tables(size):
    index = np.arange(size)
    angles = 2.0 * np.pi / size * (index[:, None] * index[None, :] % size)
    base = np.exp(1j * angles)
    far = np.conj(base) / math.sqrt(size)
    centred = np.where(index < size // 2, index, index - size).astype(np.float64)
    kernel = np.exp(-1j * np.pi * fresnel / size * centred * centred)
    near = (base * kernel[None, :]) @ np.conj(base).T / size

    def parts(table):
        stacked = np.stack([table.real, table.imag])
        return jnp.asarray(stacked.astype(ml_dtypes.bfloat16))

    order = np.concatenate([index[0::2], index[1::2]])
    return parts(far[order]), parts(far[:, order]), parts(near)


def three(table, conjugate):
    real, imag = table
    return (real, -imag, imag) if conjugate else (real, imag, -imag)


def left(table, conjugate, wave):
    real, plus, minus = three(table, conjugate)
    top = jnp.concatenate([real, minus], axis=1)
    bottom = jnp.concatenate([plus, real], axis=1)
    return (
        jnp.dot(top, wave, preferred_element_type=f32),
        jnp.dot(bottom, wave, preferred_element_type=f32),
    )


def right(table, conjugate, wave):
    real, plus, minus = three(table, conjugate)
    real_side = jnp.concatenate([real, minus], axis=0)
    imag_side = jnp.concatenate([plus, real], axis=0)
    return (
        jnp.dot(wave, real_side, preferred_element_type=f32),
        jnp.dot(wave, imag_side, preferred_element_type=f32),
    )


def one_hot(size, hit):
    row = lax.broadcasted_iota(jnp.int32, (size, size), 0)
    col = lax.broadcasted_iota(jnp.int32, (size, size), 1)
    return jnp.where(hit(row, col), 1.0, 0.0).astype(bf16)


def notes_of(span, slots, ref):
    rows = ref.shape[0]
    values = ref[rows - 16 : rows, 0:128].astype(f32)
    row = lax.broadcasted_iota(jnp.int32, values.shape, 0)
    col = lax.broadcasted_iota(jnp.int32, values.shape, 1)

    def note(at):
        return jnp.sum(jnp.where((row == 0) & (col == at), values, 0.0)).astype(jnp.int32)

    tile, slot = lax.axis_index("tile"), lax.axis_index("scan")
    ahead = span // 2
    home = (tile >= ahead) & (tile < lax.axis_size("tile") - ahead)
    live = home & (slot < note(slots))
    return note(jnp.minimum(slot, slots - 1)), live, slot, lax.rem(tile, 2)


def in_order(size, slot, measured, amps):
    half = size // 2
    for number, piece in enumerate(measured):
        rows = size // len(measured)
        at = pl.multiple_of(jnp.where(slot == number, 0, size - rows), rows)
        amps[pl.ds(at, rows), :] = piece[0:rows, :]

    def frequency(place, natural):
        return natural == jnp.where(place < half, 2 * place, 2 * (place - half) + 1)

    rows_first = jnp.dot(one_hot(size, frequency), amps[...], preferred_element_type=f32)
    return jnp.dot(
        rows_first.astype(bf16),
        one_hot(size, lambda row, col: frequency(col, row)),
        preferred_element_type=f32,
    )


def roll_kernel(size, span, slots, notes, far_rows, far_cols, *refs):
    pieces, (probe_out, near_side, far_side) = refs[:-3], refs[-3:]
    offset, _, slot, _ = notes_of(span, slots, notes)
    half = size // 2

    def moved(to, source):
        gap = to - source - offset
        return (gap == 0) | (gap == -size)

    down = one_hot(size, moved)
    across = one_hot(size, lambda row, col: moved(col, row))
    for c in range(2):
        near_side[c] = jnp.dot(
            far_rows[c], across[:, :half], preferred_element_type=f32
        ).astype(bf16)
        far_side[c] = jnp.dot(down[:half], far_cols[c], preferred_element_type=f32).astype(bf16)
    for c in range(2):
        done = 0
        for piece in pieces:
            turned = jnp.dot(down, piece[c], preferred_element_type=f32).astype(bf16)
            width = turned.shape[1]
            if len(pieces) == 2:
                at = pl.multiple_of(jnp.where(slot == done, 0, width), width)
                probe_out[c, :, pl.ds(at, width)] = turned
                done += 1
            else:
                probe_out[c, :, done : done + width] = turned
                done += width


def rolled(pieces, far_rows, far_cols, notes, size, span, slots):
    whole = pl.BlockSpec(memory_space=pltpu.VMEM)
    return pl.pallas_call(
        functools.partial(roll_kernel, size, span, slots),
        out_shape=[
            jax.ShapeDtypeStruct((2, size, size), bf16),
            jax.ShapeDtypeStruct((2, size, size // 2), bf16),
            jax.ShapeDtypeStruct((2, size // 2, size), bf16),
        ],
        in_specs=[whole] * (3 + len(pieces)),
        out_specs=[whole] * 3,
        compiler_params=pltpu.CompilerParams(vmem_limit_bytes=16 * 1024 * 1024),
        cost_estimate=pl.CostEstimate(
            flops=64 * size**3, bytes_accessed=24 * size * size, transcendentals=0
        ),
        name="rolled",
    )(notes, far_rows, far_cols, *pieces)


def tile_access(span, tile_rows, offset, core, mine, theirs):
    parts, _, _, _, width = mine.shape[1:]
    early = lax.broadcasted_iota(jnp.int32, (tile_rows, width), 0) < offset

    def place(k):
        return k // 2 if k % 2 == 0 else k // 2 + core

    def piece(k, h, s, c):
        source = mine if k % 2 == 0 else theirs
        return source[place(k), h, s, c].astype(f32)

    def patch(s, c):
        rows = []
        for k in range(span):
            blocks = [piece(k, h, s, c) for h in range(parts)]
            if k == 0:
                blocks = [jnp.where(early, piece(span, h, s, c), blocks[h]) for h in range(parts)]
            rows.append(jnp.concatenate(blocks, axis=1))
        return jnp.concatenate(rows, axis=0)

    return early, place, patch


def put_rows(rows_buf, pair):
    size = rows_buf.shape[1]
    for c in range(2):
        rows_buf[c * size : (c + 1) * size, :] = pair[c].astype(bf16)


def put_cols(cols_buf, pair):
    size = cols_buf.shape[0]
    for c in range(2):
        cols_buf[:, c * size : (c + 1) * size] = pair[c].astype(bf16)


def put_row_halves(rows_buf, first, second):
    half = rows_buf.shape[1] // 2
    for number, wave in enumerate((*first, *second)):
        rows_buf[number * half : (number + 1) * half, :] = wave.astype(bf16)


def put_col_halves(cols_buf, first, second):
    half = cols_buf.shape[0] // 2
    for number, wave in enumerate((*first, *second)):
        cols_buf[:, number * half : (number + 1) * half] = wave.astype(bf16)


def pair_of(ref):
    return ref[0].astype(f32), ref[1].astype(f32)


def parts_of(ref, rows, cols):
    return ref[0, rows, cols], ref[1, rows, cols]


def both(first, second, axis):
    return [jnp.concatenate([a, b], axis=axis) for a, b in zip(first, second)]


def plus(first, second):
    return [a + b for a, b in zip(first, second)]


def less(first, second):
    return [a - b for a, b in zip(first, second)]


def forth_kernel(
    size, span, slots, tile_rows, notes, mine, theirs, far_cols, near, probe, far_near,
    psi2, field, rows_buf, cols_buf,
):
    half = size // 2
    low, high, everything = slice(0, half), slice(half, size), slice(None)
    offset, live, _, core = notes_of(span, slots, notes)

    @pl.when(live)
    def _():
        _, _, patch = tile_access(span, tile_rows, offset, core, mine, theirs)
        firsts = [near[c, low, low].astype(f32) * 0.5 for c in range(2)]
        seconds = [near[c, low, high].astype(f32) * 0.5 for c in range(2)]
        evens = [x.astype(bf16) for x in plus(firsts, seconds)]
        odds = [x.astype(bf16) for x in less(firsts, seconds)]
        pr, pi = pair_of(probe)
        ar, ai = patch(0, 0), patch(0, 1)
        psi1 = (pr * ar - pi * ai, pr * ai + pi * ar)
        top, bottom = [x[low] for x in psi1], [x[high] for x in psi1]
        put_row_halves(rows_buf, plus(top, bottom), less(top, bottom))
        even = left(evens, False, rows_buf[0:size, :])
        odd = left(odds, False, rows_buf[size : 2 * size, :])
        half1 = both(plus(even, odd), less(even, odd), 0)
        top, bottom = [x[:, low] for x in half1], [x[:, high] for x in half1]
        put_col_halves(cols_buf, plus(top, bottom), less(top, bottom))
        even = right(evens, False, cols_buf[:, 0:size])
        odd = right(odds, False, cols_buf[:, size : 2 * size])
        two = both(plus(even, odd), less(even, odd), 1)
        psi2[0] = two[0].astype(bf16)
        psi2[1] = two[1].astype(bf16)
        wr, wi = pair_of(psi2)
        br, bi = patch(1, 0), patch(1, 1)
        wave_exit = (wr * br - wi * bi, wr * bi + wi * br)
        top, bottom = [x[low] for x in wave_exit], [x[high] for x in wave_exit]
        put_row_halves(rows_buf, plus(top, bottom), less(top, bottom))
        half2 = both(
            left(parts_of(far_near, low, everything), False, rows_buf[0:size, :]),
            left(parts_of(far_near, high, everything), False, rows_buf[size : 2 * size, :]),
            0,
        )
        top, bottom = [x[:, low] for x in half2], [x[:, high] for x in half2]
        put_col_halves(cols_buf, plus(top, bottom), less(top, bottom))
        for cols, source in ((low, cols_buf[:, 0:size]), (high, cols_buf[:, size : 2 * size])):
            fr, fi = right(parts_of(far_cols, low, cols), False, source)
            field[0, :, cols] = fr
            field[1, :, cols] = fi


def back_kernel(
    size, span, slots, tile_rows, notes, mine, theirs, far_rows, near, probe, far_far, psi2, field, *refs,
):
    measured, (keep, send, rows_buf, cols_buf) = refs[:-4], refs[-4:]
    offset, live, slot, core = notes_of(span, slots, notes)
    parts, _, _, _, width = keep.shape[1:]
    half = size // 2
    low, high, everything = slice(0, half), slice(half, size), slice(None)

    @pl.when(live)
    def _():
        early, place, patch = tile_access(span, tile_rows, offset, core, mine, theirs)

        def put_term(s, c, term):
            for k in range(span):
                for h in range(parts):
                    block = term[
                        k * tile_rows : (k + 1) * tile_rows, h * width : (h + 1) * width
                    ]
                    if k == 0:
                        keep[place(span), h, s, c] = jnp.where(early, block, 0.0).astype(bf16)
                        block = jnp.where(early, 0.0, block)
                    target = keep if k % 2 == 0 else send
                    target[place(k), h, s, c] = block.astype(bf16)

        amps = in_order(size, slot, measured, cols_buf.at[:, 0:size])
        chis = []
        for cols in (low, high):
            fr, fi = field[0, :, cols], field[1, :, cols]
            keeping = 1.0 - amps[:, cols] * lax.rsqrt(fr * fr + fi * fi + smooth)
            chis.append((fr * keeping, fi * keeping))
        put_col_halves(cols_buf, *chis)
        even = right(parts_of(far_rows, low, low), True, cols_buf[:, 0:size])
        odd = right(parts_of(far_rows, high, low), True, cols_buf[:, size : 2 * size])
        back1 = both(plus(even, odd), less(even, odd), 1)
        put_row_halves(rows_buf, [x[low] for x in back1], [x[high] for x in back1])
        even = left(parts_of(far_far, everything, low), True, rows_buf[0:size, :])
        odd = left(parts_of(far_far, everything, high), True, rows_buf[size : 2 * size, :])
        er, ei = both(plus(even, odd), less(even, odd), 0)
        br, bi = patch(1, 0), patch(1, 1)
        grad = (br * er + bi * ei, br * ei - bi * er)
        wr, wi = pair_of(psi2)
        put_term(1, 0, wr * er + wi * ei)
        put_term(1, 1, wr * ei - wi * er)
        firsts = [near[c, low, low].astype(f32) * 0.5 for c in range(2)]
        seconds = [near[c, low, high].astype(f32) * 0.5 for c in range(2)]
        evens = [x.astype(bf16) for x in plus(firsts, seconds)]
        odds = [x.astype(bf16) for x in less(firsts, seconds)]
        one, two = [x[:, low] for x in grad], [x[:, high] for x in grad]
        put_col_halves(cols_buf, plus(one, two), less(one, two))
        even = right(evens, True, cols_buf[:, 0:size])
        odd = right(odds, True, cols_buf[:, size : 2 * size])
        back2 = both(plus(even, odd), less(even, odd), 1)
        one, two = [x[low] for x in back2], [x[high] for x in back2]
        put_row_halves(rows_buf, plus(one, two), less(one, two))
        even = left(evens, True, rows_buf[0:size, :])
        odd = left(odds, True, rows_buf[size : 2 * size, :])
        gr, gi = both(plus(even, odd), less(even, odd), 0)
        pr, pi = pair_of(probe)
        put_term(0, 0, pr * gr + pi * gi)
        put_term(0, 1, pr * gi - pi * gr)
        send[(1 - core) * (span // 2)] = jnp.zeros(send.shape[1:], bf16)

    @pl.when(jnp.logical_not(live))
    def _():
        keep[...] = jnp.zeros(keep.shape, bf16)
        send[...] = jnp.zeros(send.shape, bf16)


def small_call(kernel, out_shape, scalars, values, name):
    inside = pl.BlockSpec(memory_space=pltpu.VMEM)
    return pl.pallas_call(
        kernel,
        out_shape=out_shape,
        in_specs=[pl.BlockSpec(memory_space=pltpu.SMEM)] * len(scalars) + [inside] * len(values),
        out_specs=jax.tree.map(lambda _: inside, out_shape),
        compiler_params=pltpu.CompilerParams(vmem_limit_bytes=12 * 1024 * 1024),
        cost_estimate=pl.CostEstimate(flops=0, bytes_accessed=1 << 20, transcendentals=0),
        name=name,
    )(*scalars, *values)


def placed(values, place_of, name):
    def kernel(*refs):
        for number, value in enumerate(refs[:-1]):
            refs[-1][place_of(number)] = value[...]

    shape = jax.ShapeDtypeStruct((len(values),) + values[0].shape, values[0].dtype)
    return small_call(kernel, shape, [], values, name)


def amplitude_messages(amplitudes, row_offsets, position_counts):
    slots, rows, size = amplitudes.shape

    def kernel(offsets, counts, amps, straight, crossed):
        slot = lax.axis_index("scan")
        straight[0:rows, :] = amps[slot].astype(bf16)
        crossed[...] = amps[1 - slot].astype(bf16)
        at = lax.broadcasted_iota(jnp.int32, (16, size), 1)
        notes = jnp.where(at == slots, counts[0].astype(f32), 0.0)
        for number in range(slots):
            notes = jnp.where(at == number, offsets[number].astype(f32), notes)
        straight[rows : rows + 16, :] = notes.astype(bf16)

    shapes = [jax.ShapeDtypeStruct((n, size), bf16) for n in (rows + 16, rows)]
    return small_call(kernel, shapes, [row_offsets, position_counts], [amplitudes], "messages")


def group(number):
    unit, flip = ((4, 0), (2, 1), (2, 2), (2, 3), (4, 4))[number]
    odd = lax.rem(lax.axis_index("tile") // unit, 2) == 1
    return jnp.where(odd, flip, 4 - flip)


def merged_messages(keep, got):
    def kernel(keep, got, *outs):
        for number, out in enumerate(outs):
            at = group(number)
            out[...] = (keep[at].astype(f32) + got[at].astype(f32)).astype(bf16)

    return small_call(kernel, [jax.ShapeDtypeStruct(keep.shape[1:], bf16)] * 5, [], [keep, got], "merge")


def merged_in_halves(keep, got):
    def kernel(keep, got, near_with, next_with, next_across, middle, half_own, half_away):
        def chunk(number, *half):
            at = (group(number), *half)
            return keep[at].astype(f32) + got[at].astype(f32)

        slot = lax.axis_index("scan")
        half_own[...] = chunk(3, slot)
        half_away[...] = chunk(3, 1 - slot).astype(bf16)
        for out, number in ((near_with, 1), (next_with, 0), (next_across, 4), (middle, 2)):
            out[...] = chunk(number).astype(bf16)

    whole = jax.ShapeDtypeStruct(keep.shape[1:], bf16)
    halves = [jax.ShapeDtypeStruct(keep.shape[2:], kind) for kind in (f32, bf16)]
    return small_call(kernel, [whole] * 4 + halves, [], [keep, got], "merge")


def summed(own, got):
    def kernel(own, got, out):
        out[...] = (own[...] + got[...].astype(f32)).astype(bf16)

    return small_call(kernel, jax.ShapeDtypeStruct(own.shape, bf16), [], [own, got], "near")


def halves_of_sum(values):
    def kernel(*refs):
        (own, away), slot = refs[-2:], lax.axis_index("scan")

        def half(h):
            return sum(ref[h].astype(f32) for ref in refs[:-2])

        own[...] = half(slot)
        away[...] = half(1 - slot).astype(bf16)

    shape = values[0].shape[1:]
    shapes = [jax.ShapeDtypeStruct(shape, f32), jax.ShapeDtypeStruct(shape, bf16)]
    return small_call(kernel, shapes, [], values, "sums")


def kernel_call(kernel, size, slots, tile_rows, name, out_shape, *inputs):
    inside = pl.BlockSpec(memory_space=pltpu.VMEM)
    return pl.pallas_call(
        functools.partial(kernel, size, size // tile_rows, slots, tile_rows),
        out_shape=out_shape,
        in_specs=[inside] * len(inputs),
        out_specs=[inside] * len(out_shape),
        scratch_shapes=[
            pltpu.VMEM((2 * size, size), bf16),
            pltpu.VMEM((size, 2 * size), bf16),
        ],
        compiler_params=pltpu.CompilerParams(vmem_limit_bytes=28 * 1024 * 1024),
        cost_estimate=pl.CostEstimate(
            flops=24 * size**3, bytes_accessed=size * size, transcendentals=0
        ),
        name=name,
    )(*inputs)


def shards(size, object_slab, probe_wave, amplitudes, row_offsets, position_counts):
    tile_rows = object_slab.shape[2]
    span = size // tile_rows
    count = lax.axis_size("tile")
    parts = lax.axis_size("scan")
    slots = amplitudes.shape[0]
    paired = parts == slots == 2
    ahead = span // 2
    swap = [(0, 1), (1, 0)]
    ahead_pairs = [(one, (one + ahead) % count) for one in range(count)]

    def brought(value):
        return lax.ppermute(value, "tile", ahead_pairs)

    def paired_with(value, unit):
        return lax.ppermute(value, "tile", [(one, one ^ unit) for one in range(count)])

    def paired_across(value, unit):
        pairs = []
        for one in range(count):
            step = unit if (one // unit) % 2 else -unit
            pairs.append((one, one + step if unit <= one < count - unit else one ^ 1))
        return lax.ppermute(value, "tile", pairs)

    own = object_slab.astype(bf16)
    width = own.shape[-1]
    if paired:
        beside = lax.ppermute(own, "scan", swap)
        beside, probe_wave = lax.optimization_barrier((beside, probe_wave))
        whole = placed([own, beside], lambda n: jnp.bitwise_xor(lax.axis_index("scan"), n), "halves")
        probe_pieces = [probe_wave, lax.ppermute(probe_wave, "scan", swap)]
        straight, crossed = amplitude_messages(amplitudes, row_offsets, position_counts)
        straight = brought(straight)
        crossed = lax.ppermute(
            crossed,
            ("tile", "scan"),
            [(2 * a + x, 2 * b + 1 - x) for a, b in ahead_pairs for x in range(2)],
        )
        notes = straight
        measured = [straight, crossed]
    else:
        whole = lax.all_gather(own, "scan")
        every = lax.all_gather(probe_wave, "scan")
        probe_pieces = [every[number] for number in range(parts)]
        notes = jnp.concatenate([row_offsets, position_counts]).astype(bf16)
        notes = brought(jnp.pad(notes[None], ((0, 15), (0, size - slots - 1))))
        every = lax.all_gather(brought(amplitudes.astype(bf16)), "scan")
        slot = lax.axis_index("scan")
        measured = [every[:, jnp.minimum(slot, slots - 1)].reshape((size, size))]
    next_across, next_with = paired_across(whole, 4), paired_with(whole, 4)
    near_across, near_with = paired_across(whole, 2), paired_with(whole, 2)
    middle, probe_pieces, notes = lax.optimization_barrier((whole, probe_pieces, notes))
    far_rows, far_cols, near = tables(size)
    turned, far_near, far_far = rolled(
        probe_pieces, far_rows, far_cols, notes, size, span, slots
    )
    arrived = [next_with, near_with, middle, near_across, next_across]
    mine = placed(arrived, group, "groups")
    theirs = paired_with(mine, 1)
    shape = jax.ShapeDtypeStruct
    psi2, field = kernel_call(
        forth_kernel, size, slots, tile_rows, "forth",
        [shape((2, size, size), bf16), shape((2, size, size), f32)],
        notes, mine, theirs, far_cols, near, turned, far_near,
    )
    measured[-1], field = lax.optimization_barrier((measured[-1], field))
    keep, send = kernel_call(
        back_kernel, size, slots, tile_rows, "back",
        [shape((len(arrived), parts, 2, 2, tile_rows, width), bf16)] * 2,
        notes, mine, theirs, far_rows, near, turned, far_far, psi2, field, *measured,
    )
    got = paired_with(send, 1)
    if paired:
        near_with, next_with, next_across, middle, half_own, half_away = merged_in_halves(keep, got)
        half_got = lax.ppermute(half_away, "scan", swap)
        message = summed(half_own, half_got)
        middle, message = lax.optimization_barrier((middle, message))
        kept, away = halves_of_sum(
            [
                paired_with(near_with, 2),
                paired_with(next_with, 4),
                paired_across(next_across, 4),
                middle,
            ]
        )
        for value in (lax.ppermute(away, "scan", swap), paired_across(message, 2)):
            kept = kept + value.astype(f32)
        return kept
    next_with, near_with, middle, near_across, next_across = merged_messages(keep, got)
    returned = [
        paired_with(near_with, 2),
        paired_across(near_across, 2),
        paired_with(next_with, 4),
        paired_across(next_across, 4),
        middle,
    ]
    total = sum(value.astype(f32) for value in returned)
    return lax.psum_scatter(total, "scan", scatter_dimension=0, tiled=False)


def solution(mesh):
    in_specs = (
        P(None, None, "tile", "scan"),
        P(None, None, "scan"),
        P("tile", "scan", None),
        P("tile"),
        P("tile"),
    )
    out_specs = P(None, None, "tile", "scan")

    def run(object_slab, *rest):
        return jax.shard_map(
            functools.partial(shards, object_slab.shape[3]),
            mesh=mesh, in_specs=in_specs, out_specs=out_specs, check_vma=False,
        )(object_slab, *rest)

    return run
```
